32 devices in a mesh: dp: 4 (over y, x), graph: 8 (over z, core).
Axes of the slice: x: 2, y: 2, z: 4, core: 2. Of those that a mesh axis runs over, the one named last changes fastest.
Arguments:
- edge_state: bfloat16 [4, 16384, 512], P('dp', 'graph'), may hold values from -6 to 6
- cotangent: bfloat16 [4, 16384, 512], P('dp', 'graph'), may hold values from -6 to 6
- edge_count: int32 [4, 8], P('dp', 'graph'), may hold values from 1024 to 2048, as said below
- triplet_basis: bfloat16 [4, 16, 65536], P('dp', None, 'graph'), may hold values from -6 to 6
- triplet_in: int32 [4, 65536], P('dp', 'graph'), may hold values from 0 to 2047, as said below
- triplet_out: int32 [4, 65536], P('dp', 'graph'), may hold values from 0 to 2047, as said below
- down_weight: bfloat16 [512, 64], replicated, may hold values from -0.25 to 0.25
- basis_weight: bfloat16 [16, 64], replicated, may hold values from -1.5 to 1.5
- bilinear_weight: bfloat16 [64, 64], replicated, may hold values from -0.75 to 0.75
- up_weight: bfloat16 [64, 512], replicated, may hold values from -0.75 to 0.75
- first_weight: bfloat16 [512, 512], replicated, may hold values from -0.25 to 0.25
- second_weight: bfloat16 [512, 512], replicated, may hold values from -0.25 to 0.25
Outputs:
- edge_grad: bfloat16 [4, 16384, 512], P('dp', 'graph')
- down_grad: float32 [512, 64], replicated
- basis_grad: float32 [16, 64], replicated
- bilinear_grad: float32 [64, 64], replicated
- up_grad: float32 [64, 512], replicated
- first_grad: float32 [512, 512], replicated
- second_grad: float32 [512, 512], replicated
The draws below stay inside these ranges and needn't reach their ends.
Inputs may be any that keep to these rules, and one draw needn't show every extreme that they name: `edge_count`: every entry is a multiple of 128; in every batch some shard holds all 2048 slots live. Slot s * 8192 + j * 1024 + k (s and j below 8, k below 1024) holds a triplet of shard s whose in-edge is row triplet_in of shard j, a live row: below edge_count[b, j]. Slot s * 8192 + t holds a triplet whose out-edge is row triplet_out of shard s, a live row: below edge_count[b, s].
All inputs are finite; a program needn't handle non-finite values.
Results may differ from the reference program's by a relative error of at most 0.0096.
Values may be sent and summed in bfloat16 or wider, within the bound.
No kernel may reach another device: no remote copies, remote signals or barrier semaphores. Data moves between devices by JAX's collectives and lax.ppermute only.
A program may use at most 128 MiB of HBM per device.

```python
import math
import jax
import jax.numpy as jnp
from jax import lax

H = 512
K = 64
NB = 16
E_DEV = 2048
BATCHES = 4
SHARDS = 8
EDGES = 16384
TRI_DEV = 8192
TRIPLETS = 65536
CAP = 1024


def edge_counts(key):
    base_key = jax.random.fold_in(key, 11)
    low_blocks = E_DEV // 256
    high_blocks = E_DEV // 128 + 1
    block_count = jax.random.randint(base_key, (BATCHES, SHARDS), low_blocks, high_blocks)
    full_shard = jax.random.randint(jax.random.fold_in(base_key, 1), (BATCHES, 1), 0, SHARDS)
    shard_ids = jnp.arange(SHARDS, dtype=jnp.int32)[None, :]
    block_count = jnp.where(shard_ids == full_shard, E_DEV // 128, block_count)
    return (block_count * 128).astype(jnp.int32)


def draw_edge_count(key, part):
    return edge_counts(key)


def draw_triplet_in(key, part):
    counts = edge_counts(key)
    slot_ids = jnp.arange(SHARDS * TRI_DEV, dtype=jnp.int32)
    owner_ids = slot_ids % TRI_DEV // CAP
    limit_rows = counts[:, owner_ids]
    raw_bits = jax.random.randint(jax.random.fold_in(key, 23), (BATCHES, SHARDS * TRI_DEV), 0, 1 << 30)
    picked = raw_bits % limit_rows
    first_slot = (slot_ids < TRI_DEV) & (slot_ids % CAP == 0)
    return jnp.where(first_slot[None, :], limit_rows - 1, picked).astype(jnp.int32)


def draw_triplet_out(key, part):
    counts = edge_counts(key)
    slot_ids = jnp.arange(SHARDS * TRI_DEV, dtype=jnp.int32)
    owner_ids = slot_ids // TRI_DEV
    limit_rows = counts[:, owner_ids]
    raw_bits = jax.random.randint(jax.random.fold_in(key, 37), (BATCHES, SHARDS * TRI_DEV), 0, 1 << 30)
    picked = raw_bits % limit_rows
    first_slot = slot_ids % TRI_DEV == 0
    return jnp.where(first_slot[None, :], limit_rows - 1, picked).astype(jnp.int32)


def level_of(rng, dims, pieces, smallest, high):
    loudness, own = 1.0, jax.random.fold_in(rng, 6)
    for axis_at, parts in pieces:
        steps = jnp.exp(jax.random.uniform(jax.random.fold_in(own, axis_at), (parts,), jnp.float32, smallest / len(pieces), high / len(pieces)))
        loudness = loudness * jnp.repeat(steps, dims[axis_at] // parts).reshape([-1 if axis == axis_at else 1 for axis in range(len(dims))])
    return loudness


def normal_values(rng, shape, scale, limit, split=(), held_as=jnp.bfloat16):
    result = scale * jax.random.normal(rng, shape, jnp.float32)
    if split:
        result = result * level_of(rng, shape, split, -0.22, 0.18)
    return jnp.clip(result, -limit, limit).astype(held_as)


def setup_inputs(seed: int = 0) -> dict:
    keys = jax.random.split(jax.random.key(seed), 13)
    edge_state = normal_values(keys[0], (BATCHES, EDGES, H), 1.0, 6.0, ((0, 4), (1, 8)))
    cotangent = normal_values(keys[1], (BATCHES, EDGES, H), 1.0, 6.0, ((0, 4), (1, 8)))
    edge_count = draw_edge_count(jax.random.fold_in(keys[12], 71), 0)
    triplet_basis = normal_values(keys[3], (BATCHES, NB, TRIPLETS), 1.0, 6.0, ((0, 4), (2, 8)))
    triplet_in = draw_triplet_in(jax.random.fold_in(keys[12], 71), 0)
    triplet_out = draw_triplet_out(jax.random.fold_in(keys[12], 71), 0)
    down_weight = normal_values(keys[6], (H, K), H ** -0.5, 0.25)
    basis_weight = normal_values(keys[7], (NB, K), NB ** -0.5, 1.5)
    bilinear_weight = normal_values(keys[8], (K, K), K ** -0.5, 0.75)
    up_weight = normal_values(keys[9], (K, H), K ** -0.5, 0.75)
    first_weight = normal_values(keys[10], (H, H), H ** -0.5, 0.25)
    second_weight = normal_values(keys[11], (H, H), H ** -0.5, 0.25)
    return dict(edge_state=edge_state, cotangent=cotangent, edge_count=edge_count, triplet_basis=triplet_basis, triplet_in=triplet_in, triplet_out=triplet_out, down_weight=down_weight, basis_weight=basis_weight, bilinear_weight=bilinear_weight, up_weight=up_weight, first_weight=first_weight, second_weight=second_weight)


HALF = 0.7071067811865476

def silu_slope(argument):
    logistic = jax.nn.sigmoid(argument)
    return logistic * (1.0 + argument * (1.0 - logistic))

def contract(left, right, left_dim, right_dim):
    return lax.dot_general(left, right, (((left_dim,), (right_dim,)), ((), ())), preferred_element_type=jnp.float32)

def one_batch(edge_state, cotangent, counts, triplet_basis, triplet_in, triplet_out, down_weight, basis_weight, bilinear_weight, up_weight, first_weight, second_weight):
    edge_ids = jnp.arange(EDGES, dtype=jnp.int32)
    live_mask = (edge_ids % E_DEV < counts[edge_ids // E_DEV]).astype(jnp.float32)
    slot_ids = jnp.arange(TRIPLETS, dtype=jnp.int32)
    in_edge = slot_ids % TRI_DEV // CAP * E_DEV + triplet_in
    out_edge = slot_ids // TRI_DEV * E_DEV + triplet_out
    pre_down = contract(down_weight, edge_state, 0, 1)
    down_rows = jax.nn.silu(pre_down).astype(jnp.bfloat16)
    tri_coef = contract(basis_weight, triplet_basis, 0, 0)
    fetched = jnp.take(down_rows, in_edge, axis=1)
    message = tri_coef * fetched.astype(jnp.float32)
    gathered = jnp.zeros((K, EDGES), jnp.float32).at[:, out_edge].add(message).astype(jnp.bfloat16)
    mixed_rows = contract(bilinear_weight, gathered, 0, 0).astype(jnp.bfloat16)
    pre_up = contract(mixed_rows, up_weight, 0, 0)
    summed = edge_state.astype(jnp.float32) + jax.nn.silu(pre_up)
    summed_half = summed.astype(jnp.bfloat16)
    pre_first = jnp.dot(summed_half, first_weight, preferred_element_type=jnp.float32)
    first_rows = jax.nn.silu(pre_first).astype(jnp.bfloat16)
    pre_second = jnp.dot(first_rows, second_weight, preferred_element_type=jnp.float32)
    back_top = cotangent.astype(jnp.float32) * live_mask[:, None] * HALF
    back_second = (back_top * silu_slope(pre_second)).astype(jnp.bfloat16)
    back_first = (contract(back_second, second_weight, 1, 1) * silu_slope(pre_first)).astype(jnp.bfloat16)
    back_summed = back_top + contract(back_first, first_weight, 1, 1)
    back_up = (back_summed * silu_slope(pre_up)).astype(jnp.bfloat16)
    back_mixed = contract(up_weight, back_up, 1, 1).astype(jnp.bfloat16)
    back_gathered = contract(bilinear_weight, back_mixed, 1, 0)
    back_message = jnp.take(back_gathered, out_edge, axis=1)
    back_coef = (back_message * fetched.astype(jnp.float32)).astype(jnp.bfloat16)
    back_down = jnp.zeros((K, EDGES), jnp.float32).at[:, in_edge].add(back_message * tri_coef)
    back_pre = (back_down * silu_slope(pre_down)).astype(jnp.bfloat16)
    edge_grad = (back_summed + contract(back_pre, down_weight, 0, 1)).astype(jnp.bfloat16)
    totals = (contract(edge_state, back_pre, 0, 1), contract(triplet_basis, back_coef, 1, 1), contract(gathered, back_mixed, 1, 1), contract(mixed_rows, back_up, 1, 0), contract(summed_half, back_first, 0, 0), contract(first_rows, back_second, 0, 0))
    return (edge_grad, totals)

def reference(edge_state, cotangent, edge_count, triplet_basis, triplet_in, triplet_out, down_weight, basis_weight, bilinear_weight, up_weight, first_weight, second_weight):
    grads = []
    running = None
    for batch_id in range(BATCHES):
        edge_grad, totals = one_batch(edge_state[batch_id], cotangent[batch_id], edge_count[batch_id], triplet_basis[batch_id], triplet_in[batch_id], triplet_out[batch_id], down_weight, basis_weight, bilinear_weight, up_weight, first_weight, second_weight)
        grads.append(edge_grad)
        if running is None:
            running = totals
        else:
            running = tuple((old + new for old, new in zip(running, totals)))
    grad_scale = 1.0 / math.sqrt(BATCHES * EDGES)
    return (jnp.stack(grads), running[0] * grad_scale, running[1] * grad_scale, running[2] * grad_scale, running[3] * grad_scale, running[4] * grad_scale, running[5] * grad_scale)
```

```python
import functools
import math

import jax
import jax.numpy as jnp
from jax import lax
from jax.experimental import pallas as pl
from jax.experimental.pallas import tpu as pltpu
from jax.sharding import PartitionSpec as P

HALF = 0.7071067811865476
F32 = jnp.float32
BF16 = jnp.bfloat16
VMEM_LIMIT = 48 * 1024 * 1024


def contract(left, right, left_dim, right_dim):
    return lax.dot_general(
        left, right, (((left_dim,), (right_dim,)), ((), ())), preferred_element_type=F32
    )


def sigmoid(value):
    return 0.5 + 0.5 * jnp.tanh(0.5 * value)


def lanes_of(row_count):
    return math.gcd(row_count, 256)


def split_index(index_row, lanes):
    slots = index_row.shape[1]
    low = jnp.bitwise_and(index_row, lanes - 1)
    high = jnp.right_shift(index_row, lanes.bit_length() - 1)
    lane_ids = lax.broadcasted_iota(jnp.int32, (lanes, slots), 0)
    return high, jnp.where(lane_ids == low, 1.0, 0.0).astype(BF16)


def stack_groups(rows, lanes):
    groups = rows.shape[1] // lanes
    return jnp.concatenate([rows[:, g * lanes : (g + 1) * lanes] for g in range(groups)], axis=0)


def pick_rows(stacked, high, lane_hot, narrow):
    groups = stacked.shape[0] // narrow
    every = contract(stacked, lane_hot, 1, 0)
    picked = jnp.where(high == 0, every[:narrow], 0.0)
    for g in range(1, groups):
        picked = jnp.where(high == g, every[g * narrow : (g + 1) * narrow], picked)
    return picked


def place_rows(values, high, lane_hot, groups):
    zero = jnp.zeros((), values.dtype)
    spread = jnp.concatenate([jnp.where(high == g, values, zero) for g in range(groups)], axis=0)
    return contract(spread.astype(BF16), lane_hot, 1, 1)


def down_kernel(edge_ref, weight_ref, rows_ref, slope_ref):
    pre = contract(weight_ref[...], edge_ref[...], 0, 1)
    logistic = sigmoid(pre)
    rows_ref[...] = (pre * logistic).astype(BF16)
    slope_ref[...] = logistic * (1.0 + pre * (1.0 - logistic))


def forward_kernel(
    rows_ref, in_ref, out_ref, basis_ref, weight_ref, gathered_ref, fetched_ref, total
):
    step = pl.program_id(0)
    narrow, row_count = gathered_ref.shape
    lanes = lanes_of(row_count)
    groups = row_count // lanes

    @pl.when(step == 0)
    def _():
        total[...] = jnp.zeros_like(total)

    high, lane_hot = split_index(in_ref[0], lanes)
    fetched = pick_rows(stack_groups(rows_ref[0], lanes), high, lane_hot, narrow)
    fetched_ref[...] = fetched.astype(BF16)
    message = contract(weight_ref[...], basis_ref[...], 0, 0) * fetched
    high, lane_hot = split_index(out_ref[0], lanes)
    total[...] += place_rows(message, high, lane_hot, groups)

    @pl.when(step == pl.num_programs(0) - 1)
    def _():
        for g in range(groups):
            gathered_ref[:, g * lanes : (g + 1) * lanes] = total[
                g * narrow : (g + 1) * narrow, :
            ].astype(BF16)


def dense_kernel(
    count_ref,
    edge_ref,
    cotangent_ref,
    gathered_ref,
    bilinear_ref,
    up_ref,
    first_ref,
    second_ref,
    summed_ref,
    back_ref,
    bilinear_grad_ref,
    up_grad_ref,
    first_grad_ref,
    second_grad_ref,
):
    step = pl.program_id(0)
    tile = edge_ref.shape[0]

    @pl.when(step == 0)
    def _():
        for ref in (bilinear_grad_ref, up_grad_ref, first_grad_ref, second_grad_ref):
            ref[...] = jnp.zeros_like(ref)

    gathered = gathered_ref[...]
    mixed = contract(bilinear_ref[...], gathered, 0, 0).astype(BF16)
    pre_up = contract(mixed, up_ref[...], 0, 0)
    up_logistic = sigmoid(pre_up)
    summed_half = (edge_ref[...].astype(F32) + pre_up * up_logistic).astype(BF16)
    pre_first = contract(summed_half, first_ref[...], 1, 0)
    first_logistic = sigmoid(pre_first)
    first_rows = (pre_first * first_logistic).astype(BF16)
    pre_second = contract(first_rows, second_ref[...], 1, 0)
    logistic = sigmoid(pre_second)
    row_ids = step * tile + lax.broadcasted_iota(jnp.int32, (tile, 1), 0)
    live = jnp.where(row_ids < count_ref[0, 0], HALF, 0.0)
    back_top = cotangent_ref[...].astype(F32) * live
    back_second = (back_top * (logistic * (1.0 + pre_second * (1.0 - logistic)))).astype(BF16)
    slope = first_logistic * (1.0 + pre_first * (1.0 - first_logistic))
    back_first = (contract(back_second, second_ref[...], 1, 1) * slope).astype(BF16)
    back_summed = back_top + contract(back_first, first_ref[...], 1, 1)
    summed_ref[...] = back_summed.astype(BF16)
    slope = up_logistic * (1.0 + pre_up * (1.0 - up_logistic))
    back_up = (back_summed * slope).astype(BF16)
    back_mixed = contract(up_ref[...], back_up, 1, 1).astype(BF16)
    back_ref[...] = contract(bilinear_ref[...], back_mixed, 1, 0).astype(BF16)
    bilinear_grad_ref[...] += contract(gathered, back_mixed, 1, 1)
    up_grad_ref[...] += contract(mixed, back_up, 1, 0)
    first_grad_ref[...] += contract(summed_half, back_first, 0, 0)
    second_grad_ref[...] += contract(first_rows, back_second, 0, 0)


def backward_kernel(
    back_ref, fetched_ref, in_ref, out_ref, basis_ref, weight_ref, part_ref, grad_ref
):
    narrow, row_count = back_ref.shape
    lanes = lanes_of(row_count)
    groups = row_count // lanes

    @pl.when(pl.program_id(0) == 0)
    def _():
        grad_ref[...] = jnp.zeros_like(grad_ref)

    high, lane_hot = split_index(out_ref[0], lanes)
    message = pick_rows(stack_groups(back_ref[...], lanes), high, lane_hot, narrow)
    back_coef = (message * fetched_ref[...].astype(F32)).astype(BF16)
    grad_ref[...] += contract(basis_ref[...], back_coef, 1, 1)
    message = message * contract(weight_ref[...], basis_ref[...], 0, 0)
    high, lane_hot = split_index(in_ref[0], lanes)
    part = place_rows(message, high, lane_hot, groups)
    for g in range(groups):
        part_ref[0, :, g * lanes : (g + 1) * lanes] = part[g * narrow : (g + 1) * narrow].astype(
            BF16
        )


def final_kernel(back_ref, slope_ref, edge_ref, summed_ref, weight_ref, edge_grad_ref, grad_ref):
    @pl.when(pl.program_id(0) == 0)
    def _():
        grad_ref[...] = jnp.zeros_like(grad_ref)

    back_pre = (back_ref[...].astype(F32) * slope_ref[...]).astype(BF16)
    grad_ref[...] += contract(back_pre, edge_ref[...], 1, 0)
    edge_grad_ref[...] = (
        summed_ref[...].astype(F32) + contract(back_pre, weight_ref[...], 0, 1)
    ).astype(BF16)


def call(kernel, grid, in_specs, out_specs, out_shape, flops, transcendentals=0, scratch=()):
    def run(*operands):
        size = sum(x.size * x.dtype.itemsize for x in operands)
        size += sum(x.size * x.dtype.itemsize for x in out_shape)
        return pl.pallas_call(
            kernel,
            grid=grid,
            in_specs=in_specs,
            out_specs=out_specs,
            out_shape=out_shape,
            scratch_shapes=scratch,
            compiler_params=pltpu.CompilerParams(vmem_limit_bytes=VMEM_LIMIT),
            cost_estimate=pl.CostEstimate(
                flops=flops, bytes_accessed=size, transcendentals=transcendentals
            ),
        )(*operands)

    return run


def whole(*shape):
    return pl.BlockSpec(shape, lambda i: (0,) * len(shape))


def local(
    edge_state,
    cotangent,
    edge_count,
    triplet_basis,
    triplet_in,
    triplet_out,
    down_weight,
    basis_weight,
    bilinear_weight,
    up_weight,
    first_weight,
    second_weight,
):
    edge_rows = edge_state[0]
    row_count, wide = edge_rows.shape
    shards = lax.axis_size("graph")
    narrow = down_weight.shape[1]
    basis = triplet_basis[0]
    basis_width, tri_rows = basis.shape
    slots = tri_rows // shards
    lanes = lanes_of(row_count)
    in_local = triplet_in.reshape(shards, 1, slots)
    out_local = triplet_out.reshape(shards, 1, slots)
    tile = math.gcd(row_count, 512)
    tiles = row_count // tile

    def shape(dims, dtype):
        return jax.ShapeDtypeStruct(dims, dtype)

    down_rows, down_slope = call(
        down_kernel,
        (tiles,),
        [pl.BlockSpec((tile, wide), lambda i: (i, 0)), whole(wide, narrow)],
        [pl.BlockSpec((narrow, tile), lambda i: (0, i))] * 2,
        [shape((narrow, row_count), BF16), shape((narrow, row_count), F32)],
        2 * row_count * wide * narrow,
        row_count * narrow,
    )(edge_rows, down_weight)

    all_rows = lax.all_gather(down_rows, "graph", axis=0, tiled=False)

    index_spec = pl.BlockSpec((1, 1, slots), lambda j: (j, 0, 0))
    basis_spec = pl.BlockSpec((basis_width, slots), lambda j: (0, j))
    slot_spec = pl.BlockSpec((narrow, slots), lambda j: (0, j))
    part_spec = pl.BlockSpec((1, narrow, row_count), lambda j: (j, 0, 0))
    move_flops = 4 * tri_rows * row_count * narrow
    gathered, fetched = call(
        forward_kernel,
        (shards,),
        [part_spec, index_spec, index_spec, basis_spec, whole(basis_width, narrow)],
        [whole(narrow, row_count), slot_spec],
        [shape((narrow, row_count), BF16), shape((narrow, tri_rows), BF16)],
        move_flops,
        scratch=[pltpu.VMEM((narrow * (row_count // lanes), lanes), F32)],
    )(all_rows, in_local, out_local, basis, basis_weight)

    row_spec = pl.BlockSpec((tile, wide), lambda i: (i, 0))
    column_spec = pl.BlockSpec((narrow, tile), lambda i: (0, i))
    back_summed, back_gathered, bilinear_grad, up_grad, first_grad, second_grad = call(
        dense_kernel,
        (tiles,),
        [
            pl.BlockSpec(memory_space=pltpu.SMEM),
            row_spec,
            row_spec,
            column_spec,
            whole(narrow, narrow),
            whole(narrow, wide),
            whole(wide, wide),
            whole(wide, wide),
        ],
        [
            row_spec,
            column_spec,
            whole(narrow, narrow),
            whole(narrow, wide),
            whole(wide, wide),
            whole(wide, wide),
        ],
        [
            shape((row_count, wide), BF16),
            shape((narrow, row_count), BF16),
            shape((narrow, narrow), F32),
            shape((narrow, wide), F32),
            shape((wide, wide), F32),
            shape((wide, wide), F32),
        ],
        12 * row_count * wide * wide + 6 * row_count * wide * narrow,
        3 * row_count * wide,
    )(
        edge_count,
        edge_rows,
        cotangent[0],
        gathered,
        bilinear_weight,
        up_weight,
        first_weight,
        second_weight,
    )

    first_grad, second_grad = lax.psum((first_grad, second_grad), ("dp", "graph"))

    parts, basis_grad = call(
        backward_kernel,
        (shards,),
        [
            whole(narrow, row_count),
            slot_spec,
            index_spec,
            index_spec,
            basis_spec,
            whole(basis_width, narrow),
        ],
        [part_spec, whole(basis_width, narrow)],
        [shape((shards, narrow, row_count), BF16), shape((basis_width, narrow), F32)],
        move_flops,
    )(back_gathered, fetched, in_local, out_local, basis, basis_weight)

    back_down = lax.psum_scatter(parts, "graph", scatter_dimension=0, tiled=False)

    edge_grad, down_grad = call(
        final_kernel,
        (tiles,),
        [column_spec, column_spec, row_spec, row_spec, whole(wide, narrow)],
        [row_spec, whole(narrow, wide)],
        [shape((row_count, wide), BF16), shape((narrow, wide), F32)],
        4 * row_count * wide * narrow,
    )(back_down, down_slope, edge_rows, back_summed, down_weight)

    down_grad, basis_grad, bilinear_grad, up_grad = lax.psum(
        (down_grad, basis_grad, bilinear_grad, up_grad), ("dp", "graph")
    )
    grad_scale = 1.0 / math.sqrt(lax.axis_size("dp") * shards * row_count)
    return (
        edge_grad[None],
        down_grad.T * grad_scale,
        basis_grad * grad_scale,
        bilinear_grad * grad_scale,
        up_grad * grad_scale,
        first_grad * grad_scale,
        second_grad * grad_scale,
    )


def solution(mesh):
    in_specs = (
        P("dp", "graph", None),
        P("dp", "graph", None),
        P("dp", "graph"),
        P("dp", None, "graph"),
        P("dp", "graph"),
        P("dp", "graph"),
        P(),
        P(),
        P(),
        P(),
        P(),
        P(),
    )
    out_specs = (P("dp", "graph", None), P(), P(), P(), P(), P(), P())
    return jax.shard_map(local, mesh=mesh, in_specs=in_specs, out_specs=out_specs, check_vma=False)
```

```python
import functools
import math

import jax
import jax.numpy as jnp
from jax import lax
from jax.experimental import pallas as pl
from jax.experimental.pallas import tpu as pltpu
from jax.sharding import PartitionSpec as P

HALF = 0.7071067811865476
F32 = jnp.float32
BF16 = jnp.bfloat16
VMEM_LIMIT = 48 * 1024 * 1024


def contract(left, right, left_dim, right_dim):
    return lax.dot_general(
        left, right, (((left_dim,), (right_dim,)), ((), ())), preferred_element_type=F32
    )


def sigmoid(value):
    return 0.5 + 0.5 * jnp.tanh(0.5 * value)


def split_index(index_row, lanes):
    slots = index_row.shape[1]
    low = jnp.bitwise_and(index_row, lanes - 1)
    high = jnp.right_shift(index_row, lanes.bit_length() - 1)
    lane_ids = lax.broadcasted_iota(jnp.int32, (lanes, slots), 0)
    return high, jnp.where(lane_ids == low, 1.0, 0.0).astype(BF16)


def stack(rows, lanes):
    groups = rows.shape[1] // lanes
    return jnp.concatenate([rows[:, g * lanes : (g + 1) * lanes] for g in range(groups)], axis=0)


def unstack(rows, narrow):
    groups = rows.shape[0] // narrow
    return jnp.concatenate([rows[g * narrow : (g + 1) * narrow] for g in range(groups)], axis=1)


def pick_rows(stacked, high, lane_hot, narrow):
    groups = stacked.shape[0] // narrow
    every = contract(stacked, lane_hot, 1, 0)
    picked = jnp.where(high == 0, every[:narrow], 0.0)
    for g in range(1, groups):
        picked = jnp.where(high == g, every[g * narrow : (g + 1) * narrow], picked)
    return picked


def place_rows(values, high, lane_hot, groups):
    zero = jnp.zeros((), values.dtype)
    spread = jnp.concatenate([jnp.where(high == g, values, zero) for g in range(groups)], axis=0)
    return contract(spread.astype(BF16), lane_hot, 1, 1)


def down_kernel(edge_ref, weight_ref, rows_ref, slope_ref):
    lanes = rows_ref.shape[1]
    pre = contract(weight_ref[...], edge_ref[...], 0, 1)
    logistic = sigmoid(pre)
    rows_ref[...] = stack((pre * logistic).astype(BF16), lanes)
    slope_ref[...] = stack(logistic * (1.0 + pre * (1.0 - logistic)), lanes)


def forward_kernel(blocks, first, plan_ref, *refs):
    rows = refs[:blocks]
    in_ref, out_ref, basis_ref, weight_ref = refs[blocks : blocks + 4]
    total_ref, fetched_ref = refs[-2:]
    narrow = weight_ref.shape[1]
    groups = total_ref.shape[0] // narrow
    lanes = total_ref.shape[1]
    slots = in_ref.shape[2]
    if first:
        total_ref[...] = jnp.zeros_like(total_ref)
    else:
        total_ref[...] = refs[blocks + 4][...]

    for i in range(blocks):

        @pl.when(plan_ref[1, i] == 1)
        def _():
            shard = plan_ref[0, i]
            at = pl.ds(pl.multiple_of(shard * slots, slots), slots)
            high, lane_hot = split_index(in_ref[shard], lanes)
            fetched = pick_rows(rows[i][...], high, lane_hot, narrow)
            fetched_ref[i] = fetched.astype(BF16)
            message = contract(weight_ref[...], basis_ref[:, at], 0, 0) * fetched
            high, lane_hot = split_index(out_ref[shard], lanes)
            total_ref[...] += place_rows(message, high, lane_hot, groups)


def dense_kernel(
    count_ref,
    edge_ref,
    cotangent_ref,
    gathered_ref,
    bilinear_ref,
    up_ref,
    first_ref,
    second_ref,
    summed_ref,
    back_ref,
    grads_ref,
    total,
):
    step = pl.program_id(0)
    tile, wide = edge_ref.shape
    narrow = bilinear_ref.shape[0]
    lanes = gathered_ref.shape[1]

    @pl.when(step == 0)
    def _():
        total[...] = jnp.zeros_like(total)

    gathered = unstack(gathered_ref[...].astype(BF16), narrow)
    mixed = contract(bilinear_ref[...], gathered, 0, 0).astype(BF16)
    pre_up = contract(mixed, up_ref[...], 0, 0)
    up_logistic = sigmoid(pre_up)
    summed_half = (edge_ref[...].astype(F32) + pre_up * up_logistic).astype(BF16)
    pre_first = contract(summed_half, first_ref[...], 1, 0)
    first_logistic = sigmoid(pre_first)
    first_rows = (pre_first * first_logistic).astype(BF16)
    pre_second = contract(first_rows, second_ref[...], 1, 0)
    logistic = sigmoid(pre_second)
    row_ids = step * tile + lax.broadcasted_iota(jnp.int32, (tile, 1), 0)
    live = jnp.where(row_ids < count_ref[0, 0], HALF, 0.0)
    back_top = cotangent_ref[...].astype(F32) * live
    back_second = (back_top * (logistic * (1.0 + pre_second * (1.0 - logistic)))).astype(BF16)
    slope = first_logistic * (1.0 + pre_first * (1.0 - first_logistic))
    back_first = (contract(back_second, second_ref[...], 1, 1) * slope).astype(BF16)
    back_summed = back_top + contract(back_first, first_ref[...], 1, 1)
    summed_ref[...] = back_summed.astype(BF16)
    slope = up_logistic * (1.0 + pre_up * (1.0 - up_logistic))
    back_up = (back_summed * slope).astype(BF16)
    back_mixed = contract(up_ref[...], back_up, 1, 1).astype(BF16)
    back_ref[...] = stack(contract(bilinear_ref[...], back_mixed, 1, 0).astype(BF16), lanes)
    total[:wide] += contract(summed_half, back_first, 0, 0)
    total[wide : 2 * wide] += contract(first_rows, back_second, 0, 0)
    total[2 * wide : 2 * wide + narrow] += contract(mixed, back_up, 1, 0)
    total[2 * wide + narrow :, :narrow] += contract(gathered, back_mixed, 1, 1)

    @pl.when(step == pl.num_programs(0) - 1)
    def _():
        parts, _, width = grads_ref.shape
        for p in range(parts):
            grads_ref[p] = total[:, p * width : (p + 1) * width].astype(BF16)


def backward_kernel(blocks, first, plan_ref, back_ref, fetched_ref, *refs):
    in_ref, out_ref, basis_ref, weight_ref = refs[:4]
    parts = refs[-1 - blocks : -1]
    grad_ref = refs[-1]
    narrow = weight_ref.shape[1]
    groups = back_ref.shape[0] // narrow
    lanes = back_ref.shape[1]
    slots = in_ref.shape[2]
    if first:
        grad_ref[...] = jnp.zeros_like(grad_ref)
    else:
        grad_ref[...] = refs[4][...]

    for i in range(blocks):

        @pl.when(plan_ref[1, i] == 1)
        def _():
            shard = plan_ref[0, i]
            at = pl.ds(pl.multiple_of(shard * slots, slots), slots)
            basis = basis_ref[:, at]
            high, lane_hot = split_index(out_ref[shard], lanes)
            message = pick_rows(back_ref[...], high, lane_hot, narrow)
            back_coef = (message * fetched_ref[i].astype(F32)).astype(BF16)
            grad_ref[...] += contract(basis, back_coef, 1, 1)
            message = message * contract(weight_ref[...], basis, 0, 0)
            high, lane_hot = split_index(in_ref[shard], lanes)
            parts[i][...] = place_rows(message, high, lane_hot, groups).astype(BF16)

        @pl.when(plan_ref[1, i] == 0)
        def _():
            parts[i][...] = jnp.zeros_like(parts[i])


def final_kernel(count, *refs):
    parts = refs[:count]
    slope_ref, edge_ref, summed_ref, weight_ref, edge_grad_ref, grad_ref = refs[count:]
    narrow = weight_ref.shape[1]

    @pl.when(pl.program_id(0) == 0)
    def _():
        grad_ref[...] = jnp.zeros_like(grad_ref)

    back_down = parts[0][...].astype(F32)
    for part in parts[1:]:
        back_down += part[...].astype(F32)
    back_pre = unstack((back_down * slope_ref[...]).astype(BF16), narrow)
    grad_ref[...] += contract(back_pre, edge_ref[...], 1, 0)
    edge_grad_ref[...] = (
        summed_ref[...].astype(F32) + contract(back_pre, weight_ref[...], 0, 1)
    ).astype(BF16)


def call(kernel, grid, in_specs, out_specs, out_shape, flops, transcendentals=0, scratch=()):
    def run(*operands):
        size = sum(x.size * x.dtype.itemsize for x in operands)
        size += sum(x.size * x.dtype.itemsize for x in out_shape)
        return pl.pallas_call(
            kernel,
            grid=grid,
            in_specs=in_specs,
            out_specs=out_specs,
            out_shape=out_shape,
            scratch_shapes=scratch,
            compiler_params=pltpu.CompilerParams(vmem_limit_bytes=VMEM_LIMIT),
            cost_estimate=pl.CostEstimate(
                flops=flops, bytes_accessed=size, transcendentals=transcendentals
            ),
        )(*operands)

    return run


def whole(*shape):
    return pl.BlockSpec(shape, lambda *_: (0,) * len(shape))


SMEM = pl.BlockSpec(memory_space=pltpu.SMEM)


def shape(dims, dtype):
    return jax.ShapeDtypeStruct(dims, dtype)


class Line:
    def __init__(self):
        self.size = lax.axis_size("graph")
        self.cores = 2 if self.size % 2 == 0 else 1
        self.chips = math.gcd(self.size // self.cores, 4)
        self.span = self.chips * self.cores
        self.groups = self.size // self.span
        me = lax.axis_index("graph")
        self.core = me % self.cores
        self.chip = me // self.cores % self.chips
        self.group = me // self.span

    def hop(self, array, step, senders):
        pairs = [
            (base + chip * self.cores + core, base + (chip + step) * self.cores + core)
            for base in range(0, self.size, self.span)
            for chip in senders
            for core in range(self.cores)
        ]
        return lax.ppermute(array, "graph", pairs)

    def swap(self, array):
        return lax.ppermute(array, "graph", [(g, g ^ 1) for g in range(self.size)])

    def turn(self, array):
        return lax.ppermute(array, "graph", turned(self.size, self.groups, self.span, -1))

    def turn_back(self, array):
        return lax.ppermute(array, "graph", turned(self.size, self.groups, self.span, 1))

    def plan(self, turn, offsets):
        shards, exist = [], []
        base = (self.group + turn) % self.groups * self.span
        for offset in offsets:
            chip = self.chip + offset
            inside = jnp.logical_and(chip >= 0, chip < self.chips)
            chip = jnp.clip(chip, 0, self.chips - 1)
            for other in range(self.cores):
                core = self.core if other == 0 else 1 - self.core
                shards.append(base + chip * self.cores + core)
                exist.append(inside.astype(jnp.int32))
        return jnp.stack([jnp.stack(shards), jnp.stack(exist)]).astype(jnp.int32)


def add(*arrays):
    return sum(a.astype(F32) for a in arrays).astype(BF16)


def exchange_sum(pieces, axis, size, me, stride=1):
    count = lax.axis_size(axis)
    arrived = [lax.dynamic_index_in_dim(pieces, me, 0, keepdims=False)]
    for turn in range(1, size):
        away = lax.dynamic_index_in_dim(pieces, (me + turn) % size, 0, keepdims=False)
        arrived.append(lax.ppermute(away, axis, turned(count, size, stride, turn)))
    return add(*arrived)


def turned(count, size, stride, turn):
    pairs = []
    for g in range(count):
        place = g // stride % size
        pairs.append((g, g + ((place + turn) % size - place) * stride))
    return pairs


def exchange_all(piece, axis, size, me, stride=1):
    count = lax.axis_size(axis)
    out = jnp.zeros((size,) + piece.shape, piece.dtype)
    out = lax.dynamic_update_index_in_dim(out, piece, me, 0)
    for turn in range(1, size):
        other = lax.ppermute(piece, axis, turned(count, size, stride, turn))
        out = lax.dynamic_update_index_in_dim(out, other, (me - turn) % size, 0)
    return out


def sum_everywhere(array, line):
    rows, lanes = array.shape
    stages = [("graph", line.cores, line.core, 1)]
    stages.append(("dp", lax.axis_size("dp"), lax.axis_index("dp"), 1))
    stages.append(("graph", line.chips, line.chip, line.cores))
    stages.append(("graph", line.groups, line.group, line.span))
    for axis, size, me, stride in stages:
        if size > 1:
            pieces = array.reshape(size, array.shape[0] // size, lanes)
            array = exchange_sum(pieces, axis, size, me, stride)
    for axis, size, me, stride in stages[::-1]:
        if size > 1:
            array = exchange_all(array, axis, size, me, stride)
            array = array.reshape(-1, lanes)
    return array


def local(
    edge_state,
    cotangent,
    edge_count,
    triplet_basis,
    triplet_in,
    triplet_out,
    down_weight,
    basis_weight,
    bilinear_weight,
    up_weight,
    first_weight,
    second_weight,
):
    edge_rows = edge_state[0]
    row_count, wide = edge_rows.shape
    line = Line()
    shards, cores, chips = line.size, line.cores, line.chips
    narrow = down_weight.shape[1]
    basis = triplet_basis[0]
    basis_width, tri_rows = basis.shape
    slots = tri_rows // shards
    lanes = math.gcd(row_count, 256)
    stacked = narrow * (row_count // lanes)
    in_local = triplet_in.reshape(shards, 1, slots)
    out_local = triplet_out.reshape(shards, 1, slots)
    tile = math.gcd(row_count, 512)
    tiles = row_count // tile
    row_spec = pl.BlockSpec((tile, wide), lambda i: (i, 0))
    stack_spec = pl.BlockSpec((narrow * (tile // lanes), lanes), lambda i: (i, 0))

    down_rows, down_slope = call(
        down_kernel,
        (tiles,),
        [row_spec, whole(wide, narrow)],
        [stack_spec] * 2,
        [shape((stacked, lanes), BF16), shape((stacked, lanes), F32)],
        2 * row_count * wide * narrow,
        row_count * narrow,
    )(edge_rows, down_weight)

    block_flops = 4 * slots * row_count * narrow
    triplet_specs = [
        whole(shards, 1, slots),
        whole(shards, 1, slots),
        whole(basis_width, tri_rows),
        whole(basis_width, narrow),
    ]
    triplets = (in_local, out_local, basis, basis_weight)

    def forward(plan, rows, total):
        extra = () if total is None else (total,)
        return call(
            functools.partial(forward_kernel, len(rows), total is None),
            (),
            [SMEM]
            + [whole(stacked, lanes)] * len(rows)
            + triplet_specs
            + [whole(stacked, lanes)] * len(extra),
            [whole(stacked, lanes), whole(len(rows), narrow, slots)],
            [shape((stacked, lanes), F32), shape((len(rows), narrow, slots), BF16)],
            len(rows) * block_flops,
        )(plan, *rows, *triplets, *extra)

    def both(array):
        return [array, line.swap(array)] if cores == 2 else [array]

    def forward_line(turn, rows, total):
        fetched = []
        total, got = forward(line.plan(turn, (0,)), both(rows), total)
        fetched.append(got)
        from_left = from_right = rows
        for d in range(1, chips):
            from_left = line.hop(from_left, 1, range(d - 1, chips - 1))
            from_right = line.hop(from_right, -1, range(1, chips - d + 1))
            plan = line.plan(turn, (-d, d))
            total, got = forward(plan, both(from_left) + both(from_right), total)
            fetched.append(got)
        return total, fetched

    total, fetched = forward_line(0, down_rows, None)
    if line.groups > 1:

        def forward_turn(carry, turn):
            rows, total = carry
            rows = line.turn(rows)
            total, got = forward_line(turn, rows, total)
            return (rows, total), got

        (_, total), more_fetched = lax.scan(
            forward_turn, (down_rows, total), jnp.arange(1, line.groups)
        )

    grad_rows = 2 * wide + 2 * narrow
    grad_parts = wide // 128
    back_summed, back_gathered, dense_grads = call(
        dense_kernel,
        (tiles,),
        [
            SMEM,
            row_spec,
            row_spec,
            stack_spec,
            whole(narrow, narrow),
            whole(narrow, wide),
            whole(wide, wide),
            whole(wide, wide),
        ],
        [row_spec, stack_spec, whole(grad_parts, grad_rows, 128)],
        [
            shape((row_count, wide), BF16),
            shape((stacked, lanes), BF16),
            shape((grad_parts, grad_rows, 128), BF16),
        ],
        12 * row_count * wide * wide + 6 * row_count * wide * narrow,
        3 * row_count * wide,
        scratch=[pltpu.VMEM((grad_rows, wide), F32)],
    )(
        edge_count,
        edge_rows,
        cotangent[0],
        total,
        bilinear_weight,
        up_weight,
        first_weight,
        second_weight,
    )

    def backward(plan, got, grad):
        blocks = got.shape[0]
        extra = () if grad is None else (grad,)
        out = call(
            functools.partial(backward_kernel, blocks, grad is None),
            (),
            [SMEM, whole(stacked, lanes), whole(blocks, narrow, slots)]
            + triplet_specs
            + [whole(basis_width, narrow)] * len(extra),
            [whole(stacked, lanes)] * blocks + [whole(basis_width, narrow)],
            [shape((stacked, lanes), BF16)] * blocks + [shape((basis_width, narrow), F32)],
            blocks * block_flops,
        )(plan, back_gathered, got, *triplets, *extra)
        return out[:-1], out[-1]

    def own_plane(parts):
        return [parts[0], line.swap(parts[1])] if cores == 2 else [parts[0]]

    def backward_line(turn, fetched, basis_grad):
        to_left, to_right = [], []
        for d in range(chips - 1, 0, -1):
            parts, basis_grad = backward(line.plan(turn, (-d, d)), fetched[d], basis_grad)
            left = add(*own_plane(parts[:cores]), *to_left)
            right = add(*own_plane(parts[cores:]), *to_right)
            to_left = [line.hop(left, -1, range(d, chips))]
            to_right = [line.hop(right, 1, range(0, chips - d))]
        parts, basis_grad = backward(line.plan(turn, (0,)), fetched[0], basis_grad)
        return own_plane(parts) + to_left + to_right, basis_grad

    back_parts, basis_grad = backward_line(0, fetched, None)
    if line.groups > 1:

        def backward_turn(carry, one):
            traveling, basis_grad = carry
            turn, got = one
            parts, basis_grad = backward_line(turn, got, basis_grad)
            return (line.turn_back(add(traveling, *parts)), basis_grad), None

        (traveling, basis_grad), _ = lax.scan(
            backward_turn,
            (jnp.zeros((stacked, lanes), BF16), basis_grad),
            (jnp.arange(1, line.groups), more_fetched),
            reverse=True,
        )
        back_parts = back_parts + [traveling]

    dense_grads = sum_everywhere(dense_grads.reshape(grad_parts * grad_rows, 128), line)

    edge_grad, down_grad = call(
        functools.partial(final_kernel, len(back_parts)),
        (tiles,),
        [stack_spec] * len(back_parts) + [stack_spec, row_spec, row_spec, whole(wide, narrow)],
        [row_spec, whole(narrow, wide)],
        [shape((row_count, wide), BF16), shape((narrow, wide), F32)],
        4 * row_count * wide * narrow,
    )(*back_parts, down_slope, edge_rows, back_summed, down_weight)

    small = jnp.concatenate(
        [down_grad, jnp.pad(basis_grad, ((0, narrow - basis_width), (0, wide - narrow)))]
    ).astype(BF16)
    small = small.reshape(2 * narrow, wide // 128, 128).transpose(1, 0, 2).reshape(-1, 128)
    small = sum_everywhere(small, line)

    scale = 1.0 / math.sqrt(lax.axis_size("dp") * shards * row_count)

    def joined(flat, rows):
        return (
            flat.reshape(-1, rows, 128).transpose(1, 0, 2).reshape(rows, wide).astype(F32) * scale
        )

    small = joined(small, 2 * narrow)
    dense_grads = joined(dense_grads, grad_rows)
    return (
        edge_grad[None],
        small[:narrow].T,
        small[narrow : narrow + basis_width, :narrow],
        dense_grads[2 * wide + narrow :, :narrow],
        dense_grads[2 * wide : 2 * wide + narrow],
        dense_grads[:wide],
        dense_grads[wide : 2 * wide],
    )


def solution(mesh):
    in_specs = (
        P("dp", "graph", None),
        P("dp", "graph", None),
        P("dp", "graph"),
        P("dp", None, "graph"),
        P("dp", "graph"),
        P("dp", "graph"),
        P(),
        P(),
        P(),
        P(),
        P(),
        P(),
    )
    out_specs = (P("dp", "graph", None), P(), P(), P(), P(), P(), P())
    return jax.shard_map(local, mesh=mesh, in_specs=in_specs, out_specs=out_specs, check_vma=False)
```

```python
import functools
import math

import jax
import jax.numpy as jnp
from jax import lax
from jax.experimental import pallas as pl
from jax.experimental.pallas import tpu as pltpu
from jax.sharding import PartitionSpec as P

HALF = 0.7071067811865476
F32 = jnp.float32
BF16 = jnp.bfloat16
VMEM_LIMIT = 48 * 1024 * 1024


def contract(left, right, left_dim, right_dim):
    return lax.dot_general(
        left, right, (((left_dim,), (right_dim,)), ((), ())), preferred_element_type=F32
    )


def sigmoid(value):
    return 0.5 + 0.5 * jnp.tanh(0.5 * value)


def split_index(index_row, lanes):
    slots = index_row.shape[1]
    low = jnp.bitwise_and(index_row, lanes - 1)
    high = jnp.right_shift(index_row, lanes.bit_length() - 1)
    lane_ids = lax.broadcasted_iota(jnp.int32, (lanes, slots), 0)
    return high, jnp.where(lane_ids == low, 1.0, 0.0).astype(BF16)


def stack(rows, lanes):
    groups = rows.shape[1] // lanes
    return jnp.concatenate([rows[:, g * lanes : (g + 1) * lanes] for g in range(groups)], axis=0)


def unstack(rows, narrow):
    groups = rows.shape[0] // narrow
    return jnp.concatenate([rows[g * narrow : (g + 1) * narrow] for g in range(groups)], axis=1)


def pick_rows(stacked, high, lane_hot, narrow):
    groups = stacked.shape[0] // narrow
    every = contract(stacked, lane_hot, 1, 0)
    picked = jnp.where(high == 0, every[:narrow], 0.0)
    for g in range(1, groups):
        picked = jnp.where(high == g, every[g * narrow : (g + 1) * narrow], picked)
    return picked


def place_rows(values, high, lane_hot, groups):
    zero = jnp.zeros((), values.dtype)
    spread = jnp.concatenate([jnp.where(high == g, values, zero) for g in range(groups)], axis=0)
    return contract(spread.astype(BF16), lane_hot, 1, 1)


def down_kernel(edge_ref, weight_ref, rows_ref, slope_ref):
    lanes = rows_ref.shape[1]
    pre = contract(weight_ref[...], edge_ref[...], 1, 1)
    logistic = sigmoid(pre)
    rows_ref[...] = stack((pre * logistic).astype(BF16), lanes)
    slope_ref[...] = stack(logistic * (1.0 + pre * (1.0 - logistic)), lanes)


def forward_kernel(shard_ref, rows_ref, *refs):
    ends, basis, weight_ref = refs[:2], refs[2:4], refs[4]
    totals, fetched_ref = refs[-3:-1], refs[-1]
    shard = shard_ref[0]
    narrow = weight_ref.shape[1]
    groups = totals[0].shape[0] // narrow
    lanes = totals[0].shape[1]
    slots = ends[0].shape[3]
    at = pl.ds(pl.multiple_of(shard * slots, slots), slots)
    for i in range(2):
        high, lane_hot = split_index(ends[i][0, shard], lanes)
        fetched = pick_rows(rows_ref[...], high, lane_hot, narrow)
        fetched_ref[i] = fetched.astype(BF16)
        message = contract(weight_ref[...], basis[i][:, at], 0, 0) * fetched
        high, lane_hot = split_index(ends[i][1, shard], lanes)
        placed = place_rows(message, high, lane_hot, groups)
        if len(refs) == 10:
            placed += refs[5 + i][...]
        totals[i][...] = placed


def dense_kernel(
    count_ref,
    edge_ref,
    cotangent_ref,
    gathered_ref,
    more_ref,
    bilinear_ref,
    up_ref,
    first_ref,
    second_ref,
    summed_ref,
    back_ref,
    grads_ref,
    total,
):
    step = pl.program_id(0)
    tile, wide = edge_ref.shape
    narrow = bilinear_ref.shape[0]
    lanes = gathered_ref.shape[1]

    @pl.when(step == 0)
    def _():
        total[...] = jnp.zeros_like(total)

    gathered = unstack((gathered_ref[...] + more_ref[...]).astype(BF16), narrow)
    mixed = contract(bilinear_ref[...], gathered, 0, 0).astype(BF16)
    pre_up = contract(mixed, up_ref[...], 0, 0)
    up_logistic = sigmoid(pre_up)
    summed_half = (edge_ref[...].astype(F32) + pre_up * up_logistic).astype(BF16)
    pre_first = contract(summed_half, first_ref[...], 1, 0)
    first_logistic = sigmoid(pre_first)
    first_rows = (pre_first * first_logistic).astype(BF16)
    pre_second = contract(first_rows, second_ref[...], 1, 0)
    logistic = sigmoid(pre_second)
    row_ids = step * tile + lax.broadcasted_iota(jnp.int32, (tile, 1), 0)
    live = jnp.where(row_ids < count_ref[0, 0], HALF, 0.0)
    back_top = cotangent_ref[...].astype(F32) * live
    back_second = (back_top * (logistic * (1.0 + pre_second * (1.0 - logistic)))).astype(BF16)
    slope = first_logistic * (1.0 + pre_first * (1.0 - first_logistic))
    back_first = (contract(back_second, second_ref[...], 1, 1) * slope).astype(BF16)
    back_summed = back_top + contract(back_first, first_ref[...], 1, 1)
    summed_ref[...] = back_summed.astype(BF16)
    slope = up_logistic * (1.0 + pre_up * (1.0 - up_logistic))
    back_up = (back_summed * slope).astype(BF16)
    back_mixed = contract(up_ref[...], back_up, 1, 1).astype(BF16)
    back_ref[...] = stack(contract(bilinear_ref[...], back_mixed, 1, 0).astype(BF16), lanes)
    total[:wide] += contract(summed_half, back_first, 0, 0)
    total[wide : 2 * wide] += contract(first_rows, back_second, 0, 0)
    total[2 * wide : 2 * wide + narrow] += contract(mixed, back_up, 1, 0)
    total[2 * wide + narrow :, :narrow] += contract(gathered, back_mixed, 1, 1)

    @pl.when(step == pl.num_programs(0) - 1)
    def _():
        grads_ref[...] = total[...].astype(BF16)


def backward_kernel(shard_ref, own_ref, sibling_ref, fetched_ref, *refs):
    ends, basis, weight_ref = refs[:2], refs[2:4], refs[4]
    part_ref, grad_ref = refs[-2:]
    shard = shard_ref[0]
    narrow = weight_ref.shape[1]
    groups = part_ref.shape[0] // narrow
    lanes = part_ref.shape[1]
    slots = ends[0].shape[3]
    at = pl.ds(pl.multiple_of(shard * slots, slots), slots)
    grad = refs[5][...] if len(refs) == 8 else jnp.zeros(grad_ref.shape, F32)
    part = jnp.zeros(part_ref.shape, F32)
    for i, back_ref in enumerate((own_ref, sibling_ref)):
        block = basis[i][:, at]
        high, lane_hot = split_index(ends[i][1, shard], lanes)
        message = pick_rows(back_ref[...], high, lane_hot, narrow)
        back_coef = (message * fetched_ref[i].astype(F32)).astype(BF16)
        grad += contract(block, back_coef, 1, 1)
        message = message * contract(weight_ref[...], block, 0, 0)
        high, lane_hot = split_index(ends[i][0, shard], lanes)
        part += place_rows(message, high, lane_hot, groups)
    part_ref[...] = part.astype(BF16)
    grad_ref[...] = grad


def final_kernel(count, *refs):
    parts = refs[:count]
    slope_ref, edge_ref, summed_ref, weight_ref, basis_ref, edge_grad_ref, grads_ref, total = refs[
        count:
    ]
    step = pl.program_id(0)
    narrow = weight_ref.shape[0]
    basis_width = basis_ref.shape[0]

    @pl.when(step == 0)
    def _():
        total[...] = jnp.zeros_like(total)

    back_down = parts[0][...].astype(F32)
    for part in parts[1:]:
        back_down += part[...].astype(F32)
    back_pre = unstack((back_down * slope_ref[...]).astype(BF16), narrow)
    total[:narrow] += contract(back_pre, edge_ref[...], 1, 0)
    edge_grad_ref[...] = (
        summed_ref[...].astype(F32) + contract(back_pre, weight_ref[...], 0, 0)
    ).astype(BF16)

    @pl.when(step == pl.num_programs(0) - 1)
    def _():
        total[narrow : narrow + basis_width, :narrow] = basis_ref[...]
        grads_ref[...] = total[...].astype(BF16)


def scale_kernel(scale, source_ref, *outs):
    row = 0
    for out in outs:
        rows, columns = out.shape
        out[...] = source_ref[row : row + rows, :columns].astype(F32) * scale
        row += rows


def call(kernel, grid, in_specs, out_specs, out_shape, flops, transcendentals=0, scratch=(), aliases=None):
    def run(*operands):
        size = sum(x.size * x.dtype.itemsize for x in operands)
        size += sum(x.size * x.dtype.itemsize for x in out_shape)
        return pl.pallas_call(
            kernel,
            grid=grid,
            in_specs=in_specs,
            out_specs=out_specs,
            out_shape=out_shape,
            scratch_shapes=scratch,
            input_output_aliases=aliases or {},
            compiler_params=pltpu.CompilerParams(vmem_limit_bytes=VMEM_LIMIT),
            cost_estimate=pl.CostEstimate(
                flops=flops, bytes_accessed=size, transcendentals=transcendentals
            ),
        )(*operands)

    return run


def whole(*shape):
    return pl.BlockSpec(shape, lambda *_: (0,) * len(shape))


SMEM = pl.BlockSpec(memory_space=pltpu.SMEM)


def shape(dims, dtype):
    return jax.ShapeDtypeStruct(dims, dtype)


def turned(count, size, stride, turn):
    pairs = []
    for g in range(count):
        place = g // stride % size
        pairs.append((g, g + ((place + turn) % size - place) * stride))
    return pairs


class Line:
    cores = 2

    def __init__(self):
        self.size = lax.axis_size("graph")
        self.chips = math.gcd(self.size // self.cores, 4)
        self.span = self.chips * self.cores
        self.groups = self.size // self.span
        me = lax.axis_index("graph")
        self.core = me % self.cores
        self.chip = me // self.cores % self.chips
        self.group = me // self.span

    def send(self, array, moves):
        pairs = [
            (base + one * self.cores + core, base + other * self.cores + core)
            for base in range(0, self.size, self.span)
            for one, other in moves
            for core in range(self.cores)
        ]
        return lax.ppermute(array, "graph", pairs)

    def trade(self, array, bit):
        return self.send(array, [(chip, chip ^ bit) for chip in range(self.chips)])

    def swap(self, array):
        return lax.ppermute(array, "graph", [(g, g ^ 1) for g in range(self.size)])

    def next_group(self, array):
        return lax.ppermute(array, "graph", turned(self.size, self.groups, self.span, -1))

    def last_group(self, array):
        return lax.ppermute(array, "graph", turned(self.size, self.groups, self.span, 1))

    def shard(self, turn, bits):
        group = (self.group + turn) % self.groups
        shard = group * self.span + (self.chip ^ bits) * self.cores + self.core
        return shard.astype(jnp.int32).reshape(1)


def add(*arrays):
    return sum(a.astype(F32) for a in arrays).astype(BF16)


def after(arrays, *others):
    return lax.optimization_barrier((tuple(arrays), others))[0]


def piece_of(array, size, me):
    rows = array.shape[0] // size
    return lax.dynamic_slice_in_dim(array, me * rows, rows, 0)


def scatter_sum(array, axis, size, me, stride):
    count = lax.axis_size(axis)
    arrived = [piece_of(array, size, me)]
    for turn in range(1, size):
        away = piece_of(array, size, (me + turn) % size)
        arrived.append(lax.ppermute(away, axis, turned(count, size, stride, turn)))
    return add(*arrived)


def gather_pieces(piece, axis, size, me, stride):
    count = lax.axis_size(axis)
    rows = piece.shape[0]
    out = jnp.zeros((size * rows, piece.shape[1]), piece.dtype)
    out = lax.dynamic_update_slice_in_dim(out, piece, me * rows, 0)
    for turn in range(1, size):
        other = lax.ppermute(piece, axis, turned(count, size, stride, turn))
        out = lax.dynamic_update_slice_in_dim(out, other, (me - turn) % size * rows, 0)
    return out


def sum_everywhere(array, line, scattered):
    stages = [("core", "graph", line.cores, line.core, 1)]
    stages.append(("dp", "dp", lax.axis_size("dp"), lax.axis_index("dp"), 1))
    stages.append(("chip", "graph", line.chips, line.chip, line.cores))
    stages.append(("group", "graph", line.groups, line.group, line.span))
    shared = []
    for name, axis, size, me, stride in stages:
        bit = 1
        while bit < size:
            if name == "dp" and name in scattered and array.shape[0] % (8 * size) == 0:
                array = scatter_sum(array, axis, size, me, stride)
                shared.append((axis, size, me, stride))
                break
            if name in scattered and array.shape[0] % 16 == 0:
                shift = stride * bit
                array = scatter_sum(array, axis, 2, me // bit % 2, shift)
                shared.append((axis, 2, me // bit % 2, shift))
            else:
                pairs = [(g, g ^ (stride * bit)) for g in range(lax.axis_size(axis))]
                array = add(array, lax.ppermute(array, axis, pairs))
            bit *= 2
    for axis, size, me, stride in shared[::-1]:
        array = gather_pieces(array, axis, size, me, stride)
    return array


def local(
    edge_state,
    cotangent,
    edge_count,
    triplet_basis,
    triplet_in,
    triplet_out,
    down_weight,
    basis_weight,
    bilinear_weight,
    up_weight,
    first_weight,
    second_weight,
):
    edge_rows = edge_state[0]
    row_count, wide = edge_rows.shape
    line = Line()
    shards, chips = line.size, line.chips
    narrow = down_weight.shape[1]
    down_weight = down_weight.T
    basis = triplet_basis[0]
    basis_width, tri_rows = basis.shape
    slots = tri_rows // shards
    lanes = math.gcd(row_count, 256)
    stacked = narrow * (row_count // lanes)
    tile = math.gcd(row_count, 512)
    tiles = row_count // tile
    row_spec = pl.BlockSpec((tile, wide), lambda i: (i, 0))
    stack_spec = pl.BlockSpec((narrow * (tile // lanes), lanes), lambda i: (i, 0))
    rows_spec = whole(stacked, lanes)

    ends = jnp.stack([triplet_in.reshape(shards, 1, slots), triplet_out.reshape(shards, 1, slots)])
    ends_sibling = line.swap(ends)
    basis_sibling = line.swap(basis)
    triplets = (ends, ends_sibling, basis, basis_sibling, basis_weight)
    triplet_specs = (
        [whole(2, shards, 1, slots)] * 2
        + [whole(basis_width, tri_rows)] * 2
        + [whole(basis_width, narrow)]
    )
    block_flops = 8 * slots * row_count * narrow

    down_rows, down_slope = call(
        down_kernel,
        (tiles,),
        [row_spec, whole(narrow, wide)],
        [stack_spec] * 2,
        [shape((stacked, lanes), BF16), shape((stacked, lanes), F32)],
        2 * row_count * wide * narrow,
        row_count * narrow,
    )(edge_rows, down_weight)

    def forward(shard, rows, totals):
        out = call(
            forward_kernel,
            (),
            [SMEM, rows_spec] + triplet_specs + [rows_spec] * len(totals),
            [rows_spec] * 2 + [whole(2, narrow, slots)],
            [shape((stacked, lanes), F32)] * 2 + [shape((2, narrow, slots), BF16)],
            block_flops,
            aliases={7 + i: i for i in range(len(totals))},
        )(shard, rows, *triplets, *totals)
        return tuple(out[:2]), out[2]

    def forward_line(turn, rows, totals):
        far = line.trade(rows, 2) if chips == 4 else None
        near = line.trade(rows, 1) if chips > 1 else None
        totals, got = forward(line.shard(turn, 0), rows, totals)
        fetched = [got]
        if chips > 1:
            totals, got = forward(line.shard(turn, 1), near, totals)
            fetched.append(got)
        if chips == 4:
            rows, far = after((rows, far), *totals)
            last = line.send(rows, [(1, 2), (2, 1)]) + line.send(far, [(2, 3), (1, 0)])
            totals, got = forward(line.shard(turn, 2), far, totals)
            fetched.append(got)
            totals, got = forward(line.shard(turn, 3), last, totals)
            fetched.append(got)
        return totals, fetched

    totals, fetched = forward_line(0, down_rows, ())
    if line.groups > 1:

        def forward_turn(carry, turn):
            rows, totals = carry
            rows = line.next_group(rows)
            totals, got = forward_line(turn, rows, totals)
            return (rows, totals), got

        (_, totals), more_fetched = lax.scan(
            forward_turn, (down_rows, totals), jnp.arange(1, line.groups)
        )

    grad_rows = 2 * wide + 2 * narrow
    back_summed, back_gathered, dense_grads = call(
        dense_kernel,
        (tiles,),
        [
            SMEM,
            row_spec,
            row_spec,
            stack_spec,
            stack_spec,
            whole(narrow, narrow),
            whole(narrow, wide),
            whole(wide, wide),
            whole(wide, wide),
        ],
        [row_spec, stack_spec, whole(grad_rows, wide)],
        [
            shape((row_count, wide), BF16),
            shape((stacked, lanes), BF16),
            shape((grad_rows, wide), BF16),
        ],
        12 * row_count * wide * wide + 6 * row_count * wide * narrow,
        3 * row_count * wide,
        scratch=[pltpu.VMEM((grad_rows, wide), F32)],
    )(
        edge_count,
        edge_rows,
        cotangent[0],
        totals[0],
        line.swap(totals[1]),
        bilinear_weight,
        up_weight,
        first_weight,
        second_weight,
    )
    back_sibling = line.swap(back_gathered)

    def backward(shard, got, grad):
        extra = () if grad is None else (grad,)
        return call(
            backward_kernel,
            (),
            [SMEM, rows_spec, rows_spec, whole(2, narrow, slots)]
            + triplet_specs
            + [whole(basis_width, narrow)] * len(extra),
            [rows_spec, whole(basis_width, narrow)],
            [shape((stacked, lanes), BF16), shape((basis_width, narrow), F32)],
            block_flops,
        )(shard, back_gathered, back_sibling, got, *triplets, *extra)

    def backward_line(turn, fetched, basis_grad):
        if chips == 4:
            last, basis_grad = backward(line.shard(turn, 3), fetched[3], basis_grad)
            passed = line.send(last, [(0, 1), (3, 2)])
            middle = line.send(last, [(1, 2), (2, 1)])
            far, basis_grad = backward(line.shard(turn, 2), fetched[2], basis_grad)
        if chips > 1:
            near, basis_grad = backward(line.shard(turn, 1), fetched[1], basis_grad)
        own, basis_grad = backward(line.shard(turn, 0), fetched[0], basis_grad)
        parts = [own]
        if chips == 4:
            passed, near = after((passed, near), own)
            parts += [middle, line.trade(add(far, passed), 2)]
            (near,) = after((near,), passed)
        if chips > 1:
            parts.append(line.trade(near, 1))
        return parts, basis_grad

    back_parts, basis_grad = backward_line(0, fetched, None)
    if line.groups > 1:

        def backward_turn(carry, one):
            traveling, basis_grad = carry
            turn, got = one
            parts, basis_grad = backward_line(turn, got, basis_grad)
            return (line.last_group(add(traveling, *parts)), basis_grad), None

        (traveling, basis_grad), _ = lax.scan(
            backward_turn,
            (jnp.zeros((stacked, lanes), BF16), basis_grad),
            (jnp.arange(1, line.groups), more_fetched),
            reverse=True,
        )
        back_parts = back_parts + [traveling]

    small_rows = narrow + basis_width
    edge_grad, small_grads = call(
        functools.partial(final_kernel, len(back_parts)),
        (tiles,),
        [stack_spec] * len(back_parts)
        + [stack_spec, row_spec, row_spec, whole(narrow, wide), whole(basis_width, narrow)],
        [row_spec, whole(small_rows, wide)],
        [shape((row_count, wide), BF16), shape((small_rows, wide), BF16)],
        4 * row_count * wide * narrow,
        scratch=[pltpu.VMEM((small_rows, wide), F32)],
    )(*back_parts, down_slope, edge_rows, back_summed, down_weight, basis_grad)

    dense_grads = sum_everywhere(dense_grads, line, ("core", "dp", "chip"))
    small_grads = sum_everywhere(small_grads, line, ("core",))
    scale = 1.0 / math.sqrt(lax.axis_size("dp") * shards * row_count)

    def scaled(source, *dims):
        return call(
            functools.partial(scale_kernel, scale),
            (),
            [whole(*source.shape)],
            [whole(*d) for d in dims],
            [shape(d, F32) for d in dims],
            source.size,
        )(source)

    first_grad, second_grad, up_grad, bilinear_grad = scaled(
        dense_grads, (wide, wide), (wide, wide), (narrow, wide), (narrow, narrow)
    )
    down_grad, basis_grad = scaled(small_grads, (narrow, wide), (basis_width, narrow))
    return (
        edge_grad[None],
        down_grad.T,
        basis_grad,
        bilinear_grad,
        up_grad,
        first_grad,
        second_grad,
    )


def solution(mesh):
    in_specs = (
        P("dp", "graph", None),
        P("dp", "graph", None),
        P("dp", "graph"),
        P("dp", None, "graph"),
        P("dp", "graph"),
        P("dp", "graph"),
        P(),
        P(),
        P(),
        P(),
        P(),
        P(),
    )
    out_specs = (P("dp", "graph", None), P(), P(), P(), P(), P(), P())
    return jax.shard_map(local, mesh=mesh, in_specs=in_specs, out_specs=out_specs, check_vma=False)
```

```python
import functools
import math

import jax
import jax.numpy as jnp
from jax import lax
from jax.experimental import pallas as pl
from jax.experimental.pallas import tpu as pltpu
from jax.sharding import PartitionSpec as P

HALF = 0.7071067811865476
F32 = jnp.float32
BF16 = jnp.bfloat16
MIB = 1024 * 1024


def contract(left, right, left_dim, right_dim):
    return lax.dot_general(
        left, right, (((left_dim,), (right_dim,)), ((), ())), preferred_element_type=F32
    )


def sigmoid(value):
    return 0.5 + 0.5 * jnp.tanh(0.5 * value)


def split_index(index_row, lanes):
    slots = index_row.shape[1]
    low = jnp.bitwise_and(index_row, lanes - 1)
    high = jnp.right_shift(index_row, lanes.bit_length() - 1)
    lane_ids = lax.broadcasted_iota(jnp.int32, (lanes, slots), 0)
    return high, jnp.where(lane_ids == low, 1.0, 0.0).astype(BF16)


def stack(rows, lanes):
    groups = rows.shape[1] // lanes
    return jnp.concatenate([rows[:, g * lanes : (g + 1) * lanes] for g in range(groups)], axis=0)


def unstack(rows, narrow):
    groups = rows.shape[0] // narrow
    return jnp.concatenate([rows[g * narrow : (g + 1) * narrow] for g in range(groups)], axis=1)


def pick_rows(stacked, high, lane_hot, narrow):
    groups = stacked.shape[0] // narrow
    every = contract(stacked, lane_hot, 1, 0)
    picked = jnp.where(high == 0, every[:narrow], 0.0)
    for g in range(1, groups):
        picked = jnp.where(high == g, every[g * narrow : (g + 1) * narrow], picked)
    return picked


def place_rows(values, high, lane_hot, groups):
    zero = jnp.zeros((), values.dtype)
    spread = jnp.concatenate([jnp.where(high == g, values, zero) for g in range(groups)], axis=0)
    return contract(spread.astype(BF16), lane_hot, 1, 1)


def down_kernel(edge_ref, weight_ref, rows_ref, slope_ref):
    lanes = rows_ref.shape[1]
    pre = contract(weight_ref[...], edge_ref[...], 1, 1)
    logistic = sigmoid(pre)
    rows_ref[...] = stack((pre * logistic).astype(BF16), lanes)
    slope_ref[...] = stack(logistic * (1.0 + pre * (1.0 - logistic)), lanes)


def forward_kernel(shard_ref, rows_ref, *refs):
    ends, basis, weight_ref = refs[:2], refs[2:4], refs[4]
    totals, fetched_ref = refs[-3:-1], refs[-1]
    shard = shard_ref[0]
    narrow = weight_ref.shape[1]
    groups = totals[0].shape[0] // narrow
    lanes = totals[0].shape[1]
    slots = ends[0].shape[3]
    at = pl.ds(pl.multiple_of(shard * slots, slots), slots)
    for i in range(2):
        high, lane_hot = split_index(ends[i][0, shard], lanes)
        fetched = pick_rows(rows_ref[...], high, lane_hot, narrow)
        fetched_ref[i] = fetched.astype(BF16)
        message = contract(weight_ref[...], basis[i][:, at], 0, 0) * fetched
        high, lane_hot = split_index(ends[i][1, shard], lanes)
        placed = place_rows(message, high, lane_hot, groups)
        if len(refs) == 10:
            placed += refs[5 + i][...]
        totals[i][...] = placed


def dense_kernel(
    count_ref,
    edge_ref,
    cotangent_ref,
    gathered_ref,
    more_ref,
    bilinear_ref,
    up_ref,
    first_ref,
    second_ref,
    summed_ref,
    back_ref,
    grads_ref,
    total,
):
    step = pl.program_id(0)
    tile, wide = edge_ref.shape
    narrow = bilinear_ref.shape[0]
    lanes = gathered_ref.shape[1]

    @pl.when(step == 0)
    def _():
        total[...] = jnp.zeros_like(total)

    gathered = unstack((gathered_ref[...] + more_ref[...]).astype(BF16), narrow)
    mixed = contract(bilinear_ref[...], gathered, 0, 0).astype(BF16)
    pre_up = contract(mixed, up_ref[...], 0, 0)
    up_logistic = sigmoid(pre_up)
    summed_half = (edge_ref[...].astype(F32) + pre_up * up_logistic).astype(BF16)
    pre_first = contract(summed_half, first_ref[...], 1, 0)
    first_logistic = sigmoid(pre_first)
    first_rows = (pre_first * first_logistic).astype(BF16)
    pre_second = contract(first_rows, second_ref[...], 1, 0)
    logistic = sigmoid(pre_second)
    row_ids = step * tile + lax.broadcasted_iota(jnp.int32, (tile, 1), 0)
    live = jnp.where(row_ids < count_ref[0, 0], HALF, 0.0)
    back_top = cotangent_ref[...].astype(F32) * live
    back_second = (back_top * (logistic * (1.0 + pre_second * (1.0 - logistic)))).astype(BF16)
    slope = first_logistic * (1.0 + pre_first * (1.0 - first_logistic))
    back_first = (contract(back_second, second_ref[...], 1, 1) * slope).astype(BF16)
    back_summed = back_top + contract(back_first, first_ref[...], 1, 1)
    summed_ref[...] = back_summed.astype(BF16)
    slope = up_logistic * (1.0 + pre_up * (1.0 - up_logistic))
    back_up = (back_summed * slope).astype(BF16)
    back_mixed = contract(up_ref[...], back_up, 1, 1).astype(BF16)
    back_ref[...] = stack(contract(bilinear_ref[...], back_mixed, 1, 0).astype(BF16), lanes)
    total[:wide] += contract(summed_half, back_first, 0, 0)
    total[wide : 2 * wide] += contract(first_rows, back_second, 0, 0)
    total[2 * wide : 2 * wide + narrow] += contract(mixed, back_up, 1, 0)
    total[2 * wide + narrow :, :narrow] += contract(gathered, back_mixed, 1, 1)

    @pl.when(step == pl.num_programs(0) - 1)
    def _():
        grads_ref[...] = total[...].astype(BF16)


def backward_kernel(shard_ref, own_ref, sibling_ref, fetched_ref, *refs):
    ends, basis, weight_ref = refs[:2], refs[2:4], refs[4]
    part_ref, grad_ref = refs[-2:]
    shard = shard_ref[0]
    narrow = weight_ref.shape[1]
    groups = part_ref.shape[0] // narrow
    lanes = part_ref.shape[1]
    slots = ends[0].shape[3]
    at = pl.ds(pl.multiple_of(shard * slots, slots), slots)
    grad = refs[5][...] if len(refs) == 8 else jnp.zeros(grad_ref.shape, F32)
    part = jnp.zeros(part_ref.shape, F32)
    for i, back_ref in enumerate((own_ref, sibling_ref)):
        block = basis[i][:, at]
        high, lane_hot = split_index(ends[i][1, shard], lanes)
        message = pick_rows(back_ref[...], high, lane_hot, narrow)
        back_coef = (message * fetched_ref[i].astype(F32)).astype(BF16)
        grad += contract(back_coef, block, 1, 1)
        message = message * contract(weight_ref[...], block, 0, 0)
        high, lane_hot = split_index(ends[i][0, shard], lanes)
        part += place_rows(message, high, lane_hot, groups)
    part_ref[...] = part.astype(BF16)
    grad_ref[...] = grad


def final_kernel(count, *refs):
    parts = refs[:count]
    slope_ref, edge_ref, summed_ref, weight_ref, basis_ref, edge_grad_ref, grads_ref, total = refs[
        count:
    ]
    step = pl.program_id(0)
    narrow = weight_ref.shape[0]
    basis_width = basis_ref.shape[1]

    @pl.when(step == 0)
    def _():
        total[...] = jnp.zeros_like(total)

    back_down = parts[0][...].astype(F32)
    for part in parts[1:]:
        back_down += part[...].astype(F32)
    back_pre = unstack((back_down * slope_ref[...]).astype(BF16), narrow)
    total[:narrow] += contract(back_pre, edge_ref[...], 1, 0)
    edge_grad_ref[...] = (
        summed_ref[...].astype(F32) + contract(back_pre, weight_ref[...], 0, 0)
    ).astype(BF16)

    @pl.when(step == pl.num_programs(0) - 1)
    def _():
        total[narrow : narrow + basis_width, :narrow] = basis_ref[...].T
        grads_ref[...] = total[...].astype(BF16)


def scale_kernel(scale, source_ref, *outs):
    row = 0
    for out in outs:
        rows, columns = out.shape
        out[...] = source_ref[row : row + rows, :columns].astype(F32) * scale
        row += rows


def call(kernel, grid, in_specs, out_specs, out_shape, flops, transcendentals=0, scratch=(), aliases=None, vmem=20):
    def run(*operands):
        size = sum(x.size * x.dtype.itemsize for x in operands)
        size += sum(x.size * x.dtype.itemsize for x in out_shape)
        return pl.pallas_call(
            kernel,
            grid=grid,
            in_specs=in_specs,
            out_specs=out_specs,
            out_shape=out_shape,
            scratch_shapes=scratch,
            input_output_aliases=aliases or {},
            compiler_params=pltpu.CompilerParams(vmem_limit_bytes=vmem * MIB),
            cost_estimate=pl.CostEstimate(
                flops=flops, bytes_accessed=size, transcendentals=transcendentals
            ),
        )(*operands)

    return run


def whole(*shape):
    return pl.BlockSpec(shape, lambda *_: (0,) * len(shape))


SMEM = pl.BlockSpec(memory_space=pltpu.SMEM)


def shape(dims, dtype):
    return jax.ShapeDtypeStruct(dims, dtype)


def turned(count, size, stride, turn):
    pairs = []
    for g in range(count):
        place = g // stride % size
        pairs.append((g, g + ((place + turn) % size - place) * stride))
    return pairs


class Line:
    cores = 2

    def __init__(self):
        self.size = lax.axis_size("graph")
        self.chips = math.gcd(self.size // self.cores, 4)
        self.span = self.chips * self.cores
        self.groups = self.size // self.span
        me = lax.axis_index("graph")
        self.core = me % self.cores
        self.chip = me // self.cores % self.chips
        self.group = me // self.span

    def send(self, array, moves):
        pairs = [
            (base + one * self.cores + core, base + other * self.cores + core)
            for base in range(0, self.size, self.span)
            for one, other in moves
            for core in range(self.cores)
        ]
        return lax.ppermute(array, "graph", pairs)

    def trade(self, array, bit):
        return self.send(array, [(chip, chip ^ bit) for chip in range(self.chips)])

    def swap(self, array):
        return lax.ppermute(array, "graph", [(g, g ^ 1) for g in range(self.size)])

    def next_group(self, array):
        return lax.ppermute(array, "graph", turned(self.size, self.groups, self.span, -1))

    def last_group(self, array):
        return lax.ppermute(array, "graph", turned(self.size, self.groups, self.span, 1))

    def shard(self, turn, bits):
        group = (self.group + turn) % self.groups
        shard = group * self.span + (self.chip ^ bits) * self.cores + self.core
        return shard.astype(jnp.int32).reshape(1)


def add(*arrays):
    return sum(a.astype(F32) for a in arrays).astype(BF16)


def after(arrays, *others):
    return lax.optimization_barrier((tuple(arrays), others))[0]


def piece_of(array, size, me):
    rows = array.shape[0] // size
    return lax.dynamic_slice_in_dim(array, me * rows, rows, 0)


def scatter_pieces(array, axis, size, me, stride):
    count = lax.axis_size(axis)
    arrived = [piece_of(array, size, me)]
    for turn in range(1, size):
        away = piece_of(array, size, (me + turn) % size)
        arrived.append(lax.ppermute(away, axis, turned(count, size, stride, turn)))
    return arrived


def gather_pieces(piece, axis, size, me, stride):
    count = lax.axis_size(axis)
    rows = piece.shape[0]
    out = jnp.zeros((size * rows, piece.shape[1]), piece.dtype)
    out = lax.dynamic_update_slice_in_dim(out, piece, me * rows, 0)
    for turn in range(1, size):
        other = lax.ppermute(piece, axis, turned(count, size, stride, turn))
        out = lax.dynamic_update_slice_in_dim(out, other, (me - turn) % size * rows, 0)
    return out


def stages_of(line, names):
    every = {
        "core": ("graph", line.cores, line.core, 1),
        "dp": ("dp", lax.axis_size("dp"), lax.axis_index("dp"), 1),
        "chip": ("graph", line.chips, line.chip, line.cores),
        "group": ("graph", line.groups, line.group, line.span),
    }
    return [every[name] for name in names]


def butterfly(array, stages):
    for axis, size, _, stride in stages:
        bit = 1
        while bit < size:
            pairs = [(g, g ^ (stride * bit)) for g in range(lax.axis_size(axis))]
            array = add(array, lax.ppermute(array, axis, pairs))
            bit *= 2
    return array


def halves_of(stage):
    axis, size, me, stride = stage
    return (axis, 2, me % 2, stride), (axis, size // 2, me // 2, 2 * stride)


def local(
    edge_state,
    cotangent,
    edge_count,
    triplet_basis,
    triplet_in,
    triplet_out,
    down_weight,
    basis_weight,
    bilinear_weight,
    up_weight,
    first_weight,
    second_weight,
):
    edge_rows = edge_state[0]
    row_count, wide = edge_rows.shape
    line = Line()
    shards, chips = line.size, line.chips
    narrow = down_weight.shape[1]
    down_weight = down_weight.T
    basis = triplet_basis[0]
    basis_width, tri_rows = basis.shape
    slots = tri_rows // shards
    lanes = math.gcd(row_count, 256)
    stacked = narrow * (row_count // lanes)
    tile = math.gcd(row_count, 512)
    tiles = row_count // tile
    row_spec = pl.BlockSpec((tile, wide), lambda i: (i, 0))
    stack_spec = pl.BlockSpec((narrow * (tile // lanes), lanes), lambda i: (i, 0))
    rows_spec = whole(stacked, lanes)

    ends = jnp.stack([triplet_in.reshape(shards, 1, slots), triplet_out.reshape(shards, 1, slots)])
    ends_sibling = line.swap(ends)
    basis_sibling = line.swap(basis)
    triplets = (ends, ends_sibling, basis, basis_sibling, basis_weight)
    triplet_specs = (
        [whole(2, shards, 1, slots)] * 2
        + [whole(basis_width, tri_rows)] * 2
        + [whole(basis_width, narrow)]
    )
    block_flops = 8 * slots * row_count * narrow

    down_rows, down_slope = call(
        down_kernel,
        (tiles,),
        [row_spec, whole(narrow, wide)],
        [stack_spec] * 2,
        [shape((stacked, lanes), BF16), shape((stacked, lanes), F32)],
        2 * row_count * wide * narrow,
        row_count * narrow,
    )(edge_rows, down_weight)

    def forward(shard, rows, totals):
        out = call(
            forward_kernel,
            (),
            [SMEM, rows_spec] + triplet_specs + [rows_spec] * len(totals),
            [rows_spec] * 2 + [whole(2, narrow, slots)],
            [shape((stacked, lanes), F32)] * 2 + [shape((2, narrow, slots), BF16)],
            block_flops,
            aliases={7 + i: i for i in range(len(totals))},
        )(shard, rows, *triplets, *totals)
        return tuple(out[:2]), out[2]

    def forward_line(turn, rows, totals):
        far = line.trade(rows, 2) if chips == 4 else None
        near = line.trade(rows, 1) if chips > 1 else None
        totals, got = forward(line.shard(turn, 0), rows, totals)
        fetched = [got]
        if chips > 1:
            totals, got = forward(line.shard(turn, 1), near, totals)
            fetched.append(got)
        if chips == 4:
            rows, far = after((rows, far), *totals)
            last = line.send(rows, [(1, 2), (2, 1)]) + line.send(far, [(2, 3), (1, 0)])
            totals, got = forward(line.shard(turn, 2), far, totals)
            fetched.append(got)
            totals, got = forward(line.shard(turn, 3), last, totals)
            fetched.append(got)
        return totals, fetched

    totals, fetched = forward_line(0, down_rows, ())
    if line.groups > 1:

        def forward_turn(carry, turn):
            rows, totals = carry
            rows = line.next_group(rows)
            totals, got = forward_line(turn, rows, totals)
            return (rows, totals), got

        (_, totals), more_fetched = lax.scan(
            forward_turn, (down_rows, totals), jnp.arange(1, line.groups)
        )

    grad_rows = 2 * wide + 2 * narrow
    back_summed, back_gathered, dense_grads = call(
        dense_kernel,
        (tiles,),
        [
            SMEM,
            row_spec,
            row_spec,
            stack_spec,
            stack_spec,
            whole(narrow, narrow),
            whole(narrow, wide),
            whole(wide, wide),
            whole(wide, wide),
        ],
        [row_spec, stack_spec, whole(grad_rows, wide)],
        [
            shape((row_count, wide), BF16),
            shape((stacked, lanes), BF16),
            shape((grad_rows, wide), BF16),
        ],
        12 * row_count * wide * wide + 6 * row_count * wide * narrow,
        3 * row_count * wide,
        scratch=[pltpu.VMEM((grad_rows, wide), F32)],
        vmem=32,
    )(
        edge_count,
        edge_rows,
        cotangent[0],
        totals[0],
        line.swap(totals[1]),
        bilinear_weight,
        up_weight,
        first_weight,
        second_weight,
    )
    back_sibling = line.swap(back_gathered)
    core, dp, chip, group = stages_of(line, ("core", "dp", "chip", "group"))
    dense_grads = add(*scatter_pieces(dense_grads, *core))

    def backward(shard, got, grad):
        extra = () if grad is None else (grad,)
        return call(
            backward_kernel,
            (),
            [SMEM, rows_spec, rows_spec, whole(2, narrow, slots)]
            + triplet_specs
            + [whole(narrow, basis_width)] * len(extra),
            [rows_spec, whole(narrow, basis_width)],
            [shape((stacked, lanes), BF16), shape((narrow, basis_width), F32)],
            block_flops,
        )(shard, back_gathered, back_sibling, got, *triplets, *extra)

    def backward_line(turn, fetched, basis_grad, summed=None):
        parts = []
        if chips == 4:
            last, basis_grad = backward(line.shard(turn, 3), fetched[3], basis_grad)
            passed = line.send(last, [(0, 1), (3, 2)])
            middle = line.send(last, [(1, 2), (2, 1)])
            if summed is not None:
                (basis_grad,) = after((basis_grad,), summed)
                arriving = scatter_pieces(summed, *dp)
            far, basis_grad = backward(line.shard(turn, 2), fetched[2], basis_grad)
        if chips > 1:
            near, basis_grad = backward(line.shard(turn, 1), fetched[1], basis_grad)
        if chips == 4:
            passed, middle = after((passed, middle), near)
            if summed is not None:
                summed = add(*after(arriving, near))
                (basis_grad,) = after((basis_grad,), summed)
            far = add(far, passed)
            near, basis_grad = after((near, basis_grad), far)
            parts += [middle, line.trade(far, 2)]
        if chips > 1:
            parts.append(line.trade(near, 1))
        own, basis_grad = backward(line.shard(turn, 0), fetched[0], basis_grad)
        return [own] + parts, basis_grad, summed

    back_parts, basis_grad, dense_grads = backward_line(0, fetched, None, dense_grads)
    if chips < 4:
        dense_grads = add(*scatter_pieces(dense_grads, *dp))
    first_bit, other_bits = halves_of(chip) if chips > 1 else (chip, chip)
    if chips > 1:
        dense_grads = add(*scatter_pieces(dense_grads, *first_bit))
        dense_grads = butterfly(dense_grads, [other_bits])
    dense_grads = butterfly(dense_grads, [group])
    if line.groups > 1:

        def backward_turn(carry, one):
            traveling, basis_grad = carry
            turn, got = one
            parts, basis_grad, _ = backward_line(turn, got, basis_grad)
            return (line.last_group(add(traveling, *parts)), basis_grad), None

        (traveling, basis_grad), _ = lax.scan(
            backward_turn,
            (jnp.zeros((stacked, lanes), BF16), basis_grad),
            (jnp.arange(1, line.groups), more_fetched),
            reverse=True,
        )
        back_parts = back_parts + [traveling]

    small_rows = narrow + basis_width
    edge_grad, small_grads = call(
        functools.partial(final_kernel, len(back_parts)),
        (tiles,),
        [stack_spec] * len(back_parts)
        + [stack_spec, row_spec, row_spec, whole(narrow, wide), whole(narrow, basis_width)],
        [row_spec, whole(small_rows, wide)],
        [shape((row_count, wide), BF16), shape((small_rows, wide), BF16)],
        4 * row_count * wide * narrow,
        scratch=[pltpu.VMEM((small_rows, wide), F32)],
    )(*back_parts, down_slope, edge_rows, back_summed, down_weight, basis_grad)

    small_grads = add(*scatter_pieces(small_grads, *core))
    small_grads = butterfly(small_grads, [chip, group, dp])
    small_grads = gather_pieces(small_grads, *core)
    if chips > 1:
        dense_grads = gather_pieces(dense_grads, *first_bit)
    dense_grads = gather_pieces(dense_grads, *dp)
    dense_grads = gather_pieces(dense_grads, *core)
    scale = 1.0 / math.sqrt(lax.axis_size("dp") * shards * row_count)

    def scaled(source, *dims):
        return call(
            functools.partial(scale_kernel, scale),
            (),
            [whole(*source.shape)],
            [whole(*d) for d in dims],
            [shape(d, F32) for d in dims],
            source.size,
        )(source)

    first_grad, second_grad, up_grad, bilinear_grad = scaled(
        dense_grads, (wide, wide), (wide, wide), (narrow, wide), (narrow, narrow)
    )
    down_grad, basis_grad = scaled(small_grads, (narrow, wide), (basis_width, narrow))
    return (
        edge_grad[None],
        down_grad.T,
        basis_grad,
        bilinear_grad,
        up_grad,
        first_grad,
        second_grad,
    )


def solution(mesh):
    in_specs = (
        P("dp", "graph", None),
        P("dp", "graph", None),
        P("dp", "graph"),
        P("dp", None, "graph"),
        P("dp", "graph"),
        P("dp", "graph"),
        P(),
        P(),
        P(),
        P(),
        P(),
        P(),
    )
    out_specs = (P("dp", "graph", None), P(), P(), P(), P(), P(), P())
    return jax.shard_map(local, mesh=mesh, in_specs=in_specs, out_specs=out_specs, check_vma=False)
```

```python
import functools
import math

import jax
import jax.numpy as jnp
from jax import lax
from jax.experimental import pallas as pl
from jax.experimental.pallas import tpu as pltpu
from jax.sharding import PartitionSpec as P

HALF = 0.7071067811865476
F32 = jnp.float32
BF16 = jnp.bfloat16
MIB = 1024 * 1024


def contract(left, right, left_dim, right_dim):
    return lax.dot_general(
        left, right, (((left_dim,), (right_dim,)), ((), ())), preferred_element_type=F32
    )


def sigmoid(value):
    return 0.5 + 0.5 * jnp.tanh(0.5 * value)


def split_index(index_row, lanes):
    slots = index_row.shape[1]
    low = jnp.bitwise_and(index_row, lanes - 1)
    high = jnp.right_shift(index_row, lanes.bit_length() - 1)
    lane_ids = lax.broadcasted_iota(jnp.int32, (lanes, slots), 0)
    return high, jnp.where(lane_ids == low, 1.0, 0.0).astype(BF16)


def stack(rows, lanes):
    groups = rows.shape[1] // lanes
    return jnp.concatenate([rows[:, g * lanes : (g + 1) * lanes] for g in range(groups)], axis=0)


def unstack(rows, narrow):
    groups = rows.shape[0] // narrow
    return jnp.concatenate([rows[g * narrow : (g + 1) * narrow] for g in range(groups)], axis=1)


def pick_rows(stacked, high, lane_hot, narrow):
    groups = stacked.shape[0] // narrow
    every = contract(stacked, lane_hot, 1, 0)
    picked = jnp.where(high == 0, every[:narrow], 0.0)
    for g in range(1, groups):
        picked = jnp.where(high == g, every[g * narrow : (g + 1) * narrow], picked)
    return picked


def place_rows(values, high, lane_hot, groups):
    zero = jnp.zeros((), values.dtype)
    spread = jnp.concatenate([jnp.where(high == g, values, zero) for g in range(groups)], axis=0)
    return contract(spread.astype(BF16), lane_hot, 1, 1)


def down_kernel(edge_ref, weight_ref, rows_ref, slope_ref):
    lanes = rows_ref.shape[1]
    pre = contract(weight_ref[...], edge_ref[...], 1, 1)
    logistic = sigmoid(pre)
    rows_ref[...] = stack((pre * logistic).astype(BF16), lanes)
    slope_ref[...] = stack(logistic * (1.0 + pre * (1.0 - logistic)), lanes)


def forward_kernel(pieces, shard_ref, *refs):
    rows = jnp.concatenate([ref[...] for ref in refs[:pieces]], axis=0)
    refs = refs[pieces:]
    ends, basis, weight_ref = refs[:2], refs[2:4], refs[4]
    totals, fetched_ref, coef_ref = refs[-4:-2], refs[-2], refs[-1]
    shard = shard_ref[0]
    narrow = weight_ref.shape[1]
    groups = totals[0].shape[0] // narrow
    lanes = totals[0].shape[1]
    slots = ends[0].shape[3]
    at = pl.ds(pl.multiple_of(shard * slots, slots), slots)
    for i in range(2):
        high, lane_hot = split_index(ends[i][0, shard], lanes)
        fetched = pick_rows(rows, high, lane_hot, narrow)
        fetched_ref[i] = fetched.astype(BF16)
        coef = contract(weight_ref[...], basis[i][:, at], 0, 0)
        coef_ref[i] = coef.astype(BF16)
        high, lane_hot = split_index(ends[i][1, shard], lanes)
        placed = place_rows(coef * fetched, high, lane_hot, groups)
        if len(refs) == 11:
            placed += refs[5 + i][...]
        totals[i][...] = placed


def dense_kernel(
    count_ref,
    edge_ref,
    cotangent_ref,
    gathered_ref,
    more_ref,
    bilinear_ref,
    up_ref,
    first_ref,
    second_ref,
    summed_ref,
    back_ref,
    grads_ref,
    total,
):
    step = pl.program_id(0)
    tile, wide = edge_ref.shape
    narrow = bilinear_ref.shape[0]
    lanes = gathered_ref.shape[1]

    @pl.when(step == 0)
    def _():
        total[...] = jnp.zeros_like(total)

    gathered = unstack((gathered_ref[...] + more_ref[...]).astype(BF16), narrow)
    mixed = contract(bilinear_ref[...], gathered, 0, 0).astype(BF16)
    pre_up = contract(mixed, up_ref[...], 0, 0)
    up_logistic = sigmoid(pre_up)
    summed_half = (edge_ref[...].astype(F32) + pre_up * up_logistic).astype(BF16)
    pre_first = contract(summed_half, first_ref[...], 1, 0)
    first_logistic = sigmoid(pre_first)
    first_rows = (pre_first * first_logistic).astype(BF16)
    pre_second = contract(first_rows, second_ref[...], 1, 0)
    logistic = sigmoid(pre_second)
    row_ids = step * tile + lax.broadcasted_iota(jnp.int32, (tile, 1), 0)
    live = jnp.where(row_ids < count_ref[0, 0], HALF, 0.0)
    back_top = cotangent_ref[...].astype(F32) * live
    back_second = (back_top * (logistic * (1.0 + pre_second * (1.0 - logistic)))).astype(BF16)
    slope = first_logistic * (1.0 + pre_first * (1.0 - first_logistic))
    back_first = (contract(back_second, second_ref[...], 1, 1) * slope).astype(BF16)
    back_summed = back_top + contract(back_first, first_ref[...], 1, 1)
    summed_ref[...] = back_summed.astype(BF16)
    slope = up_logistic * (1.0 + pre_up * (1.0 - up_logistic))
    back_up = (back_summed * slope).astype(BF16)
    back_mixed = contract(up_ref[...], back_up, 1, 1).astype(BF16)
    back_ref[...] = stack(contract(bilinear_ref[...], back_mixed, 1, 0).astype(BF16), lanes)
    total[:wide] += contract(summed_half, back_first, 0, 0)
    total[wide : 2 * wide] += contract(first_rows, back_second, 0, 0)
    total[2 * wide : 2 * wide + narrow] += contract(mixed, back_up, 1, 0)
    total[2 * wide + narrow :, :narrow] += contract(gathered, back_mixed, 1, 1)

    @pl.when(step == pl.num_programs(0) - 1)
    def _():
        grads_ref[...] = total[...].astype(BF16)


def backward_kernel(shard_ref, own_ref, sibling_ref, fetched_ref, coef_ref, *refs):
    ends, part_ref, back_coef_ref = refs[:2], refs[2], refs[3]
    shard = shard_ref[0]
    narrow = fetched_ref.shape[1]
    groups = part_ref.shape[0] // narrow
    lanes = part_ref.shape[1]
    part = None
    for i, back_ref in enumerate((own_ref, sibling_ref)):
        high, lane_hot = split_index(ends[i][1, shard], lanes)
        message = pick_rows(back_ref[...], high, lane_hot, narrow)
        back_coef_ref[i] = (message * fetched_ref[i].astype(F32)).astype(BF16)
        high, lane_hot = split_index(ends[i][0, shard], lanes)
        placed = place_rows(message * coef_ref[i].astype(F32), high, lane_hot, groups)
        part = placed if part is None else part + placed
    part_ref[...] = part.astype(BF16)


def basis_kernel(shards_ref, *refs):
    back_coefs, basis, grad_ref = refs[:-3], refs[-3:-1], refs[-1]
    slots = back_coefs[0].shape[2]
    grad = jnp.zeros(grad_ref.shape, F32)
    for s, ref in enumerate(back_coefs):
        at = pl.ds(pl.multiple_of(shards_ref[s] * slots, slots), slots)
        for i in range(2):
            grad += contract(ref[i], basis[i][:, at], 1, 1)
    grad_ref[...] = grad


def final_kernel(count, *refs):
    parts = refs[:count]
    slope_ref, edge_ref, summed_ref, weight_ref, basis_ref, edge_grad_ref, grads_ref, total = refs[
        count:
    ]
    step = pl.program_id(0)
    narrow = weight_ref.shape[0]
    basis_width = basis_ref.shape[1]

    @pl.when(step == 0)
    def _():
        total[...] = jnp.zeros_like(total)

    back_down = parts[0][...].astype(F32)
    for part in parts[1:]:
        back_down += part[...].astype(F32)
    back_pre = unstack((back_down * slope_ref[...]).astype(BF16), narrow)
    total[:narrow] += contract(back_pre, edge_ref[...], 1, 0)
    edge_grad_ref[...] = (
        summed_ref[...].astype(F32) + contract(back_pre, weight_ref[...], 0, 0)
    ).astype(BF16)

    @pl.when(step == pl.num_programs(0) - 1)
    def _():
        total[narrow : narrow + basis_width, :narrow] = basis_ref[...].T
        grads_ref[...] = total[...].astype(BF16)


def scale_kernel(scale, source_ref, *outs):
    row = 0
    for out in outs:
        rows, columns = out.shape
        out[...] = source_ref[row : row + rows, :columns].astype(F32) * scale
        row += rows


def call(kernel, grid, in_specs, out_specs, out_shape, flops, transcendentals=0, scratch=(), aliases=None, **params):
    def run(*operands):
        size = sum(x.size * x.dtype.itemsize for x in operands)
        size += sum(math.prod(x.shape) * x.dtype.itemsize for x in out_shape)
        return pl.pallas_call(
            kernel,
            grid=grid,
            in_specs=in_specs,
            out_specs=out_specs,
            out_shape=out_shape,
            scratch_shapes=scratch,
            input_output_aliases=aliases or {},
            compiler_params=pltpu.CompilerParams(**{"vmem_limit_bytes": 20 * MIB, **params}),
            cost_estimate=pl.CostEstimate(
                flops=flops, bytes_accessed=size, transcendentals=transcendentals
            ),
        )(*operands)

    return run


def whole(*shape):
    return pl.BlockSpec(shape, lambda *_: (0,) * len(shape))


SMEM = pl.BlockSpec(memory_space=pltpu.SMEM)


def in_hbm(array):
    return pltpu.with_memory_space_constraint(array, pltpu.HBM)


def shape(dims, dtype):
    return jax.ShapeDtypeStruct(dims, dtype)


def turned(count, size, stride, turn):
    pairs = []
    for g in range(count):
        place = g // stride % size
        pairs.append((g, g + ((place + turn) % size - place) * stride))
    return pairs


class Line:
    cores = 2

    def __init__(self):
        self.size = lax.axis_size("graph")
        self.chips = math.gcd(self.size // self.cores, 4)
        self.span = self.chips * self.cores
        self.groups = self.size // self.span
        me = lax.axis_index("graph")
        self.core = me % self.cores
        self.chip = me // self.cores % self.chips
        self.group = me // self.span

    def send(self, array, moves):
        pairs = [
            (base + one * self.cores + core, base + other * self.cores + core)
            for base in range(0, self.size, self.span)
            for one, other in moves
            for core in range(self.cores)
        ]
        return lax.ppermute(array, "graph", pairs)

    def trade(self, array, bit):
        return self.send(array, [(chip, chip ^ bit) for chip in range(self.chips)])

    def swap(self, array):
        return lax.ppermute(array, "graph", [(g, g ^ 1) for g in range(self.size)])

    def next_group(self, array):
        return lax.ppermute(array, "graph", turned(self.size, self.groups, self.span, -1))

    def last_group(self, array):
        return lax.ppermute(array, "graph", turned(self.size, self.groups, self.span, 1))

    def shard(self, turn, bits):
        group = (self.group + turn) % self.groups
        shard = group * self.span + (self.chip ^ bits) * self.cores + self.core
        return shard.astype(jnp.int32).reshape(1)


def add(*arrays):
    return sum(a.astype(F32) for a in arrays).astype(BF16)


def after(arrays, *others):
    return lax.optimization_barrier((tuple(arrays), others))[0]


def piece_of(array, size, me):
    rows = array.shape[0] // size
    return lax.dynamic_slice_in_dim(array, me * rows, rows, 0)


def scatter_pieces(array, axis, size, me, stride):
    count = lax.axis_size(axis)
    arrived = [piece_of(array, size, me)]
    for turn in range(1, size):
        away = piece_of(array, size, (me + turn) % size)
        arrived.append(lax.ppermute(away, axis, turned(count, size, stride, turn)))
    return arrived


def gather_pieces(piece, axis, size, me, stride):
    count = lax.axis_size(axis)
    rows = piece.shape[0]
    out = jnp.zeros((size * rows, piece.shape[1]), piece.dtype)
    out = lax.dynamic_update_slice_in_dim(out, piece, me * rows, 0)
    for turn in range(1, size):
        other = lax.ppermute(piece, axis, turned(count, size, stride, turn))
        out = lax.dynamic_update_slice_in_dim(out, other, (me - turn) % size * rows, 0)
    return out


def stages_of(line, names):
    every = {
        "core": ("graph", line.cores, line.core, 1),
        "dp": ("dp", lax.axis_size("dp"), lax.axis_index("dp"), 1),
        "chip": ("graph", line.chips, line.chip, line.cores),
        "group": ("graph", line.groups, line.group, line.span),
    }
    return [every[name] for name in names]


def butterfly(array, stages):
    for axis, size, _, stride in stages:
        bit = 1
        while bit < size:
            pairs = [(g, g ^ (stride * bit)) for g in range(lax.axis_size(axis))]
            array = add(array, lax.ppermute(array, axis, pairs))
            bit *= 2
    return array


def halves_of(stage):
    axis, size, me, stride = stage
    return (axis, 2, me % 2, stride), (axis, size // 2, me // 2, 2 * stride)


def local(
    edge_state,
    cotangent,
    edge_count,
    triplet_basis,
    triplet_in,
    triplet_out,
    down_weight,
    basis_weight,
    bilinear_weight,
    up_weight,
    first_weight,
    second_weight,
):
    edge_rows = edge_state[0]
    row_count, wide = edge_rows.shape
    line = Line()
    shards, chips = line.size, line.chips
    narrow = down_weight.shape[1]
    down_weight = down_weight.T
    basis = triplet_basis[0]
    basis_width, tri_rows = basis.shape
    slots = tri_rows // shards
    lanes = math.gcd(row_count, 256)
    stacked = narrow * (row_count // lanes)
    tile = math.gcd(row_count, 512)
    tiles = row_count // tile
    row_spec = pl.BlockSpec((tile, wide), lambda i: (i, 0))
    stack_spec = pl.BlockSpec((narrow * (tile // lanes), lanes), lambda i: (i, 0))
    rows_spec = whole(stacked, lanes)

    ends = jnp.stack([triplet_in.reshape(shards, 1, slots), triplet_out.reshape(shards, 1, slots)])
    ends_sibling = line.swap(ends)
    basis_sibling = line.swap(basis)
    triplets = (ends, ends_sibling, basis, basis_sibling, basis_weight)
    triplet_specs = (
        [whole(2, shards, 1, slots)] * 2
        + [whole(basis_width, tri_rows)] * 2
        + [whole(basis_width, narrow)]
    )
    block_flops = 8 * slots * row_count * narrow

    down_rows, down_slope = call(
        down_kernel,
        (tiles,),
        [row_spec, whole(narrow, wide)],
        [stack_spec] * 2,
        [shape((stacked, lanes), BF16), shape((stacked, lanes), F32)],
        2 * row_count * wide * narrow,
        row_count * narrow,
    )(in_hbm(edge_rows), down_weight)

    slot_spec = whole(2, narrow, slots)
    slot_shape = shape((2, narrow, slots), BF16)

    def forward(shard, rows, totals):
        first = len(rows) + 6
        out = call(
            functools.partial(forward_kernel, len(rows)),
            (),
            [SMEM]
            + [whole(*piece.shape) for piece in rows]
            + triplet_specs
            + [rows_spec] * len(totals),
            [rows_spec] * 2 + [slot_spec] * 2,
            [shape((stacked, lanes), F32)] * 2 + [slot_shape] * 2,
            block_flops,
            aliases={first + i: i for i in range(len(totals))},
        )(shard, *rows, *triplets, *totals)
        return tuple(out[:2]), tuple(out[2:])

    def forward_line(turn, rows, totals):
        halves = (rows[: stacked // 2], rows[stacked // 2 :])
        far = [line.trade(half, 2) for half in halves] if chips == 4 else None
        near = line.trade(rows, 1) if chips > 1 else None
        totals, got = forward(line.shard(turn, 0), [rows], totals)
        kept = [got]
        last = []

        def pass_on(half, *others):
            mine, far[half] = after((halves[half], far[half]), *others)
            middle = line.send(mine, [(1, 2), (2, 1)])
            last.append(middle + line.send(far[half], [(2, 3), (1, 0)]))

        if chips == 4:
            pass_on(0, *totals)
        if chips > 1:
            totals, got = forward(line.shard(turn, 1), [near], totals)
            kept.append(got)
        if chips == 4:
            pass_on(1, *totals)
            totals, got = forward(line.shard(turn, 2), far, totals)
            kept.append(got)
            totals, got = forward(line.shard(turn, 3), last, totals)
            kept.append(got)
        return totals, kept

    totals, kept = forward_line(0, down_rows, ())
    if line.groups > 1:

        def forward_turn(carry, turn):
            rows, totals = carry
            rows = line.next_group(rows)
            totals, got = forward_line(turn, rows, totals)
            return (rows, totals), got

        (_, totals), more_kept = lax.scan(
            forward_turn, (down_rows, totals), jnp.arange(1, line.groups)
        )

    grad_rows = 2 * wide + 2 * narrow
    back_summed, back_gathered, dense_grads = call(
        dense_kernel,
        (tiles,),
        [
            SMEM,
            row_spec,
            row_spec,
            stack_spec,
            stack_spec,
            whole(narrow, narrow),
            whole(narrow, wide),
            whole(wide, wide),
            whole(wide, wide),
        ],
        [row_spec, stack_spec, whole(grad_rows, wide)],
        [
            pltpu.HBM((row_count, wide), BF16),
            shape((stacked, lanes), BF16),
            shape((grad_rows, wide), BF16),
        ],
        12 * row_count * wide * wide + 6 * row_count * wide * narrow,
        3 * row_count * wide,
        scratch=[pltpu.VMEM((grad_rows, wide), F32)],
        vmem_limit_bytes=32 * MIB,
        fuse_transposed_lhs_in_matmul=True,
    )(
        edge_count,
        in_hbm(edge_rows),
        in_hbm(cotangent[0]),
        totals[0],
        line.swap(totals[1]),
        bilinear_weight,
        up_weight,
        in_hbm(first_weight),
        in_hbm(second_weight),
    )
    back_sibling = line.swap(back_gathered)
    core, dp, chip, group = stages_of(line, ("core", "dp", "chip", "group"))
    dense_grads = add(*scatter_pieces(dense_grads, *core))

    def backward(shard, got, others=()):
        back, *got = after((back_gathered, *got), *others)
        return call(
            backward_kernel,
            (),
            [SMEM, rows_spec, rows_spec, slot_spec, slot_spec] + triplet_specs[:2],
            [rows_spec, slot_spec],
            [shape((stacked, lanes), BF16), slot_shape],
            block_flops,
        )(shard, back, back_sibling, *got, ends, ends_sibling)

    def backward_line(turn, kept, summed=None):
        parts = []
        back_coefs = [None] * chips
        others = ()
        if chips == 4:
            last, back_coefs[3] = backward(line.shard(turn, 3), kept[3])
            passed = line.send(last, [(0, 1), (3, 2)])
            middle = line.send(last, [(1, 2), (2, 1)])
            others = (last,)
            if summed is not None:
                others = (last, summed)
                arriving = scatter_pieces(summed, *dp)
            far, back_coefs[2] = backward(line.shard(turn, 2), kept[2], others)
            others = (far,)
        if chips > 1:
            near, back_coefs[1] = backward(line.shard(turn, 1), kept[1], others)
            others = (near,)
        if chips == 4:
            passed, middle = after((passed, middle), near)
            if summed is not None:
                summed = add(*after(arriving, near))
                (far,) = after((far,), summed)
            far = add(far, passed)
            (near,) = after((near,), far)
            others = (far,)
            parts += [middle, line.trade(far, 2)]
        if chips > 1:
            parts.append(line.trade(near, 1))
        own, back_coefs[0] = backward(line.shard(turn, 0), kept[0], others)
        basis_grad = call(
            basis_kernel,
            (),
            [SMEM] + [slot_spec] * chips + triplet_specs[2:4],
            [whole(narrow, basis_width)],
            [shape((narrow, basis_width), F32)],
            4 * chips * slots * narrow * basis_width,
        )(
            jnp.concatenate([line.shard(turn, bits) for bits in range(chips)]),
            *back_coefs,
            basis,
            basis_sibling,
        )[0]
        return [own] + parts, basis_grad, summed

    back_parts, basis_grad, dense_grads = backward_line(0, kept, dense_grads)
    if chips < 4:
        dense_grads = add(*scatter_pieces(dense_grads, *dp))
    first_bit, other_bits = halves_of(chip) if chips > 1 else (chip, chip)
    if chips > 1:
        dense_grads = add(*scatter_pieces(dense_grads, *first_bit))
        dense_grads = butterfly(dense_grads, [other_bits])
    dense_grads = butterfly(dense_grads, [group])
    if line.groups > 1:

        def backward_turn(carry, one):
            traveling, basis_grad = carry
            turn, got = one
            parts, more, _ = backward_line(turn, got)
            return (line.last_group(add(traveling, *parts)), basis_grad + more), None

        (traveling, basis_grad), _ = lax.scan(
            backward_turn,
            (jnp.zeros((stacked, lanes), BF16), basis_grad),
            (jnp.arange(1, line.groups), more_kept),
            reverse=True,
        )
        back_parts = back_parts + [traveling]

    small_rows = narrow + basis_width
    edge_grad, small_grads = call(
        functools.partial(final_kernel, len(back_parts)),
        (tiles,),
        [stack_spec] * len(back_parts)
        + [stack_spec, row_spec, row_spec, whole(narrow, wide), whole(narrow, basis_width)],
        [row_spec, whole(small_rows, wide)],
        [shape((row_count, wide), BF16), shape((small_rows, wide), BF16)],
        4 * row_count * wide * narrow,
        scratch=[pltpu.VMEM((small_rows, wide), F32)],
    )(
        *back_parts,
        down_slope,
        in_hbm(edge_rows),
        in_hbm(back_summed),
        down_weight,
        basis_grad,
    )

    small_grads = add(*scatter_pieces(small_grads, *core))
    small_grads = butterfly(small_grads, [chip, group, dp])
    small_grads = gather_pieces(small_grads, *core)
    if chips > 1:
        dense_grads = gather_pieces(dense_grads, *first_bit)
    dense_grads = gather_pieces(dense_grads, *dp)
    dense_grads = gather_pieces(dense_grads, *core)
    scale = 1.0 / math.sqrt(lax.axis_size("dp") * shards * row_count)

    def scaled(source, *dims):
        return call(
            functools.partial(scale_kernel, scale),
            (),
            [whole(*source.shape)],
            [whole(*d) for d in dims],
            [shape(d, F32) for d in dims],
            source.size,
        )(source)

    first_grad, second_grad, up_grad, bilinear_grad = scaled(
        dense_grads, (wide, wide), (wide, wide), (narrow, wide), (narrow, narrow)
    )
    down_grad, basis_grad = scaled(small_grads, (narrow, wide), (basis_width, narrow))
    return (
        edge_grad[None],
        down_grad.T,
        basis_grad,
        bilinear_grad,
        up_grad,
        first_grad,
        second_grad,
    )


def solution(mesh):
    in_specs = (
        P("dp", "graph", None),
        P("dp", "graph", None),
        P("dp", "graph"),
        P("dp", None, "graph"),
        P("dp", "graph"),
        P("dp", "graph"),
        P(),
        P(),
        P(),
        P(),
        P(),
        P(),
    )
    out_specs = (P("dp", "graph", None), P(), P(), P(), P(), P(), P())
    return jax.shard_map(local, mesh=mesh, in_specs=in_specs, out_specs=out_specs, check_vma=False)
```

```python
import functools
import math

import jax
import jax.numpy as jnp
from jax import lax
from jax.experimental import pallas as pl
from jax.experimental.pallas import tpu as pltpu
from jax.sharding import PartitionSpec as P

HALF = 0.7071067811865476
F32 = jnp.float32
BF16 = jnp.bfloat16
MIB = 1024 * 1024


def contract(left, right, left_dim, right_dim):
    return lax.dot_general(
        left, right, (((left_dim,), (right_dim,)), ((), ())), preferred_element_type=F32
    )


def sigmoid(value):
    return 0.5 + 0.5 * jnp.tanh(0.5 * value)


def split_index(index_row, lanes):
    slots = index_row.shape[1]
    low = jnp.bitwise_and(index_row, lanes - 1)
    high = jnp.right_shift(index_row, lanes.bit_length() - 1)
    lane_ids = lax.broadcasted_iota(jnp.int32, (lanes, slots), 0)
    return high, jnp.where(lane_ids == low, 1.0, 0.0).astype(BF16)


def stack(rows, lanes):
    groups = rows.shape[1] // lanes
    return jnp.concatenate([rows[:, g * lanes : (g + 1) * lanes] for g in range(groups)], axis=0)


def unstack(rows, narrow):
    groups = rows.shape[0] // narrow
    return jnp.concatenate([rows[g * narrow : (g + 1) * narrow] for g in range(groups)], axis=1)


def pick_rows(stacked, high, lane_hot, narrow):
    groups = stacked.shape[0] // narrow
    every = contract(stacked, lane_hot, 1, 0)
    picked = jnp.where(high == 0, every[:narrow], 0.0)
    for g in range(1, groups):
        picked = jnp.where(high == g, every[g * narrow : (g + 1) * narrow], picked)
    return picked


def place_rows(values, high, lane_hot, groups):
    zero = jnp.zeros((), values.dtype)
    spread = jnp.concatenate([jnp.where(high == g, values, zero) for g in range(groups)], axis=0)
    return contract(spread.astype(BF16), lane_hot, 1, 1)


def down_kernel(edge_ref, weight_ref, rows_ref, slope_ref):
    lanes = rows_ref.shape[1]
    pre = contract(edge_ref[...], weight_ref[...], 1, 1).T
    logistic = sigmoid(pre)
    rows_ref[...] = stack((pre * logistic).astype(BF16), lanes)
    slope_ref[...] = stack(logistic * (1.0 + pre * (1.0 - logistic)), lanes)


def forward_kernel(shard_ref, rows_ref, *refs):
    rows = rows_ref[...]
    ends, basis, weight_ref = refs[:2], refs[2:4], refs[4]
    totals, fetched_ref, coef_ref = refs[-4:-2], refs[-2], refs[-1]
    shard = shard_ref[0]
    narrow = weight_ref.shape[1]
    groups = totals[0].shape[0] // narrow
    lanes = totals[0].shape[1]
    slots = ends[0].shape[3]
    at = pl.ds(pl.multiple_of(shard * slots, slots), slots)
    for i in range(2):
        high, lane_hot = split_index(ends[i][0, shard], lanes)
        fetched = pick_rows(rows, high, lane_hot, narrow)
        fetched_ref[i] = fetched.astype(BF16)
        coef = contract(weight_ref[...], basis[i][:, at], 0, 0)
        coef_ref[i] = coef.astype(BF16)
        high, lane_hot = split_index(ends[i][1, shard], lanes)
        placed = place_rows(coef * fetched, high, lane_hot, groups)
        if len(refs) == 11:
            placed += refs[5 + i][...]
        totals[i][...] = placed


def dense_kernel(
    count_ref,
    edge_ref,
    cotangent_ref,
    gathered_ref,
    more_ref,
    bilinear_ref,
    up_ref,
    first_ref,
    first_turned_ref,
    second_ref,
    second_turned_ref,
    summed_ref,
    back_ref,
    grads_ref,
    total,
):
    step = pl.program_id(0)
    tile, wide = edge_ref.shape
    narrow = bilinear_ref.shape[0]
    lanes = gathered_ref.shape[1]

    @pl.when(step == 0)
    def _():
        total[...] = jnp.zeros_like(total)

    gathered = unstack((gathered_ref[...] + more_ref[...]).astype(BF16), narrow)
    mixed = contract(bilinear_ref[...], gathered, 0, 0).astype(BF16)
    pre_up = contract(mixed, up_ref[...], 0, 0)
    up_logistic = sigmoid(pre_up)
    summed_half = (edge_ref[...].astype(F32) + pre_up * up_logistic).astype(BF16)
    pre_first = contract(summed_half, first_ref[...], 1, 0)
    first_logistic = sigmoid(pre_first)
    first_rows = (pre_first * first_logistic).astype(BF16)
    pre_second = contract(first_rows, second_ref[...], 1, 0)
    logistic = sigmoid(pre_second)
    row_ids = step * tile + lax.broadcasted_iota(jnp.int32, (tile, 1), 0)
    live = jnp.where(row_ids < count_ref[0, 0], HALF, 0.0)
    back_top = cotangent_ref[...].astype(F32) * live
    back_second = (back_top * (logistic * (1.0 + pre_second * (1.0 - logistic)))).astype(BF16)
    slope = first_logistic * (1.0 + pre_first * (1.0 - first_logistic))
    back_first = (contract(back_second, second_turned_ref[...], 1, 0) * slope).astype(BF16)
    back_summed = back_top + contract(back_first, first_turned_ref[...], 1, 0)
    summed_ref[...] = back_summed.astype(BF16)
    slope = up_logistic * (1.0 + pre_up * (1.0 - up_logistic))
    back_up = (back_summed * slope).astype(BF16)
    back_mixed = contract(back_up, up_ref[...], 1, 1).T.astype(BF16)
    back_ref[...] = stack(contract(bilinear_ref[...], back_mixed, 1, 0).astype(BF16), lanes)
    total[:wide] += contract(summed_half, back_first, 0, 0)
    total[wide : 2 * wide] += contract(first_rows, back_second, 0, 0)
    total[2 * wide : 2 * wide + narrow] += contract(mixed, back_up, 1, 0)
    total[2 * wide + narrow :, :narrow] += contract(gathered, back_mixed, 1, 1)

    @pl.when(step == pl.num_programs(0) - 1)
    def _():
        grads_ref[...] = total[...].astype(BF16)


def backward_kernel(shard_ref, own_ref, sibling_ref, fetched_ref, coef_ref, *refs):
    ends, part_ref, back_coef_ref = refs[:2], refs[2], refs[3]
    shard = shard_ref[0]
    narrow = fetched_ref.shape[1]
    groups = part_ref.shape[0] // narrow
    lanes = part_ref.shape[1]
    part = None
    for i, back_ref in enumerate((own_ref, sibling_ref)):
        high, lane_hot = split_index(ends[i][1, shard], lanes)
        message = pick_rows(back_ref[...], high, lane_hot, narrow)
        back_coef_ref[i] = (message * fetched_ref[i].astype(F32)).astype(BF16)
        high, lane_hot = split_index(ends[i][0, shard], lanes)
        placed = place_rows(message * coef_ref[i].astype(F32), high, lane_hot, groups)
        part = placed if part is None else part + placed
    part_ref[...] = part.astype(BF16)


def basis_kernel(shards_ref, *refs):
    back_coefs, basis, grad_ref = refs[:-3], refs[-3:-1], refs[-1]
    slots = back_coefs[0].shape[2]
    grad = jnp.zeros(grad_ref.shape, F32)
    for s, ref in enumerate(back_coefs):
        at = pl.ds(pl.multiple_of(shards_ref[s] * slots, slots), slots)
        for i in range(2):
            grad += contract(ref[i], basis[i][:, at], 1, 1)
    grad_ref[...] = grad


def final_kernel(count, *refs):
    parts = refs[:count]
    slope_ref, edge_ref, summed_ref, weight_ref, basis_ref, edge_grad_ref, grads_ref, total = refs[
        count:
    ]
    step = pl.program_id(0)
    narrow = weight_ref.shape[0]
    basis_width = basis_ref.shape[1]

    @pl.when(step == 0)
    def _():
        total[...] = jnp.zeros_like(total)

    back_down = parts[0][...].astype(F32)
    for part in parts[1:]:
        back_down += part[...].astype(F32)
    back_pre = unstack((back_down * slope_ref[...]).astype(BF16), narrow)
    total[:narrow] += contract(back_pre, edge_ref[...], 1, 0)
    edge_grad_ref[...] = (
        summed_ref[...].astype(F32) + contract(back_pre, weight_ref[...], 0, 0)
    ).astype(BF16)

    @pl.when(step == pl.num_programs(0) - 1)
    def _():
        total[narrow : narrow + basis_width, :narrow] = basis_ref[...].T
        grads_ref[...] = total[...].astype(BF16)


def scale_kernel(scale, source_ref, *outs):
    row = 0
    for out in outs:
        rows, columns = out.shape
        out[...] = source_ref[row : row + rows, :columns].astype(F32) * scale
        row += rows


def call(kernel, grid, in_specs, out_specs, out_shape, flops, transcendentals=0, scratch=(), aliases=None, **params):
    def run(*operands):
        size = sum(x.size * x.dtype.itemsize for x in operands)
        size += sum(math.prod(x.shape) * x.dtype.itemsize for x in out_shape)
        return pl.pallas_call(
            kernel,
            grid=grid,
            in_specs=in_specs,
            out_specs=out_specs,
            out_shape=out_shape,
            scratch_shapes=scratch,
            input_output_aliases=aliases or {},
            compiler_params=pltpu.CompilerParams(**{"vmem_limit_bytes": 20 * MIB, **params}),
            cost_estimate=pl.CostEstimate(
                flops=flops, bytes_accessed=size, transcendentals=transcendentals
            ),
        )(*operands)

    return run


def whole(*shape):
    return pl.BlockSpec(shape, lambda *_: (0,) * len(shape))


SMEM = pl.BlockSpec(memory_space=pltpu.SMEM)


def in_hbm(array):
    return pltpu.with_memory_space_constraint(array, pltpu.HBM)


def shape(dims, dtype):
    return jax.ShapeDtypeStruct(dims, dtype)


def turned(count, size, stride, turn):
    pairs = []
    for g in range(count):
        place = g // stride % size
        pairs.append((g, g + ((place + turn) % size - place) * stride))
    return pairs


class Line:
    cores = 2

    def __init__(self):
        self.size = lax.axis_size("graph")
        self.chips = math.gcd(self.size // self.cores, 4)
        self.span = self.chips * self.cores
        self.groups = self.size // self.span
        me = lax.axis_index("graph")
        self.core = me % self.cores
        self.chip = me // self.cores % self.chips
        self.group = me // self.span

    def send(self, array, moves):
        pairs = [
            (base + one * self.cores + core, base + other * self.cores + core)
            for base in range(0, self.size, self.span)
            for one, other in moves
            for core in range(self.cores)
        ]
        return lax.ppermute(array, "graph", pairs)

    def trade(self, array, bit):
        return self.send(array, [(chip, chip ^ bit) for chip in range(self.chips)])

    def swap(self, array):
        return lax.ppermute(array, "graph", [(g, g ^ 1) for g in range(self.size)])

    def next_group(self, array):
        return lax.ppermute(array, "graph", turned(self.size, self.groups, self.span, -1))

    def last_group(self, array):
        return lax.ppermute(array, "graph", turned(self.size, self.groups, self.span, 1))

    def shard(self, turn, bits):
        group = (self.group + turn) % self.groups
        shard = group * self.span + (self.chip ^ bits) * self.cores + self.core
        return shard.astype(jnp.int32).reshape(1)


def add(*arrays):
    return sum(a.astype(F32) for a in arrays).astype(BF16)


def after(arrays, *others):
    return lax.optimization_barrier((tuple(arrays), others))[0]


def piece_of(array, size, me):
    rows = array.shape[0] // size
    return lax.dynamic_slice_in_dim(array, me * rows, rows, 0)


def scatter_pieces(array, axis, size, me, stride):
    count = lax.axis_size(axis)
    arrived = [piece_of(array, size, me)]
    for turn in range(1, size):
        away = piece_of(array, size, (me + turn) % size)
        arrived.append(lax.ppermute(away, axis, turned(count, size, stride, turn)))
    return arrived


def gather_pieces(piece, axis, size, me, stride):
    count = lax.axis_size(axis)
    rows = piece.shape[0]
    out = jnp.zeros((size * rows, piece.shape[1]), piece.dtype)
    out = lax.dynamic_update_slice_in_dim(out, piece, me * rows, 0)
    for turn in range(1, size):
        other = lax.ppermute(piece, axis, turned(count, size, stride, turn))
        out = lax.dynamic_update_slice_in_dim(out, other, (me - turn) % size * rows, 0)
    return out


def dp_pairs(line, step):
    bits = lax.axis_size("dp").bit_length() - 1
    pairs = []
    for dp in range(lax.axis_size("dp")):
        for g in range(line.size):
            bit = (step + g % line.cores) % bits
            pairs.append((dp * line.size + g, (dp ^ (1 << bit)) * line.size + g))
    return pairs


def dp_place(line, step):
    bits = lax.axis_size("dp").bit_length() - 1
    return lax.axis_index("dp") >> ((step + line.core) % bits) & 1


def across_dp(array, line, step):
    place = dp_place(line, step)
    away = lax.ppermute(piece_of(array, 2, 1 - place), ("dp", "graph"), dp_pairs(line, step))
    return [piece_of(array, 2, place), away]


def joined_dp(piece, line, step):
    other = lax.ppermute(piece, ("dp", "graph"), dp_pairs(line, step))
    first = dp_place(line, step) == 0
    return jnp.where(
        first, jnp.concatenate([piece, other]), jnp.concatenate([other, piece])
    )


def summed_dp(array, line):
    for step in range(lax.axis_size("dp").bit_length() - 1):
        other = lax.ppermute(array, ("dp", "graph"), dp_pairs(line, step))
        array = add(array, other)
    return array


def stages_of(line, names):
    every = {
        "core": ("graph", line.cores, line.core, 1),
        "chip": ("graph", line.chips, line.chip, line.cores),
        "group": ("graph", line.groups, line.group, line.span),
    }
    return [every[name] for name in names]


def butterfly(array, stages):
    for axis, size, _, stride in stages:
        bit = 1
        while bit < size:
            pairs = [(g, g ^ (stride * bit)) for g in range(lax.axis_size(axis))]
            array = add(array, lax.ppermute(array, axis, pairs))
            bit *= 2
    return array


def halves_of(stage):
    axis, size, me, stride = stage
    return (axis, 2, me % 2, stride), (axis, size // 2, me // 2, 2 * stride)


def local(
    edge_state,
    cotangent,
    edge_count,
    triplet_basis,
    triplet_in,
    triplet_out,
    down_weight,
    basis_weight,
    bilinear_weight,
    up_weight,
    first_weight,
    second_weight,
):
    edge_rows = edge_state[0]
    row_count, wide = edge_rows.shape
    line = Line()
    shards, chips = line.size, line.chips
    narrow = down_weight.shape[1]
    down_weight = down_weight.T
    basis = triplet_basis[0]
    basis_width, tri_rows = basis.shape
    slots = tri_rows // shards
    lanes = math.gcd(row_count, 256)
    stacked = narrow * (row_count // lanes)
    tile = math.gcd(row_count, 512)
    tiles = row_count // tile
    row_spec = pl.BlockSpec((tile, wide), lambda i: (i, 0))
    stack_spec = pl.BlockSpec((narrow * (tile // lanes), lanes), lambda i: (i, 0))
    rows_spec = whole(stacked, lanes)

    ends = jnp.stack([triplet_in.reshape(shards, 1, slots), triplet_out.reshape(shards, 1, slots)])
    triplet_specs = (
        [whole(2, shards, 1, slots)] * 2
        + [whole(basis_width, tri_rows)] * 2
        + [whole(basis_width, narrow)]
    )
    block_flops = 8 * slots * row_count * narrow

    down_rows, down_slope = call(
        down_kernel,
        (tiles,),
        [row_spec, whole(narrow, wide)],
        [stack_spec] * 2,
        [shape((stacked, lanes), BF16), shape((stacked, lanes), F32)],
        2 * row_count * wide * narrow,
        row_count * narrow,
    )(in_hbm(edge_rows), in_hbm(down_weight))

    slot_spec = whole(2, narrow, slots)
    slot_shape = pltpu.HBM((2, narrow, slots), BF16)

    ends, leaving = after((ends, basis), down_rows)
    ends_sibling = line.swap(ends)
    basis_sibling = line.swap(leaving)
    triplets = (ends, ends_sibling, basis, basis_sibling, basis_weight)

    def forward(shard, rows, totals, final=False):
        total_shape = shape((stacked, lanes), F32)
        out = call(
            forward_kernel,
            (),
            [SMEM, rows_spec] + triplet_specs + [rows_spec] * len(totals),
            [rows_spec] * 2 + [slot_spec] * 2,
            [pltpu.HBM((stacked, lanes), F32) if final else total_shape, total_shape]
            + [slot_shape] * 2,
            block_flops,
            aliases={7 + i: i for i in range(len(totals)) if i == 1 or not final},
        )(shard, rows, *triplets, *totals)
        return tuple(out[:2]), tuple(out[2:])

    def forward_line(turn, rows, totals, *others):
        kept = [None] * chips
        far = line.trade(rows, 2) if chips == 4 else None
        near = line.trade(rows, 1) if chips > 1 else None
        totals, kept[0] = forward(line.shard(turn, 0), rows, totals)
        if chips == 4:
            rows, far = after((rows, far), *totals)
            last = line.send(rows, [(1, 2), (2, 1)]) + line.send(far, [(2, 3), (1, 0)])
            totals, kept[2] = forward(line.shard(turn, 2), far, totals)
        if chips > 1:
            (near,) = after((near,), *totals, *others)
            totals, kept[1] = forward(line.shard(turn, 1), near, totals)
        if chips == 4:
            totals, kept[3] = forward(line.shard(turn, 3), last, totals, line.groups == 1)
        return totals, kept

    first_turned, second_turned = after((first_weight, second_weight), down_rows)
    first_turned, second_turned = first_turned.T, second_turned.T
    totals, kept = forward_line(0, down_rows, (), first_turned, second_turned)
    if line.groups > 1:

        def forward_turn(carry, turn):
            rows, totals = carry
            rows = line.next_group(rows)
            totals, got = forward_line(turn, rows, totals)
            return (rows, totals), got

        (_, totals), more_kept = lax.scan(
            forward_turn, (down_rows, totals), jnp.arange(1, line.groups)
        )

    grad_rows = 2 * wide + 2 * narrow
    back_summed, back_gathered, dense_grads = call(
        dense_kernel,
        (tiles,),
        [
            SMEM,
            row_spec,
            row_spec,
            stack_spec,
            stack_spec,
            whole(narrow, narrow),
            whole(narrow, wide),
            whole(wide, wide),
            whole(wide, wide),
            whole(wide, wide),
            whole(wide, wide),
        ],
        [row_spec, stack_spec, whole(grad_rows, wide)],
        [
            pltpu.HBM((row_count, wide), BF16),
            shape((stacked, lanes), BF16),
            shape((grad_rows, wide), BF16),
        ],
        12 * row_count * wide * wide + 6 * row_count * wide * narrow,
        3 * row_count * wide,
        scratch=[pltpu.VMEM((grad_rows, wide), F32)],
        vmem_limit_bytes=32 * MIB,
    )(
        edge_count,
        in_hbm(edge_rows),
        in_hbm(cotangent[0]),
        in_hbm(totals[0]) if line.groups == 1 else totals[0],
        line.swap(totals[1]),
        bilinear_weight,
        up_weight,
        in_hbm(first_weight),
        first_turned,
        in_hbm(second_weight),
        second_turned,
    )
    back_sibling = line.swap(back_gathered)
    core, chip, group = stages_of(line, ("core", "chip", "group"))
    dense_grads = add(*scatter_pieces(dense_grads, *core))

    def backward(shard, got, others=()):
        back, *got = after((back_gathered, *got), *others)
        return call(
            backward_kernel,
            (),
            [SMEM, rows_spec, rows_spec, slot_spec, slot_spec] + triplet_specs[:2],
            [rows_spec, slot_spec],
            [shape((stacked, lanes), BF16), shape((2, narrow, slots), BF16)],
            block_flops,
        )(shard, back, back_sibling, *[in_hbm(x) for x in got], ends, ends_sibling)

    dp_steps = lax.axis_size("dp").bit_length() - 1

    def backward_line(turn, kept, summed=None):
        parts = []
        back_coefs = [None] * chips
        others = ()
        if chips == 4:
            last, back_coefs[3] = backward(line.shard(turn, 3), kept[3])
            passed = line.send(last, [(0, 1), (3, 2)])
            middle = line.send(last, [(1, 2), (2, 1)])
            others = (last,)
        if chips > 1:
            near, back_coefs[1] = backward(line.shard(turn, 1), kept[1], others)
            parts.append(line.trade(near, 1))
            others = (near,)
        if chips == 4:
            if summed is not None and dp_steps:
                others = (near, summed)
                summed = across_dp(summed, line, 0)
            far, back_coefs[2] = backward(line.shard(turn, 2), kept[2], others)
            passed, middle, parts[0] = after((passed, middle, parts[0]), far)
            if summed is not None and dp_steps:
                summed = add(*after(summed, far))
                (far,) = after((far,), summed)
            far = add(far, passed)
            others = (far,)
            parts += [middle, line.trade(far, 2)]
        own, back_coefs[0] = backward(line.shard(turn, 0), kept[0], others)
        basis_grad = call(
            basis_kernel,
            (),
            [SMEM] + [slot_spec] * chips + triplet_specs[2:4],
            [whole(narrow, basis_width)],
            [shape((narrow, basis_width), F32)],
            4 * chips * slots * narrow * basis_width,
        )(
            jnp.concatenate([line.shard(turn, bits) for bits in range(chips)]),
            *back_coefs,
            basis,
            basis_sibling,
        )[0]
        return [own] + parts, basis_grad, summed

    back_parts, basis_grad, dense_grads = backward_line(0, kept, dense_grads)
    for step in range(1 if chips == 4 else 0, dp_steps):
        dense_grads = add(*across_dp(dense_grads, line, step))
    first_bit, other_bits = halves_of(chip) if chips > 1 else (chip, chip)
    if chips > 1:
        dense_grads = add(*scatter_pieces(dense_grads, *first_bit))
        dense_grads = butterfly(dense_grads, [other_bits])
    dense_grads = butterfly(dense_grads, [group])
    if line.groups > 1:

        def backward_turn(carry, one):
            traveling, basis_grad = carry
            turn, got = one
            parts, more, _ = backward_line(turn, got)
            return (line.last_group(add(traveling, *parts)), basis_grad + more), None

        (traveling, basis_grad), _ = lax.scan(
            backward_turn,
            (jnp.zeros((stacked, lanes), BF16), basis_grad),
            (jnp.arange(1, line.groups), more_kept),
            reverse=True,
        )
        back_parts = back_parts + [traveling]

    small_rows = narrow + basis_width
    edge_grad, small_grads = call(
        functools.partial(final_kernel, len(back_parts)),
        (tiles,),
        [stack_spec] * len(back_parts)
        + [stack_spec, row_spec, row_spec, whole(narrow, wide), whole(narrow, basis_width)],
        [row_spec, whole(small_rows, wide)],
        [shape((row_count, wide), BF16), shape((small_rows, wide), BF16)],
        4 * row_count * wide * narrow,
        scratch=[pltpu.VMEM((small_rows, wide), F32)],
    )(
        *back_parts,
        down_slope,
        edge_rows,
        back_summed,
        down_weight,
        basis_grad,
    )

    small_grads = add(*scatter_pieces(small_grads, *core))
    small_grads = summed_dp(butterfly(small_grads, [chip, group]), line)
    small_grads = gather_pieces(small_grads, *core)
    if chips > 1:
        dense_grads = gather_pieces(dense_grads, *first_bit)
    for step in reversed(range(dp_steps)):
        dense_grads = joined_dp(dense_grads, line, step)
    dense_grads = gather_pieces(dense_grads, *core)
    scale = 1.0 / math.sqrt(lax.axis_size("dp") * shards * row_count)

    def scaled(source, *dims):
        return call(
            functools.partial(scale_kernel, scale),
            (),
            [whole(*source.shape)],
            [whole(*d) for d in dims],
            [shape(d, F32) for d in dims],
            source.size,
        )(source)

    first_grad, second_grad, up_grad, bilinear_grad = scaled(
        dense_grads, (wide, wide), (wide, wide), (narrow, wide), (narrow, narrow)
    )
    down_grad, basis_grad = scaled(small_grads, (narrow, wide), (basis_width, narrow))
    return (
        edge_grad[None],
        down_grad.T,
        basis_grad,
        bilinear_grad,
        up_grad,
        first_grad,
        second_grad,
    )


def solution(mesh):
    in_specs = (
        P("dp", "graph", None),
        P("dp", "graph", None),
        P("dp", "graph"),
        P("dp", None, "graph"),
        P("dp", "graph"),
        P("dp", "graph"),
        P(),
        P(),
        P(),
        P(),
        P(),
        P(),
    )
    out_specs = (P("dp", "graph", None), P(), P(), P(), P(), P(), P())
    return jax.shard_map(local, mesh=mesh, in_specs=in_specs, out_specs=out_specs, check_vma=False)
```

```python
import functools
import math

import jax
import jax.numpy as jnp
from jax import lax
from jax.experimental import pallas as pl
from jax.experimental.pallas import tpu as pltpu
from jax.sharding import PartitionSpec as P

HALF = 0.7071067811865476
F32 = jnp.float32
BF16 = jnp.bfloat16
MIB = 1024 * 1024


def contract(left, right, left_dim, right_dim):
    return lax.dot_general(
        left, right, (((left_dim,), (right_dim,)), ((), ())), preferred_element_type=F32
    )


def sigmoid(value):
    return 0.5 + 0.5 * jnp.tanh(0.5 * value)


def split_index(index_row, lanes):
    slots = index_row.shape[1]
    low = jnp.bitwise_and(index_row, lanes - 1)
    high = jnp.right_shift(index_row, lanes.bit_length() - 1)
    lane_ids = lax.broadcasted_iota(jnp.int32, (lanes, slots), 0)
    return high, jnp.where(lane_ids == low, 1.0, 0.0).astype(BF16)


def stack(rows, lanes):
    groups = rows.shape[1] // lanes
    return jnp.concatenate([rows[:, g * lanes : (g + 1) * lanes] for g in range(groups)], axis=0)


def unstack(rows, narrow):
    groups = rows.shape[0] // narrow
    return jnp.concatenate([rows[g * narrow : (g + 1) * narrow] for g in range(groups)], axis=1)


def pick_rows(stacked, high, lane_hot, narrow):
    groups = stacked.shape[0] // narrow
    every = contract(stacked, lane_hot, 1, 0)
    picked = jnp.where(high == 0, every[:narrow], 0.0)
    for g in range(1, groups):
        picked = jnp.where(high == g, every[g * narrow : (g + 1) * narrow], picked)
    return picked


def place_rows(values, high, lane_hot, groups):
    zero = jnp.zeros((), values.dtype)
    spread = jnp.concatenate([jnp.where(high == g, values, zero) for g in range(groups)], axis=0)
    return contract(spread.astype(BF16), lane_hot, 1, 1)


def down_kernel(edge_ref, weight_ref, rows_ref, slope_ref):
    lanes = rows_ref.shape[1]
    pre = contract(edge_ref[...], weight_ref[...], 1, 1).T
    logistic = sigmoid(pre)
    rows_ref[...] = stack((pre * logistic).astype(BF16), lanes)
    slope_ref[...] = stack(logistic * (1.0 + pre * (1.0 - logistic)), lanes)


def forward_kernel(copies, shard_ref, *refs):
    rows = refs[0][...]
    for ref in refs[1:copies]:
        rows += ref[...]
    refs = refs[copies:]
    ends, basis, weight_ref = refs[:2], refs[2:4], refs[4]
    totals, fetched_ref, coef_ref = refs[-4:-2], refs[-2], refs[-1]
    shard = shard_ref[0]
    narrow = weight_ref.shape[1]
    groups = totals[0].shape[0] // narrow
    lanes = totals[0].shape[1]
    slots = ends[0].shape[3]
    at = pl.ds(pl.multiple_of(shard * slots, slots), slots)
    for i in range(2):
        high, lane_hot = split_index(ends[i][0, shard], lanes)
        fetched = pick_rows(rows, high, lane_hot, narrow)
        fetched_ref[i] = fetched.astype(BF16)
        coef = contract(weight_ref[...], basis[i][:, at], 0, 0)
        coef_ref[i] = coef.astype(BF16)
        high, lane_hot = split_index(ends[i][1, shard], lanes)
        placed = place_rows(coef * fetched, high, lane_hot, groups)
        if len(refs) == 11:
            placed += refs[5 + i][...]
        totals[i][...] = placed


def dense_kernel(
    count_ref,
    edge_ref,
    cotangent_ref,
    gathered_ref,
    more_ref,
    bilinear_ref,
    up_ref,
    first_ref,
    first_turned_ref,
    second_ref,
    second_turned_ref,
    summed_ref,
    back_ref,
    grads_ref,
    total,
):
    step = pl.program_id(0)
    tile, wide = edge_ref.shape
    narrow = bilinear_ref.shape[0]
    lanes = gathered_ref.shape[1]

    @pl.when(step == 0)
    def _():
        total[...] = jnp.zeros_like(total)

    gathered = unstack((gathered_ref[...] + more_ref[...]).astype(BF16), narrow)
    mixed = contract(bilinear_ref[...], gathered, 0, 0).astype(BF16)
    pre_up = contract(mixed, up_ref[...], 0, 0)
    up_logistic = sigmoid(pre_up)
    summed_half = (edge_ref[...].astype(F32) + pre_up * up_logistic).astype(BF16)
    pre_first = contract(summed_half, first_ref[...], 1, 0)
    first_logistic = sigmoid(pre_first)
    first_rows = (pre_first * first_logistic).astype(BF16)
    pre_second = contract(first_rows, second_ref[...], 1, 0)
    logistic = sigmoid(pre_second)
    row_ids = step * tile + lax.broadcasted_iota(jnp.int32, (tile, 1), 0)
    live = jnp.where(row_ids < count_ref[0, 0], HALF, 0.0)
    back_top = cotangent_ref[...].astype(F32) * live
    back_second = (back_top * (logistic * (1.0 + pre_second * (1.0 - logistic)))).astype(BF16)
    slope = first_logistic * (1.0 + pre_first * (1.0 - first_logistic))
    back_first = (contract(back_second, second_turned_ref[...], 1, 0) * slope).astype(BF16)
    back_summed = back_top + contract(back_first, first_turned_ref[...], 1, 0)
    summed_ref[...] = back_summed.astype(BF16)
    slope = up_logistic * (1.0 + pre_up * (1.0 - up_logistic))
    back_up = (back_summed * slope).astype(BF16)
    back_mixed = contract(back_up, up_ref[...], 1, 1).T.astype(BF16)
    back_ref[...] = stack(contract(bilinear_ref[...], back_mixed, 1, 0).astype(BF16), lanes)
    total[:wide] += contract(summed_half, back_first, 0, 0)
    total[wide : 2 * wide] += contract(first_rows, back_second, 0, 0)
    total[2 * wide : 2 * wide + narrow] += contract(mixed, back_up, 1, 0)
    total[2 * wide + narrow :, :narrow] += contract(gathered, back_mixed, 1, 1)

    @pl.when(step == pl.num_programs(0) - 1)
    def _():
        grads_ref[...] = total[...].astype(BF16)


def backward_kernel(count, shards_ref, own_ref, sibling_ref, *refs):
    fetched, coefs, ends = refs[:count], refs[count : 2 * count], refs[2 * count : 2 * count + 2]
    parts, back_coefs = refs[2 * count + 2 : 3 * count + 2], refs[3 * count + 2 :]
    narrow = fetched[0].shape[1]
    groups = own_ref.shape[0] // narrow
    lanes = own_ref.shape[1]
    for s in range(count):
        shard = shards_ref[s]
        part = None
        for i, back_ref in enumerate((own_ref, sibling_ref)):
            high, lane_hot = split_index(ends[i][1, shard], lanes)
            message = pick_rows(back_ref[...], high, lane_hot, narrow)
            back_coefs[s][i] = (message * fetched[s][i].astype(F32)).astype(BF16)
            high, lane_hot = split_index(ends[i][0, shard], lanes)
            placed = place_rows(message * coefs[s][i].astype(F32), high, lane_hot, groups)
            part = placed if part is None else part + placed
        parts[s][...] = part.astype(BF16)


def basis_kernel(shards_ref, *refs):
    back_coefs, basis, grad_ref = refs[:-3], refs[-3:-1], refs[-1]
    slots = back_coefs[0].shape[2]
    grad = jnp.zeros(grad_ref.shape, F32)
    for s, ref in enumerate(back_coefs):
        at = pl.ds(pl.multiple_of(shards_ref[s] * slots, slots), slots)
        for i in range(2):
            grad += contract(ref[i], basis[i][:, at], 1, 1)
    grad_ref[...] = grad


def final_kernel(count, *refs):
    parts = refs[:count]
    slope_ref, edge_ref, summed_ref, weight_ref, basis_ref, edge_grad_ref, grads_ref, total = refs[
        count:
    ]
    step = pl.program_id(0)
    narrow = weight_ref.shape[0]
    basis_width = basis_ref.shape[1]

    @pl.when(step == 0)
    def _():
        total[...] = jnp.zeros_like(total)

    back_down = parts[0][...].astype(F32)
    for part in parts[1:]:
        back_down += part[...].astype(F32)
    back_pre = unstack((back_down * slope_ref[...]).astype(BF16), narrow)
    total[:narrow] += contract(back_pre, edge_ref[...], 1, 0)
    edge_grad_ref[...] = (
        summed_ref[...].astype(F32) + contract(back_pre, weight_ref[...], 0, 0)
    ).astype(BF16)

    @pl.when(step == pl.num_programs(0) - 1)
    def _():
        total[narrow : narrow + basis_width, :narrow] = basis_ref[...].T
        grads_ref[...] = total[...].astype(BF16)


def scale_kernel(scale, source_ref, *outs):
    row = 0
    for out in outs:
        rows, columns = out.shape
        out[...] = source_ref[row : row + rows, :columns].astype(F32) * scale
        row += rows


def call(kernel, grid, in_specs, out_specs, out_shape, flops, transcendentals=0, scratch=(), aliases=None, **params):
    def run(*operands):
        size = sum(x.size * x.dtype.itemsize for x in operands)
        size += sum(math.prod(x.shape) * x.dtype.itemsize for x in out_shape)
        return pl.pallas_call(
            kernel,
            grid=grid,
            in_specs=in_specs,
            out_specs=out_specs,
            out_shape=out_shape,
            scratch_shapes=scratch,
            input_output_aliases=aliases or {},
            compiler_params=pltpu.CompilerParams(**{"vmem_limit_bytes": 32 * MIB, **params}),
            cost_estimate=pl.CostEstimate(
                flops=flops, bytes_accessed=size, transcendentals=transcendentals
            ),
        )(*operands)

    return run


def whole(*shape):
    return pl.BlockSpec(shape, lambda *_: (0,) * len(shape))


SMEM = pl.BlockSpec(memory_space=pltpu.SMEM)


def in_hbm(array):
    return pltpu.with_memory_space_constraint(array, pltpu.HBM)


def shape(dims, dtype):
    return jax.ShapeDtypeStruct(dims, dtype)


def turned(count, size, stride, turn):
    pairs = []
    for g in range(count):
        place = g // stride % size
        pairs.append((g, g + ((place + turn) % size - place) * stride))
    return pairs


class Line:
    cores = 2

    def __init__(self):
        self.size = lax.axis_size("graph")
        self.chips = math.gcd(self.size // self.cores, 4)
        self.span = self.chips * self.cores
        self.groups = self.size // self.span
        me = lax.axis_index("graph")
        self.core = me % self.cores
        self.chip = me // self.cores % self.chips
        self.group = me // self.span

    def send(self, array, moves):
        pairs = [
            (base + one * self.cores + core, base + other * self.cores + core)
            for base in range(0, self.size, self.span)
            for one, other in moves
            for core in range(self.cores)
        ]
        return lax.ppermute(array, "graph", pairs)

    def trade(self, array, bit):
        return self.send(array, [(chip, chip ^ bit) for chip in range(self.chips)])

    def swap(self, array):
        return lax.ppermute(array, "graph", [(g, g ^ 1) for g in range(self.size)])

    def next_group(self, array):
        return lax.ppermute(array, "graph", turned(self.size, self.groups, self.span, -1))

    def last_group(self, array):
        return lax.ppermute(array, "graph", turned(self.size, self.groups, self.span, 1))

    def shard(self, turn, bits):
        group = (self.group + turn) % self.groups
        shard = group * self.span + (self.chip ^ bits) * self.cores + self.core
        return shard.astype(jnp.int32).reshape(1)


def add(*arrays):
    return sum(a.astype(F32) for a in arrays).astype(BF16)


def after(arrays, *others):
    return lax.optimization_barrier((tuple(arrays), others))[0]


def dp_pairs(line, step):
    bits = lax.axis_size("dp").bit_length() - 1
    pairs = []
    for dp in range(lax.axis_size("dp")):
        for g in range(line.size):
            bit = (step + g % line.cores) % bits
            pairs.append((dp * line.size + g, (dp ^ (1 << bit)) * line.size + g))
    return pairs


def dp_place(line, step):
    bits = lax.axis_size("dp").bit_length() - 1
    return lax.axis_index("dp") >> ((step + line.core) % bits) & 1


def halves(array, place):
    rows = array.shape[0] // 2
    first = place == 0
    return (
        jnp.where(first, array[:rows], array[rows:]),
        jnp.where(first, array[rows:], array[:rows]),
    )


def joined(mine, other, place):
    return jnp.where(
        place == 0, jnp.concatenate([mine, other]), jnp.concatenate([other, mine])
    )


def across_dp(array, line, step):
    mine, away = halves(array, dp_place(line, step))
    return [mine, lax.ppermute(away, ("dp", "graph"), dp_pairs(line, step))]


def across_cores(array, line):
    mine, away = halves(array, line.core)
    return [mine, line.swap(away)]


def joined_dp(piece, line, step):
    other = lax.ppermute(piece, ("dp", "graph"), dp_pairs(line, step))
    return joined(piece, other, dp_place(line, step))


def summed_dp(array, line):
    for step in range(lax.axis_size("dp").bit_length() - 1):
        other = lax.ppermute(array, ("dp", "graph"), dp_pairs(line, step))
        array = add(array, other)
    return array


def summed_graph(array, line, bits):
    for bit in bits:
        pairs = [(g, g ^ (1 << bit)) for g in range(line.size)]
        array = add(array, lax.ppermute(array, "graph", pairs))
    return array


def local(
    edge_state,
    cotangent,
    edge_count,
    triplet_basis,
    triplet_in,
    triplet_out,
    down_weight,
    basis_weight,
    bilinear_weight,
    up_weight,
    first_weight,
    second_weight,
):
    edge_rows = edge_state[0]
    row_count, wide = edge_rows.shape
    line = Line()
    shards, chips = line.size, line.chips
    narrow = down_weight.shape[1]
    down_weight = down_weight.T
    basis = triplet_basis[0]
    basis_width, tri_rows = basis.shape
    slots = tri_rows // shards
    lanes = math.gcd(row_count, 256)
    stacked = narrow * (row_count // lanes)
    tile = math.gcd(row_count, 512)
    tiles = row_count // tile
    row_spec = pl.BlockSpec((tile, wide), lambda i: (i, 0))
    stack_spec = pl.BlockSpec((narrow * (tile // lanes), lanes), lambda i: (i, 0))
    rows_spec = whole(stacked, lanes)

    ends = jnp.stack([triplet_in.reshape(shards, 1, slots), triplet_out.reshape(shards, 1, slots)])
    triplet_specs = (
        [whole(2, shards, 1, slots)] * 2
        + [whole(basis_width, tri_rows)] * 2
        + [whole(basis_width, narrow)]
    )
    block_flops = 8 * slots * row_count * narrow

    down_rows, down_slope = call(
        down_kernel,
        (tiles,),
        [row_spec, whole(narrow, wide)],
        [stack_spec] * 2,
        [shape((stacked, lanes), BF16), shape((stacked, lanes), F32)],
        2 * row_count * wide * narrow,
        row_count * narrow,
    )(in_hbm(edge_rows), in_hbm(down_weight))

    slot_spec = whole(2, narrow, slots)
    slot_shape = shape((2, narrow, slots), BF16)

    ends, leaving = after((ends, basis), down_rows)
    ends_sibling = line.swap(ends)
    basis_sibling = line.swap(leaving)
    triplets = (ends, ends_sibling, basis, basis_sibling, basis_weight)

    def forward(shard, rows, totals):
        first = len(rows) + 6
        out = call(
            functools.partial(forward_kernel, len(rows)),
            (),
            [SMEM] + [rows_spec] * len(rows) + triplet_specs + [rows_spec] * len(totals),
            [rows_spec] * 2 + [slot_spec] * 2,
            [shape((stacked, lanes), F32)] * 2 + [slot_shape] * 2,
            block_flops,
            aliases={first + i: i for i in range(len(totals))},
        )(shard, *rows, *triplets, *totals)
        return tuple(out[:2]), tuple(out[2:])

    def forward_line(turn, rows, totals, *others):
        kept = [None] * chips
        far = line.trade(rows, 2) if chips == 4 else None
        near = line.trade(rows, 1) if chips > 1 else None
        totals, kept[0] = forward(line.shard(turn, 0), [rows], totals)
        if chips == 4:
            rows, far = after((rows, far), *totals)
            last = [line.send(rows, [(1, 2), (2, 1)]), line.send(far, [(2, 3), (1, 0)])]
            totals, kept[2] = forward(line.shard(turn, 2), [far], totals)
        if chips > 1:
            (near,) = after((near,), *totals, *others)
            totals, kept[1] = forward(line.shard(turn, 1), [near], totals)
        if chips == 4:
            totals, kept[3] = forward(line.shard(turn, 3), last, totals)
        return totals, kept

    first_turned, second_turned = after((first_weight, second_weight), down_rows)
    first_turned, second_turned = first_turned.T, second_turned.T
    totals, kept = forward_line(0, down_rows, (), first_turned, second_turned)
    if line.groups > 1:

        def forward_turn(carry, turn):
            rows, totals = carry
            rows = line.next_group(rows)
            totals, got = forward_line(turn, rows, totals)
            return (rows, totals), got

        (_, totals), more_kept = lax.scan(
            forward_turn, (down_rows, totals), jnp.arange(1, line.groups)
        )

    grad_rows = 2 * wide + 2 * narrow
    back_summed, back_gathered, dense_grads = call(
        dense_kernel,
        (tiles,),
        [
            SMEM,
            row_spec,
            row_spec,
            stack_spec,
            stack_spec,
            whole(narrow, narrow),
            whole(narrow, wide),
            whole(wide, wide),
            whole(wide, wide),
            whole(wide, wide),
            whole(wide, wide),
        ],
        [row_spec, stack_spec, whole(grad_rows, wide)],
        [
            pltpu.HBM((row_count, wide), BF16),
            shape((stacked, lanes), BF16),
            shape((grad_rows, wide), BF16),
        ],
        12 * row_count * wide * wide + 6 * row_count * wide * narrow,
        3 * row_count * wide,
        scratch=[pltpu.VMEM((grad_rows, wide), F32)],
    )(
        edge_count,
        edge_rows,
        cotangent[0],
        totals[0],
        line.swap(totals[1]),
        bilinear_weight,
        up_weight,
        first_weight,
        first_turned,
        second_weight,
        second_turned,
    )
    back_sibling = line.swap(back_gathered)

    def backward(turn, bits, kept, others=()):
        count = len(bits)
        (back,) = after((back_gathered,), *others)
        out = call(
            functools.partial(backward_kernel, count),
            (),
            [SMEM] + [rows_spec] * 2 + [slot_spec] * (2 * count) + triplet_specs[:2],
            [rows_spec] * count + [slot_spec] * count,
            [shape((stacked, lanes), BF16)] * count + [slot_shape] * count,
            count * block_flops,
        )(
            jnp.concatenate([line.shard(turn, one) for one in bits]),
            back,
            back_sibling,
            *[kept[one][0] for one in bits],
            *[kept[one][1] for one in bits],
            ends,
            ends_sibling,
        )
        return out[:count], out[count:]

    dp_steps = lax.axis_size("dp").bit_length() - 1
    graph_bits = line.size.bit_length() - 1

    def backward_line(turn, kept, pieces=None):
        parts, back_coefs, others = [], [], ()
        summed = None
        if chips == 4:
            (last,), got = backward(turn, (3,), kept)
            back_coefs = [*got, *back_coefs]
            passed = line.send(last, [(0, 1), (3, 2)])
            middle = line.send(last, [(1, 2), (2, 1)])
            others = (last,)
            if pieces is not None:
                summed = add(*after(pieces, last))
                others = (last, summed)
            (far,), got = backward(turn, (2,), kept, others)
            back_coefs = [*got, *back_coefs]
            passed, middle = after((passed, middle), far)
            far = add(far, passed)
            others = (far,)
            parts = [middle, line.trade(far, 2)]
        elif pieces is not None:
            summed = add(*pieces)
        if chips > 1:
            (near, own), got = backward(turn, (1, 0), kept, others)
            parts.append(line.trade(near, 1))
        else:
            (own,), got = backward(turn, (0,), kept, others)
        back_coefs = [*reversed(got), *back_coefs]
        basis_grad = call(
            basis_kernel,
            (),
            [SMEM] + [slot_spec] * chips + triplet_specs[2:4],
            [whole(narrow, basis_width)],
            [shape((narrow, basis_width), F32)],
            4 * chips * slots * narrow * basis_width,
        )(
            jnp.concatenate([line.shard(turn, bits) for bits in range(chips)]),
            *back_coefs,
            basis,
            basis_sibling,
        )[0]
        return [own] + parts, basis_grad, summed

    back_parts, basis_grad, dense_grads = backward_line(0, kept, across_cores(dense_grads, line))
    for step in range(dp_steps):
        dense_grads = add(*across_dp(dense_grads, line, step))
    dense_grads = summed_graph(dense_grads, line, range(1, graph_bits))
    if line.groups > 1:

        def backward_turn(carry, one):
            traveling, basis_grad = carry
            turn, got = one
            parts, more, _ = backward_line(turn, got)
            return (line.last_group(add(traveling, *parts)), basis_grad + more), None

        (traveling, basis_grad), _ = lax.scan(
            backward_turn,
            (jnp.zeros((stacked, lanes), BF16), basis_grad),
            (jnp.arange(1, line.groups), more_kept),
            reverse=True,
        )
        back_parts = back_parts + [traveling]

    small_rows = narrow + basis_width
    edge_grad, small_grads = call(
        functools.partial(final_kernel, len(back_parts)),
        (tiles,),
        [stack_spec] * len(back_parts)
        + [stack_spec, row_spec, row_spec, whole(narrow, wide), whole(narrow, basis_width)],
        [row_spec, whole(small_rows, wide)],
        [shape((row_count, wide), BF16), shape((small_rows, wide), BF16)],
        4 * row_count * wide * narrow,
        scratch=[pltpu.VMEM((small_rows, wide), F32)],
    )(
        *back_parts,
        down_slope,
        edge_rows,
        back_summed,
        down_weight,
        basis_grad,
    )

    small_grads = add(*across_cores(small_grads, line))
    small_grads = summed_graph(summed_dp(small_grads, line), line, range(1, graph_bits))
    small_grads = joined(small_grads, line.swap(small_grads), line.core)
    for step in reversed(range(dp_steps)):
        dense_grads = joined_dp(dense_grads, line, step)
    dense_grads = joined(dense_grads, line.swap(dense_grads), line.core)
    scale = 1.0 / math.sqrt(lax.axis_size("dp") * shards * row_count)

    def scaled(source, *dims):
        return call(
            functools.partial(scale_kernel, scale),
            (),
            [whole(*source.shape)],
            [whole(*d) for d in dims],
            [shape(d, F32) for d in dims],
            source.size,
        )(source)

    first_grad, second_grad, up_grad, bilinear_grad = scaled(
        dense_grads, (wide, wide), (wide, wide), (narrow, wide), (narrow, narrow)
    )
    down_grad, basis_grad = scaled(small_grads, (narrow, wide), (basis_width, narrow))
    return (
        edge_grad[None],
        down_grad.T,
        basis_grad,
        bilinear_grad,
        up_grad,
        first_grad,
        second_grad,
    )


def solution(mesh):
    in_specs = (
        P("dp", "graph", None),
        P("dp", "graph", None),
        P("dp", "graph"),
        P("dp", None, "graph"),
        P("dp", "graph"),
        P("dp", "graph"),
        P(),
        P(),
        P(),
        P(),
        P(),
        P(),
    )
    out_specs = (P("dp", "graph", None), P(), P(), P(), P(), P(), P())
    return jax.shard_map(local, mesh=mesh, in_specs=in_specs, out_specs=out_specs, check_vma=False)
```

```python
import functools
import math

import jax
import jax.numpy as jnp
from jax import lax
from jax.experimental import pallas as pl
from jax.experimental.pallas import tpu as pltpu
from jax.sharding import PartitionSpec as P

HALF = 0.7071067811865476
F32 = jnp.float32
BF16 = jnp.bfloat16
MIB = 1024 * 1024
FORWARD_GRANT = 10
BACKWARD_GRANT = 10
DENSE_GRANT = 18
FINAL_GRANT = 12


def contract(left, right, left_dim, right_dim):
    return lax.dot_general(
        left, right, (((left_dim,), (right_dim,)), ((), ())), preferred_element_type=F32
    )


def sigmoid(value):
    return 0.5 + 0.5 * jnp.tanh(0.5 * value)


def split_index(index_row, lanes):
    slots = index_row.shape[1]
    low = jnp.bitwise_and(index_row, lanes - 1)
    high = jnp.right_shift(index_row, lanes.bit_length() - 1)
    lane_ids = lax.broadcasted_iota(jnp.int32, (lanes, slots), 0)
    return high, jnp.where(lane_ids == low, 1.0, 0.0).astype(BF16)


def stack(rows, lanes):
    groups = rows.shape[1] // lanes
    return jnp.concatenate([rows[:, g * lanes : (g + 1) * lanes] for g in range(groups)], axis=0)


def unstack(rows, narrow):
    groups = rows.shape[0] // narrow
    return jnp.concatenate([rows[g * narrow : (g + 1) * narrow] for g in range(groups)], axis=1)


def pick_rows(stacked, high, lane_hot, narrow):
    groups = stacked.shape[0] // narrow
    every = contract(stacked, lane_hot, 1, 0)
    picked = jnp.where(high == 0, every[:narrow], 0.0)
    for g in range(1, groups):
        picked = jnp.where(high == g, every[g * narrow : (g + 1) * narrow], picked)
    return picked


def place_rows(values, high, lane_hot, groups):
    zero = jnp.zeros((), values.dtype)
    spread = jnp.concatenate([jnp.where(high == g, values, zero) for g in range(groups)], axis=0)
    return contract(spread.astype(BF16), lane_hot, 1, 1)


def down_kernel(edge_ref, weight_ref, rows_ref, slope_ref):
    lanes = rows_ref.shape[1]
    pre = contract(edge_ref[...], weight_ref[...], 1, 1).T
    logistic = sigmoid(pre)
    rows_ref[...] = stack((pre * logistic).astype(BF16), lanes)
    slope_ref[...] = stack(logistic * (1.0 + pre * (1.0 - logistic)), lanes)


def forward_kernel(copies, shard_ref, *refs):
    rows = refs[0][...]
    for ref in refs[1:copies]:
        rows += ref[...]
    refs = refs[copies:]
    ends, basis, weight_ref = refs[:2], refs[2:4], refs[4]
    totals, fetched_ref, coef_ref = refs[-4:-2], refs[-2], refs[-1]
    shard = shard_ref[0]
    narrow = weight_ref.shape[1]
    groups = totals[0].shape[0] // narrow
    lanes = totals[0].shape[1]
    slots = ends[0].shape[3]
    at = pl.ds(pl.multiple_of(shard * slots, slots), slots)
    for i in range(2):
        high, lane_hot = split_index(ends[i][0, shard], lanes)
        fetched = pick_rows(rows, high, lane_hot, narrow)
        fetched_ref[i] = fetched.astype(BF16)
        coef = contract(weight_ref[...], basis[i][:, at], 0, 0)
        coef_ref[i] = coef.astype(BF16)
        high, lane_hot = split_index(ends[i][1, shard], lanes)
        placed = place_rows(coef * fetched, high, lane_hot, groups)
        if len(refs) == 11:
            placed += refs[5 + i][...]
        totals[i][...] = placed


def dense_kernel(
    count_ref,
    edge_ref,
    cotangent_ref,
    gathered_ref,
    more_ref,
    bilinear_ref,
    up_ref,
    first_ref,
    first_turned_ref,
    second_ref,
    second_turned_ref,
    summed_ref,
    back_ref,
    grads_ref,
    total,
):
    step = pl.program_id(0)
    tile, wide = edge_ref.shape
    narrow = bilinear_ref.shape[0]
    lanes = gathered_ref.shape[1]

    @pl.when(step == 0)
    def _():
        total[...] = jnp.zeros_like(total)

    gathered = unstack((gathered_ref[...] + more_ref[...]).astype(BF16), narrow)
    mixed = contract(bilinear_ref[...], gathered, 0, 0).astype(BF16)
    pre_up = contract(mixed, up_ref[...], 0, 0)
    up_logistic = sigmoid(pre_up)
    summed_half = (edge_ref[...].astype(F32) + pre_up * up_logistic).astype(BF16)
    pre_first = contract(summed_half, first_ref[...], 1, 0)
    first_logistic = sigmoid(pre_first)
    first_rows = (pre_first * first_logistic).astype(BF16)
    pre_second = contract(first_rows, second_ref[...], 1, 0)
    logistic = sigmoid(pre_second)
    row_ids = step * tile + lax.broadcasted_iota(jnp.int32, (tile, 1), 0)
    live = jnp.where(row_ids < count_ref[0, 0], HALF, 0.0)
    back_top = cotangent_ref[...].astype(F32) * live
    back_second = (back_top * (logistic * (1.0 + pre_second * (1.0 - logistic)))).astype(BF16)
    slope = first_logistic * (1.0 + pre_first * (1.0 - first_logistic))
    back_first = (contract(back_second, second_turned_ref[...], 1, 0) * slope).astype(BF16)
    back_summed = back_top + contract(back_first, first_turned_ref[...], 1, 0)
    summed_ref[...] = back_summed.astype(BF16)
    slope = up_logistic * (1.0 + pre_up * (1.0 - up_logistic))
    back_up = (back_summed * slope).astype(BF16)
    back_mixed = contract(back_up, up_ref[...], 1, 1).T.astype(BF16)
    back_ref[...] = stack(contract(bilinear_ref[...], back_mixed, 1, 0).astype(BF16), lanes)
    total[:wide] += contract(summed_half, back_first, 0, 0)
    total[wide : 2 * wide] += contract(first_rows, back_second, 0, 0)
    total[2 * wide : 2 * wide + narrow] += contract(mixed, back_up, 1, 0)
    total[2 * wide + narrow :, :narrow] += contract(gathered, back_mixed, 1, 1)

    @pl.when(step == pl.num_programs(0) - 1)
    def _():
        grads_ref[...] = total[...].astype(BF16)


def backward_kernel(count, shards_ref, own_ref, sibling_ref, *refs):
    fetched, coefs, ends = refs[:count], refs[count : 2 * count], refs[2 * count : 2 * count + 2]
    parts, back_coefs = refs[2 * count + 2 : 3 * count + 2], refs[3 * count + 2 :]
    narrow = fetched[0].shape[1]
    groups = own_ref.shape[0] // narrow
    lanes = own_ref.shape[1]
    for s in range(count):
        shard = shards_ref[s]
        part = None
        for i, back_ref in enumerate((own_ref, sibling_ref)):
            high, lane_hot = split_index(ends[i][1, shard], lanes)
            message = pick_rows(back_ref[...], high, lane_hot, narrow)
            back_coefs[s][i] = (message * fetched[s][i].astype(F32)).astype(BF16)
            high, lane_hot = split_index(ends[i][0, shard], lanes)
            placed = place_rows(message * coefs[s][i].astype(F32), high, lane_hot, groups)
            part = placed if part is None else part + placed
        parts[s][...] = part.astype(BF16)


def basis_kernel(shards_ref, *refs):
    back_coefs, basis, grad_ref = refs[:-3], refs[-3:-1], refs[-1]
    slots = back_coefs[0].shape[2]
    grad = jnp.zeros(grad_ref.shape, F32)
    for s, ref in enumerate(back_coefs):
        at = pl.ds(pl.multiple_of(shards_ref[s] * slots, slots), slots)
        for i in range(2):
            grad += contract(ref[i], basis[i][:, at], 1, 1)
    grad_ref[...] = grad


def final_kernel(count, *refs):
    parts = refs[:count]
    slope_ref, edge_ref, summed_ref, weight_ref, basis_ref, edge_grad_ref, grads_ref, total = refs[
        count:
    ]
    step = pl.program_id(0)
    narrow = weight_ref.shape[0]
    basis_width = basis_ref.shape[1]

    @pl.when(step == 0)
    def _():
        total[...] = jnp.zeros_like(total)

    back_down = parts[0][...].astype(F32)
    for part in parts[1:]:
        back_down += part[...].astype(F32)
    back_pre = unstack((back_down * slope_ref[...]).astype(BF16), narrow)
    total[:narrow] += contract(back_pre, edge_ref[...], 1, 0)
    edge_grad_ref[...] = (
        summed_ref[...].astype(F32) + contract(back_pre, weight_ref[...], 0, 0)
    ).astype(BF16)

    @pl.when(step == pl.num_programs(0) - 1)
    def _():
        total[narrow : narrow + basis_width, :narrow] = basis_ref[...].T
        grads_ref[...] = total[...].astype(BF16)


def scale_kernel(scale, source_ref, *outs):
    row = 0
    for out in outs:
        rows, columns = out.shape
        out[...] = source_ref[row : row + rows, :columns].astype(F32) * scale
        row += rows


def call(kernel, grid, in_specs, out_specs, out_shape, flops, transcendentals=0, scratch=(), aliases=None, grant=8):
    def run(*operands):
        size = sum(x.size * x.dtype.itemsize for x in operands)
        size += sum(math.prod(x.shape) * x.dtype.itemsize for x in out_shape)
        return pl.pallas_call(
            kernel,
            grid=grid,
            in_specs=in_specs,
            out_specs=out_specs,
            out_shape=out_shape,
            scratch_shapes=scratch,
            input_output_aliases=aliases or {},
            compiler_params=pltpu.CompilerParams(vmem_limit_bytes=grant * MIB),
            cost_estimate=pl.CostEstimate(
                flops=flops, bytes_accessed=size, transcendentals=transcendentals
            ),
        )(*operands)

    return run


def whole(*shape):
    return pl.BlockSpec(shape, lambda *_: (0,) * len(shape))


SMEM = pl.BlockSpec(memory_space=pltpu.SMEM)


def in_hbm(array):
    return pltpu.with_memory_space_constraint(array, pltpu.HBM)


def shape(dims, dtype):
    return jax.ShapeDtypeStruct(dims, dtype)


def turned(count, size, stride, turn):
    pairs = []
    for g in range(count):
        place = g // stride % size
        pairs.append((g, g + ((place + turn) % size - place) * stride))
    return pairs


class Line:
    cores = 2

    def __init__(self):
        self.size = lax.axis_size("graph")
        self.chips = math.gcd(self.size // self.cores, 4)
        self.span = self.chips * self.cores
        self.groups = self.size // self.span
        me = lax.axis_index("graph")
        self.core = me % self.cores
        self.chip = me // self.cores % self.chips
        self.group = me // self.span

    def send(self, array, moves):
        pairs = [
            (base + one * self.cores + core, base + other * self.cores + core)
            for base in range(0, self.size, self.span)
            for one, other in moves
            for core in range(self.cores)
        ]
        return lax.ppermute(array, "graph", pairs)

    def trade(self, array, bit):
        return self.send(array, [(chip, chip ^ bit) for chip in range(self.chips)])

    def swap(self, array):
        return lax.ppermute(array, "graph", [(g, g ^ 1) for g in range(self.size)])

    def next_group(self, array):
        return lax.ppermute(array, "graph", turned(self.size, self.groups, self.span, -1))

    def last_group(self, array):
        return lax.ppermute(array, "graph", turned(self.size, self.groups, self.span, 1))

    def shard(self, turn, bits):
        group = (self.group + turn) % self.groups
        shard = group * self.span + (self.chip ^ bits) * self.cores + self.core
        return shard.astype(jnp.int32).reshape(1)


def add(*arrays):
    return sum(a.astype(F32) for a in arrays).astype(BF16)


def after(arrays, *others):
    return lax.optimization_barrier((tuple(arrays), others))[0]


def dp_pairs(line, step):
    bits = lax.axis_size("dp").bit_length() - 1
    pairs = []
    for dp in range(lax.axis_size("dp")):
        for g in range(line.size):
            bit = (step + g % line.cores) % bits
            pairs.append((dp * line.size + g, (dp ^ (1 << bit)) * line.size + g))
    return pairs


def dp_place(line, step):
    bits = lax.axis_size("dp").bit_length() - 1
    return lax.axis_index("dp") >> ((step + line.core) % bits) & 1


def halves(array, place):
    rows = array.shape[0] // 2
    first = place == 0
    return (
        jnp.where(first, array[:rows], array[rows:]),
        jnp.where(first, array[rows:], array[:rows]),
    )


def joined(mine, other, place):
    return jnp.where(
        place == 0, jnp.concatenate([mine, other]), jnp.concatenate([other, mine])
    )


def across_dp(array, line, step):
    mine, away = halves(array, dp_place(line, step))
    return [mine, lax.ppermute(away, ("dp", "graph"), dp_pairs(line, step))]


def across_cores(array, line):
    mine, away = halves(array, line.core)
    return [mine, line.swap(away)]


def joined_dp(piece, line, step, *others):
    other = lax.ppermute(piece, ("dp", "graph"), dp_pairs(line, step))
    (other,) = after((other,), *others)
    return joined(piece, other, dp_place(line, step))


def summed_dp(array, line):
    for step in range(lax.axis_size("dp").bit_length() - 1):
        other = lax.ppermute(array, ("dp", "graph"), dp_pairs(line, step))
        array = add(array, other)
    return array


def summed_graph(array, line, bits, *others):
    for bit in bits:
        pairs = [(g, g ^ (1 << bit)) for g in range(line.size)]
        (other,) = after((lax.ppermute(array, "graph", pairs),), *others)
        array = add(array, other)
    return array


def local(
    edge_state,
    cotangent,
    edge_count,
    triplet_basis,
    triplet_in,
    triplet_out,
    down_weight,
    basis_weight,
    bilinear_weight,
    up_weight,
    first_weight,
    second_weight,
):
    edge_rows = edge_state[0]
    row_count, wide = edge_rows.shape
    line = Line()
    shards, chips = line.size, line.chips
    narrow = down_weight.shape[1]
    down_weight = down_weight.T
    basis = triplet_basis[0]
    basis_width, tri_rows = basis.shape
    slots = tri_rows // shards
    lanes = math.gcd(row_count, 256)
    stacked = narrow * (row_count // lanes)
    tile = math.gcd(row_count, 512)
    tiles = row_count // tile
    row_spec = pl.BlockSpec((tile, wide), lambda i: (i, 0))
    stack_spec = pl.BlockSpec((narrow * (tile // lanes), lanes), lambda i: (i, 0))
    rows_spec = whole(stacked, lanes)

    ends = jnp.stack([triplet_in.reshape(shards, 1, slots), triplet_out.reshape(shards, 1, slots)])
    triplet_specs = (
        [whole(2, shards, 1, slots)] * 2
        + [whole(basis_width, tri_rows)] * 2
        + [whole(basis_width, narrow)]
    )
    block_flops = 8 * slots * row_count * narrow

    down_rows, down_slope = call(
        down_kernel,
        (tiles,),
        [row_spec, whole(narrow, wide)],
        [stack_spec] * 2,
        [shape((stacked, lanes), BF16), shape((stacked, lanes), F32)],
        2 * row_count * wide * narrow,
        row_count * narrow,
    )(in_hbm(edge_rows), in_hbm(down_weight))

    slot_spec = whole(2, narrow, slots)
    slot_shape = shape((2, narrow, slots), BF16)

    ends, leaving = after((ends, basis), down_rows)
    ends_sibling = line.swap(ends)
    basis_sibling = line.swap(leaving)
    triplets = (ends, ends_sibling, basis, basis_sibling, basis_weight)

    def forward(shard, rows, totals):
        first = len(rows) + 6
        out = call(
            functools.partial(forward_kernel, len(rows)),
            (),
            [SMEM] + [rows_spec] * len(rows) + triplet_specs + [rows_spec] * len(totals),
            [rows_spec] * 2 + [slot_spec] * 2,
            [shape((stacked, lanes), F32)] * 2 + [slot_shape] * 2,
            block_flops,
            aliases={first + i: i for i in range(len(totals))},
            grant=FORWARD_GRANT,
        )(shard, *rows, *triplets, *totals)
        return tuple(out[:2]), tuple(out[2:])

    def forward_line(turn, rows, totals, *others):
        kept = [None] * chips
        far = line.trade(rows, 2) if chips == 4 else None
        near = line.trade(rows, 1) if chips > 1 else None
        totals, kept[0] = forward(line.shard(turn, 0), [rows], totals)
        if chips == 4:
            rows, far = after((rows, far), *totals)
            last = [line.send(rows, [(1, 2), (2, 1)]), line.send(far, [(2, 3), (1, 0)])]
            totals, kept[2] = forward(line.shard(turn, 2), [far], totals)
        if chips > 1:
            (near,) = after((near,), *totals, *others)
            totals, kept[1] = forward(line.shard(turn, 1), [near], totals)
        if chips == 4:
            totals, kept[3] = forward(line.shard(turn, 3), last, totals)
        return totals, kept

    first_turned, second_turned = after((first_weight, second_weight), down_rows)
    first_turned, second_turned = first_turned.T, second_turned.T
    totals, kept = forward_line(0, down_rows, (), first_turned, second_turned)
    if line.groups > 1:

        def forward_turn(carry, turn):
            rows, totals = carry
            rows = line.next_group(rows)
            totals, got = forward_line(turn, rows, totals)
            return (rows, totals), got

        (_, totals), more_kept = lax.scan(
            forward_turn, (down_rows, totals), jnp.arange(1, line.groups)
        )

    grad_rows = 2 * wide + 2 * narrow
    back_summed, back_gathered, dense_grads = call(
        dense_kernel,
        (tiles,),
        [
            SMEM,
            row_spec,
            row_spec,
            stack_spec,
            stack_spec,
            whole(narrow, narrow),
            whole(narrow, wide),
            whole(wide, wide),
            whole(wide, wide),
            whole(wide, wide),
            whole(wide, wide),
        ],
        [row_spec, stack_spec, whole(grad_rows, wide)],
        [
            pltpu.HBM((row_count, wide), BF16),
            shape((stacked, lanes), BF16),
            shape((grad_rows, wide), BF16),
        ],
        12 * row_count * wide * wide + 6 * row_count * wide * narrow,
        3 * row_count * wide,
        scratch=[pltpu.VMEM((grad_rows, wide), F32)],
        grant=DENSE_GRANT,
    )(
        edge_count,
        in_hbm(edge_rows),
        in_hbm(cotangent[0]),
        totals[0],
        line.swap(totals[1]),
        bilinear_weight,
        up_weight,
        in_hbm(first_weight),
        first_turned,
        in_hbm(second_weight),
        second_turned,
    )
    back_sibling = line.swap(back_gathered)

    def backward(turn, bits, kept, others=()):
        count = len(bits)
        (back,) = after((back_gathered,), *others)
        out = call(
            functools.partial(backward_kernel, count),
            (),
            [SMEM] + [rows_spec] * 2 + [slot_spec] * (2 * count) + triplet_specs[:2],
            [rows_spec] * count + [slot_spec] * count,
            [shape((stacked, lanes), BF16)] * count + [slot_shape] * count,
            count * block_flops,
            grant=BACKWARD_GRANT,
        )(
            jnp.concatenate([line.shard(turn, one) for one in bits]),
            back,
            back_sibling,
            *[kept[one][0] for one in bits],
            *[kept[one][1] for one in bits],
            ends,
            ends_sibling,
        )
        return out[:count], out[count:]

    dp_steps = lax.axis_size("dp").bit_length() - 1
    graph_bits = line.size.bit_length() - 1

    def backward_line(turn, kept, pieces=None):
        parts, others = [], ()
        last_coefs = near_coefs = ()
        if chips == 4:
            (last,), last_coefs = backward(turn, (3,), kept)
            passed = line.send(last, [(0, 1), (3, 2)])
            middle = line.send(last, [(1, 2), (2, 1)])
            others = (last,)
        if pieces is not None:
            pieces = add(*after(pieces, *others))
            others = (*others, pieces)
        if chips == 4:
            (near, far), near_coefs = backward(turn, (1, 2), kept, others)
            passed, middle = after((passed, middle), far)
            far = add(far, passed)
            others = (far,)
            parts = [middle, line.trade(far, 2), line.trade(near, 1)]
        elif chips == 2:
            (near,), near_coefs = backward(turn, (1,), kept, others)
            parts = [line.trade(near, 1)]
        (own,), own_coefs = backward(turn, (0,), kept, others)
        if pieces is not None:
            for step in range(dp_steps):
                pieces = add(*across_dp(pieces, line, step))
            own_coefs = after(own_coefs, pieces)
        back_coefs = [*own_coefs, *near_coefs, *last_coefs]
        basis_grad = call(
            basis_kernel,
            (),
            [SMEM] + [slot_spec] * chips + triplet_specs[2:4],
            [whole(narrow, basis_width)],
            [shape((narrow, basis_width), F32)],
            4 * chips * slots * narrow * basis_width,
        )(
            jnp.concatenate([line.shard(turn, bits) for bits in range(chips)]),
            *back_coefs,
            basis,
            basis_sibling,
        )[0]
        return [own] + parts, basis_grad, pieces

    back_parts, basis_grad, dense_grads = backward_line(0, kept, across_cores(dense_grads, line))
    dense_grads = summed_graph(dense_grads, line, range(1, 2))
    if line.groups > 1:

        def backward_turn(carry, one):
            traveling, basis_grad = carry
            turn, got = one
            parts, more, _ = backward_line(turn, got)
            return (line.last_group(add(traveling, *parts)), basis_grad + more), None

        (traveling, basis_grad), _ = lax.scan(
            backward_turn,
            (jnp.zeros((stacked, lanes), BF16), basis_grad),
            (jnp.arange(1, line.groups), more_kept),
            reverse=True,
        )
        back_parts = back_parts + [traveling]

    small_rows = narrow + basis_width
    edge_grad, small_grads = call(
        functools.partial(final_kernel, len(back_parts)),
        (tiles,),
        [stack_spec] * len(back_parts)
        + [stack_spec, row_spec, row_spec, whole(narrow, wide), whole(narrow, basis_width)],
        [row_spec, whole(small_rows, wide)],
        [shape((row_count, wide), BF16), shape((small_rows, wide), BF16)],
        4 * row_count * wide * narrow,
        scratch=[pltpu.VMEM((small_rows, wide), F32)],
        grant=FINAL_GRANT,
    )(
        *back_parts,
        down_slope,
        edge_rows,
        back_summed,
        down_weight,
        basis_grad,
    )

    small_grads = add(*across_cores(small_grads, line))
    small_grads = summed_dp(small_grads, line)
    dense_grads = summed_graph(dense_grads, line, range(2, graph_bits), small_grads)
    for bit in range(1, graph_bits):
        small_grads = summed_graph(small_grads, line, (bit,))
        if bit <= dp_steps:
            dense_grads = joined_dp(dense_grads, line, dp_steps - bit, small_grads)
    for step in reversed(range(max(0, dp_steps - graph_bits + 1))):
        dense_grads = joined_dp(dense_grads, line, step)
    dense_grads = joined(dense_grads, line.swap(dense_grads), line.core)
    small_grads = joined(small_grads, line.swap(small_grads), line.core)
    scale = 1.0 / math.sqrt(lax.axis_size("dp") * shards * row_count)

    def scaled(source, *dims):
        return call(
            functools.partial(scale_kernel, scale),
            (),
            [whole(*source.shape)],
            [whole(*d) for d in dims],
            [shape(d, F32) for d in dims],
            source.size,
        )(source)

    first_grad, second_grad, up_grad, bilinear_grad = scaled(
        dense_grads, (wide, wide), (wide, wide), (narrow, wide), (narrow, narrow)
    )
    down_grad, basis_grad = scaled(small_grads, (narrow, wide), (basis_width, narrow))
    return (
        edge_grad[None],
        down_grad.T,
        basis_grad,
        bilinear_grad,
        up_grad,
        first_grad,
        second_grad,
    )


def solution(mesh):
    in_specs = (
        P("dp", "graph", None),
        P("dp", "graph", None),
        P("dp", "graph"),
        P("dp", None, "graph"),
        P("dp", "graph"),
        P("dp", "graph"),
        P(),
        P(),
        P(),
        P(),
        P(),
        P(),
    )
    out_specs = (P("dp", "graph", None), P(), P(), P(), P(), P(), P())
    return jax.shard_map(local, mesh=mesh, in_specs=in_specs, out_specs=out_specs, check_vma=False)
```

```python
import functools
import math

import jax
import jax.numpy as jnp
from jax import lax
from jax.experimental import pallas as pl
from jax.experimental.pallas import tpu as pltpu
from jax.sharding import PartitionSpec as P

HALF = 0.7071067811865476
F32 = jnp.float32
BF16 = jnp.bfloat16
MIB = 1024 * 1024
FORWARD_GRANT = 10
BACKWARD_GRANT = 10
DENSE_GRANT = 18
FINAL_GRANT = 12


def contract(left, right, left_dim, right_dim):
    return lax.dot_general(
        left, right, (((left_dim,), (right_dim,)), ((), ())), preferred_element_type=F32
    )


def sigmoid(value):
    return 0.5 + 0.5 * jnp.tanh(0.5 * value)


def split_index(index_row, lanes):
    slots = index_row.shape[1]
    low = jnp.bitwise_and(index_row, lanes - 1)
    high = jnp.right_shift(index_row, lanes.bit_length() - 1)
    lane_ids = lax.broadcasted_iota(jnp.int32, (lanes, slots), 0)
    return high, jnp.where(lane_ids == low, 1.0, 0.0).astype(BF16)


def stack(rows, lanes):
    groups = rows.shape[1] // lanes
    return jnp.concatenate([rows[:, g * lanes : (g + 1) * lanes] for g in range(groups)], axis=0)


def unstack(rows, narrow):
    groups = rows.shape[0] // narrow
    return jnp.concatenate([rows[g * narrow : (g + 1) * narrow] for g in range(groups)], axis=1)


def pick_rows(stacked, high, lane_hot, narrow):
    groups = stacked.shape[0] // narrow
    every = contract(stacked, lane_hot, 1, 0)
    picked = jnp.where(high == 0, every[:narrow], 0.0)
    for g in range(1, groups):
        picked = jnp.where(high == g, every[g * narrow : (g + 1) * narrow], picked)
    return picked


def place_rows(values, high, lane_hot, groups):
    zero = jnp.zeros((), values.dtype)
    spread = jnp.concatenate([jnp.where(high == g, values, zero) for g in range(groups)], axis=0)
    return contract(spread.astype(BF16), lane_hot, 1, 1)


def down_kernel(edge_ref, weight_ref, rows_ref, slope_ref):
    lanes = rows_ref.shape[1]
    pre = contract(edge_ref[...], weight_ref[...], 1, 1).T
    logistic = sigmoid(pre)
    rows_ref[...] = stack((pre * logistic).astype(BF16), lanes)
    slope_ref[...] = stack(logistic * (1.0 + pre * (1.0 - logistic)), lanes)


def forward_kernel(shard_ref, rows_ref, *refs):
    rows = rows_ref[...]
    ends, basis, weight_ref = refs[:2], refs[2:4], refs[4]
    totals, fetched_ref, coef_ref = refs[-4:-2], refs[-2], refs[-1]
    shard = shard_ref[0]
    narrow = weight_ref.shape[1]
    groups = totals[0].shape[0] // narrow
    lanes = totals[0].shape[1]
    slots = ends[0].shape[3]
    at = pl.ds(pl.multiple_of(shard * slots, slots), slots)
    for i in range(2):
        high, lane_hot = split_index(ends[i][0, shard], lanes)
        fetched = pick_rows(rows, high, lane_hot, narrow)
        fetched_ref[i] = fetched.astype(BF16)
        coef = contract(weight_ref[...], basis[i][:, at], 0, 0)
        coef_ref[i] = coef.astype(BF16)
        high, lane_hot = split_index(ends[i][1, shard], lanes)
        placed = place_rows(coef * fetched, high, lane_hot, groups)
        if len(refs) == 11:
            placed += refs[5 + i][...]
        totals[i][...] = placed


def dense_kernel(
    count_ref,
    edge_ref,
    cotangent_ref,
    gathered_ref,
    more_ref,
    bilinear_ref,
    up_ref,
    first_ref,
    first_turned_ref,
    second_ref,
    second_turned_ref,
    summed_ref,
    back_ref,
    grads_ref,
    total,
):
    step = pl.program_id(0)
    tile, wide = edge_ref.shape
    narrow = bilinear_ref.shape[0]
    lanes = gathered_ref.shape[1]

    @pl.when(step == 0)
    def _():
        total[...] = jnp.zeros_like(total)

    gathered = unstack((gathered_ref[...] + more_ref[...]).astype(BF16), narrow)
    mixed = contract(bilinear_ref[...], gathered, 0, 0).astype(BF16)
    pre_up = contract(mixed, up_ref[...], 0, 0)
    up_logistic = sigmoid(pre_up)
    summed_half = (edge_ref[...].astype(F32) + pre_up * up_logistic).astype(BF16)
    pre_first = contract(summed_half, first_ref[...], 1, 0)
    first_logistic = sigmoid(pre_first)
    first_rows = (pre_first * first_logistic).astype(BF16)
    pre_second = contract(first_rows, second_ref[...], 1, 0)
    logistic = sigmoid(pre_second)
    row_ids = step * tile + lax.broadcasted_iota(jnp.int32, (tile, 1), 0)
    live = jnp.where(row_ids < count_ref[0, 0], HALF, 0.0)
    back_top = cotangent_ref[...].astype(F32) * live
    back_second = (back_top * (logistic * (1.0 + pre_second * (1.0 - logistic)))).astype(BF16)
    slope = first_logistic * (1.0 + pre_first * (1.0 - first_logistic))
    back_first = (contract(back_second, second_turned_ref[...], 1, 0) * slope).astype(BF16)
    back_summed = back_top + contract(back_first, first_turned_ref[...], 1, 0)
    summed_ref[...] = back_summed.astype(BF16)
    slope = up_logistic * (1.0 + pre_up * (1.0 - up_logistic))
    back_up = (back_summed * slope).astype(BF16)
    back_mixed = contract(back_up, up_ref[...], 1, 1).T.astype(BF16)
    back_ref[...] = stack(contract(bilinear_ref[...], back_mixed, 1, 0).astype(BF16), lanes)
    total[:wide] += contract(summed_half, back_first, 0, 0)
    total[wide : 2 * wide] += contract(first_rows, back_second, 0, 0)
    total[2 * wide : 2 * wide + narrow] += contract(mixed, back_up, 1, 0)
    total[2 * wide + narrow :, :narrow] += contract(gathered, back_mixed, 1, 1)

    @pl.when(step == pl.num_programs(0) - 1)
    def _():
        grads_ref[...] = total[...].astype(BF16)


def backward_kernel(count, shards_ref, own_ref, sibling_ref, *refs):
    fetched, coefs, ends = refs[:count], refs[count : 2 * count], refs[2 * count : 2 * count + 2]
    parts, back_coefs = refs[2 * count + 2 : 3 * count + 2], refs[3 * count + 2 :]
    narrow = fetched[0].shape[1]
    groups = own_ref.shape[0] // narrow
    lanes = own_ref.shape[1]
    for s in range(count):
        shard = shards_ref[s]
        part = None
        for i, back_ref in enumerate((own_ref, sibling_ref)):
            high, lane_hot = split_index(ends[i][1, shard], lanes)
            message = pick_rows(back_ref[...], high, lane_hot, narrow)
            back_coefs[s][i] = (message * fetched[s][i].astype(F32)).astype(BF16)
            high, lane_hot = split_index(ends[i][0, shard], lanes)
            placed = place_rows(message * coefs[s][i].astype(F32), high, lane_hot, groups)
            part = placed if part is None else part + placed
        parts[s][...] = part.astype(BF16)


def basis_kernel(shards_ref, *refs):
    back_coefs, basis, grad_ref = refs[:-3], refs[-3:-1], refs[-1]
    slots = back_coefs[0].shape[2]
    grad = jnp.zeros(grad_ref.shape, F32)
    for s, ref in enumerate(back_coefs):
        at = pl.ds(pl.multiple_of(shards_ref[s] * slots, slots), slots)
        for i in range(2):
            grad += contract(ref[i], basis[i][:, at], 1, 1)
    grad_ref[...] = grad


def final_kernel(count, *refs):
    parts = refs[:count]
    slope_ref, edge_ref, summed_ref, weight_ref, basis_ref, edge_grad_ref, grads_ref, total = refs[
        count:
    ]
    step = pl.program_id(0)
    narrow = weight_ref.shape[0]
    basis_width = basis_ref.shape[1]

    @pl.when(step == 0)
    def _():
        total[...] = jnp.zeros_like(total)

    back_down = parts[0][...].astype(F32)
    for part in parts[1:]:
        back_down += part[...].astype(F32)
    back_pre = unstack((back_down * slope_ref[...]).astype(BF16), narrow)
    total[:narrow] += contract(back_pre, edge_ref[...], 1, 0)
    edge_grad_ref[...] = (
        summed_ref[...].astype(F32) + contract(back_pre, weight_ref[...], 0, 0)
    ).astype(BF16)

    @pl.when(step == pl.num_programs(0) - 1)
    def _():
        total[narrow : narrow + basis_width, :narrow] = basis_ref[...].T
        grads_ref[...] = total[...].astype(BF16)


def scale_kernel(scale, source_ref, *outs):
    row = 0
    for out in outs:
        rows, columns = out.shape
        out[...] = source_ref[row : row + rows, :columns].astype(F32) * scale
        row += rows


def call(kernel, grid, in_specs, out_specs, out_shape, flops, transcendentals=0, scratch=(), aliases=None, grant=8):
    def run(*operands):
        size = sum(x.size * x.dtype.itemsize for x in operands)
        size += sum(math.prod(x.shape) * x.dtype.itemsize for x in out_shape)
        return pl.pallas_call(
            kernel,
            grid=grid,
            in_specs=in_specs,
            out_specs=out_specs,
            out_shape=out_shape,
            scratch_shapes=scratch,
            input_output_aliases=aliases or {},
            compiler_params=pltpu.CompilerParams(vmem_limit_bytes=grant * MIB),
            cost_estimate=pl.CostEstimate(
                flops=flops, bytes_accessed=size, transcendentals=transcendentals
            ),
        )(*operands)

    return run


def whole(*shape):
    return pl.BlockSpec(shape, lambda *_: (0,) * len(shape))


SMEM = pl.BlockSpec(memory_space=pltpu.SMEM)


def in_hbm(array):
    return pltpu.with_memory_space_constraint(array, pltpu.HBM)


def shape(dims, dtype):
    return jax.ShapeDtypeStruct(dims, dtype)


def turned(count, size, stride, turn):
    pairs = []
    for g in range(count):
        place = g // stride % size
        pairs.append((g, g + ((place + turn) % size - place) * stride))
    return pairs


class Line:
    cores = 2

    def __init__(self):
        self.size = lax.axis_size("graph")
        self.chips = math.gcd(self.size // self.cores, 4)
        self.span = self.chips * self.cores
        self.groups = self.size // self.span
        me = lax.axis_index("graph")
        self.core = me % self.cores
        self.chip = me // self.cores % self.chips
        self.group = me // self.span

    def send(self, array, moves):
        pairs = [
            (base + one * self.cores + core, base + other * self.cores + core)
            for base in range(0, self.size, self.span)
            for one, other in moves
            for core in range(self.cores)
        ]
        return lax.ppermute(array, "graph", pairs)

    def trade(self, array, bits):
        return self.send(array, [(chip, chip ^ bits) for chip in range(self.chips)])

    def swap(self, array):
        return lax.ppermute(array, "graph", [(g, g ^ 1) for g in range(self.size)])

    def next_group(self, array):
        return lax.ppermute(array, "graph", turned(self.size, self.groups, self.span, -1))

    def last_group(self, array):
        return lax.ppermute(array, "graph", turned(self.size, self.groups, self.span, 1))

    def shard(self, turn, bits):
        group = (self.group + turn) % self.groups
        shard = group * self.span + (self.chip ^ bits) * self.cores + self.core
        return shard.astype(jnp.int32).reshape(1)


def add(*arrays):
    return sum(a.astype(F32) for a in arrays).astype(BF16)


def after(arrays, *others):
    return lax.optimization_barrier((tuple(arrays), others))[0]


def dp_pairs(line, step):
    bits = lax.axis_size("dp").bit_length() - 1
    pairs = []
    for dp in range(lax.axis_size("dp")):
        for g in range(line.size):
            bit = (step + g % line.cores) % bits
            pairs.append((dp * line.size + g, (dp ^ (1 << bit)) * line.size + g))
    return pairs


def dp_place(line, step):
    bits = lax.axis_size("dp").bit_length() - 1
    return lax.axis_index("dp") >> ((step + line.core) % bits) & 1


def halves(array, place):
    rows = array.shape[0] // 2
    first = place == 0
    return (
        jnp.where(first, array[:rows], array[rows:]),
        jnp.where(first, array[rows:], array[:rows]),
    )


def joined(mine, other, place):
    return jnp.where(
        place == 0, jnp.concatenate([mine, other]), jnp.concatenate([other, mine])
    )


def across_dp(array, line, step):
    mine, away = halves(array, dp_place(line, step))
    return [mine, lax.ppermute(away, ("dp", "graph"), dp_pairs(line, step))]


def across_cores(array, line):
    mine, away = halves(array, line.core)
    return [mine, line.swap(away)]


def joined_dp(piece, line, step, *others):
    other = lax.ppermute(piece, ("dp", "graph"), dp_pairs(line, step))
    (other,) = after((other,), *others)
    return joined(piece, other, dp_place(line, step))


def summed_dp(array, line):
    for step in range(lax.axis_size("dp").bit_length() - 1):
        other = lax.ppermute(array, ("dp", "graph"), dp_pairs(line, step))
        array = add(array, other)
    return array


def summed_graph(array, line, bits, *others):
    for bit in bits:
        pairs = [(g, g ^ (1 << bit)) for g in range(line.size)]
        (other,) = after((lax.ppermute(array, "graph", pairs),), *others)
        array = add(array, other)
    return array


def local(
    edge_state,
    cotangent,
    edge_count,
    triplet_basis,
    triplet_in,
    triplet_out,
    down_weight,
    basis_weight,
    bilinear_weight,
    up_weight,
    first_weight,
    second_weight,
):
    edge_rows = edge_state[0]
    row_count, wide = edge_rows.shape
    line = Line()
    shards, chips = line.size, line.chips
    narrow = down_weight.shape[1]
    down_weight = down_weight.T
    basis = triplet_basis[0]
    basis_width, tri_rows = basis.shape
    slots = tri_rows // shards
    lanes = math.gcd(row_count, 256)
    stacked = narrow * (row_count // lanes)
    tile = math.gcd(row_count, 512)
    tiles = row_count // tile
    row_spec = pl.BlockSpec((tile, wide), lambda i: (i, 0))
    stack_spec = pl.BlockSpec((narrow * (tile // lanes), lanes), lambda i: (i, 0))
    rows_spec = whole(stacked, lanes)

    ends = jnp.stack([triplet_in.reshape(shards, 1, slots), triplet_out.reshape(shards, 1, slots)])
    triplet_specs = (
        [whole(2, shards, 1, slots)] * 2
        + [whole(basis_width, tri_rows)] * 2
        + [whole(basis_width, narrow)]
    )
    block_flops = 8 * slots * row_count * narrow

    down_rows, down_slope = call(
        down_kernel,
        (tiles,),
        [row_spec, whole(narrow, wide)],
        [stack_spec] * 2,
        [shape((stacked, lanes), BF16), shape((stacked, lanes), F32)],
        2 * row_count * wide * narrow,
        row_count * narrow,
    )(in_hbm(edge_rows), in_hbm(down_weight))

    slot_spec = whole(2, narrow, slots)
    slot_shape = pltpu.HBM((2, narrow, slots), BF16)

    ends, leaving = after((ends, basis), down_rows)
    ends_sibling = line.swap(ends)
    basis_sibling = line.swap(leaving)
    triplets = (ends, ends_sibling, basis, basis_sibling, basis_weight)

    def forward(turn, bits, rows, totals):
        total_shape = shape((stacked, lanes), F32)
        final = line.groups == 1 and bits == chips - 1
        out = call(
            forward_kernel,
            (),
            [SMEM, rows_spec] + triplet_specs + [rows_spec] * len(totals),
            [rows_spec] * 2 + [slot_spec] * 2,
            [pltpu.HBM((stacked, lanes), F32) if final else total_shape, total_shape]
            + [slot_shape] * 2,
            block_flops,
            aliases={7 + i: i for i in range(len(totals)) if i == 1 or not final},
            grant=FORWARD_GRANT,
        )(line.shard(turn, bits), rows, *triplets, *totals)
        return tuple(out[:2]), tuple(out[2:])

    def forward_line(turn, rows, totals, *others):
        arriving = [line.trade(rows, bits) for bits in range(1, chips)]
        totals, got = forward(turn, 0, rows, totals)
        kept = [got]
        for bits in range(1, chips):
            (rows,) = after((arriving[bits - 1],), *totals, *others)
            totals, got = forward(turn, bits, rows, totals)
            kept.append(got)
        return totals, kept

    first_turned, second_turned = after((first_weight, second_weight), down_rows)
    first_turned, second_turned = first_turned.T, second_turned.T
    totals, kept = forward_line(0, down_rows, (), first_turned, second_turned)
    if line.groups > 1:

        def forward_turn(carry, turn):
            rows, totals = carry
            rows = line.next_group(rows)
            totals, got = forward_line(turn, rows, totals)
            return (rows, totals), got

        (_, totals), more_kept = lax.scan(
            forward_turn, (down_rows, totals), jnp.arange(1, line.groups)
        )

    grad_rows = 2 * wide + 2 * narrow
    back_summed, back_gathered, dense_grads = call(
        dense_kernel,
        (tiles,),
        [
            SMEM,
            row_spec,
            row_spec,
            stack_spec,
            stack_spec,
            whole(narrow, narrow),
            whole(narrow, wide),
            whole(wide, wide),
            whole(wide, wide),
            whole(wide, wide),
            whole(wide, wide),
        ],
        [row_spec, stack_spec, whole(grad_rows, wide)],
        [
            pltpu.HBM((row_count, wide), BF16),
            shape((stacked, lanes), BF16),
            shape((grad_rows, wide), BF16),
        ],
        12 * row_count * wide * wide + 6 * row_count * wide * narrow,
        3 * row_count * wide,
        scratch=[pltpu.VMEM((grad_rows, wide), F32)],
        grant=DENSE_GRANT,
    )(
        edge_count,
        in_hbm(edge_rows),
        in_hbm(cotangent[0]),
        in_hbm(totals[0]) if line.groups == 1 else totals[0],
        line.swap(totals[1]),
        bilinear_weight,
        up_weight,
        in_hbm(first_weight),
        first_turned,
        in_hbm(second_weight),
        second_turned,
    )
    back_sibling = line.swap(back_gathered)

    def backward(turn, bits, kept, others=()):
        count = len(bits)
        (back,) = after((back_gathered,), *others)
        out = call(
            functools.partial(backward_kernel, count),
            (),
            [SMEM] + [rows_spec] * 2 + [slot_spec] * (2 * count) + triplet_specs[:2],
            [rows_spec] * count + [slot_spec] * count,
            [shape((stacked, lanes), BF16)] * count + [shape((2, narrow, slots), BF16)] * count,
            count * block_flops,
            grant=BACKWARD_GRANT,
        )(
            jnp.concatenate([line.shard(turn, one) for one in bits]),
            back,
            back_sibling,
            *[kept[one][0] for one in bits],
            *[kept[one][1] for one in bits],
            ends,
            ends_sibling,
        )
        return out[:count], out[count:]

    dp_steps = lax.axis_size("dp").bit_length() - 1
    graph_bits = line.size.bit_length() - 1

    def backward_line(turn, kept, pieces=None):
        parts, others = [], ()
        last_coefs = near_coefs = ()
        if chips == 4:
            (last,), last_coefs = backward(turn, (3,), kept)
            passed = line.send(last, [(0, 1), (3, 2)])
            middle = line.send(last, [(1, 2), (2, 1)])
            others = (last,)
        if pieces is not None:
            pieces = add(*after(pieces, *others))
            others = (*others, pieces)
        if chips == 4:
            (near, far), near_coefs = backward(turn, (1, 2), kept, others)
            (passed,) = after((passed,), far)
            far = add(far, passed)
            (middle,) = after((middle,), far)
            (far,) = after((far,), middle)
            others = (far,)
            parts = [middle, line.trade(far, 2), line.trade(near, 1)]
        elif chips == 2:
            (near,), near_coefs = backward(turn, (1,), kept, others)
            parts = [line.trade(near, 1)]
        (own,), own_coefs = backward(turn, (0,), kept, others)
        if pieces is not None:
            for step in range(dp_steps):
                pieces = add(*across_dp(pieces, line, step))
            own_coefs = after(own_coefs, pieces)
        back_coefs = [*own_coefs, *near_coefs, *last_coefs]
        basis_grad = call(
            basis_kernel,
            (),
            [SMEM] + [slot_spec] * chips + triplet_specs[2:4],
            [whole(narrow, basis_width)],
            [shape((narrow, basis_width), F32)],
            4 * chips * slots * narrow * basis_width,
        )(
            jnp.concatenate([line.shard(turn, bits) for bits in range(chips)]),
            *back_coefs,
            basis,
            basis_sibling,
        )[0]
        return [own] + parts, basis_grad, pieces

    back_parts, basis_grad, dense_grads = backward_line(0, kept, across_cores(dense_grads, line))
    dense_grads = summed_graph(dense_grads, line, range(1, 2))
    if line.groups > 1:

        def backward_turn(carry, one):
            traveling, basis_grad = carry
            turn, got = one
            parts, more, _ = backward_line(turn, got)
            return (line.last_group(add(traveling, *parts)), basis_grad + more), None

        (traveling, basis_grad), _ = lax.scan(
            backward_turn,
            (jnp.zeros((stacked, lanes), BF16), basis_grad),
            (jnp.arange(1, line.groups), more_kept),
            reverse=True,
        )
        back_parts = back_parts + [traveling]

    small_rows = narrow + basis_width
    edge_grad, small_grads = call(
        functools.partial(final_kernel, len(back_parts)),
        (tiles,),
        [stack_spec] * len(back_parts)
        + [stack_spec, row_spec, row_spec, whole(narrow, wide), whole(narrow, basis_width)],
        [row_spec, whole(small_rows, wide)],
        [shape((row_count, wide), BF16), shape((small_rows, wide), BF16)],
        4 * row_count * wide * narrow,
        scratch=[pltpu.VMEM((small_rows, wide), F32)],
        grant=FINAL_GRANT,
    )(
        *back_parts,
        down_slope,
        edge_rows,
        back_summed,
        down_weight,
        basis_grad,
    )

    small_grads = add(*across_cores(small_grads, line))
    small_grads = summed_dp(small_grads, line)
    dense_grads = summed_graph(dense_grads, line, range(2, graph_bits), small_grads)
    for bit in range(1, graph_bits):
        small_grads = summed_graph(small_grads, line, (bit,))
        if bit <= dp_steps:
            dense_grads = joined_dp(dense_grads, line, dp_steps - bit, small_grads)
    for step in reversed(range(max(0, dp_steps - graph_bits + 1))):
        dense_grads = joined_dp(dense_grads, line, step)
    dense_grads = joined(dense_grads, line.swap(dense_grads), line.core)
    small_grads = joined(small_grads, line.swap(small_grads), line.core)
    scale = 1.0 / math.sqrt(lax.axis_size("dp") * shards * row_count)

    def scaled(source, *dims):
        return call(
            functools.partial(scale_kernel, scale),
            (),
            [whole(*source.shape)],
            [whole(*d) for d in dims],
            [shape(d, F32) for d in dims],
            source.size,
        )(source)

    first_grad, second_grad, up_grad, bilinear_grad = scaled(
        dense_grads, (wide, wide), (wide, wide), (narrow, wide), (narrow, narrow)
    )
    down_grad, basis_grad = scaled(small_grads, (narrow, wide), (basis_width, narrow))
    return (
        edge_grad[None],
        down_grad.T,
        basis_grad,
        bilinear_grad,
        up_grad,
        first_grad,
        second_grad,
    )


def solution(mesh):
    in_specs = (
        P("dp", "graph", None),
        P("dp", "graph", None),
        P("dp", "graph"),
        P("dp", None, "graph"),
        P("dp", "graph"),
        P("dp", "graph"),
        P(),
        P(),
        P(),
        P(),
        P(),
        P(),
    )
    out_specs = (P("dp", "graph", None), P(), P(), P(), P(), P(), P())
    return jax.shard_map(local, mesh=mesh, in_specs=in_specs, out_specs=out_specs, check_vma=False)
```

```python
import functools
import math

import jax
import jax.numpy as jnp
from jax import lax
from jax.experimental import pallas as pl
from jax.experimental.pallas import tpu as pltpu
from jax.sharding import PartitionSpec as P

HALF = 0.7071067811865476
F32 = jnp.float32
BF16 = jnp.bfloat16
MIB = 1024 * 1024
FORWARD_GRANT = 10
BACKWARD_GRANT = 10
DENSE_GRANT = 18
FINAL_GRANT = 12


def contract(left, right, left_dim, right_dim):
    return lax.dot_general(
        left, right, (((left_dim,), (right_dim,)), ((), ())), preferred_element_type=F32
    )


def sigmoid(value):
    return 0.5 + 0.5 * jnp.tanh(0.5 * value)


def split_index(index_row, lanes):
    slots = index_row.shape[1]
    low = jnp.bitwise_and(index_row, lanes - 1)
    high = jnp.right_shift(index_row, lanes.bit_length() - 1)
    lane_ids = lax.broadcasted_iota(jnp.int32, (lanes, slots), 0)
    return high, jnp.where(lane_ids == low, 1.0, 0.0).astype(BF16)


def stack(rows, lanes):
    groups = rows.shape[1] // lanes
    return jnp.concatenate([rows[:, g * lanes : (g + 1) * lanes] for g in range(groups)], axis=0)


def unstack(rows, narrow):
    groups = rows.shape[0] // narrow
    return jnp.concatenate([rows[g * narrow : (g + 1) * narrow] for g in range(groups)], axis=1)


def pick_rows(stacked, high, lane_hot, narrow):
    groups = stacked.shape[0] // narrow
    every = contract(stacked, lane_hot, 1, 0)
    picked = jnp.where(high == 0, every[:narrow], 0.0)
    for g in range(1, groups):
        picked = jnp.where(high == g, every[g * narrow : (g + 1) * narrow], picked)
    return picked


def place_rows(values, high, lane_hot, groups):
    zero = jnp.zeros((), values.dtype)
    spread = jnp.concatenate([jnp.where(high == g, values, zero) for g in range(groups)], axis=0)
    return contract(spread.astype(BF16), lane_hot, 1, 1)


def down_kernel(edge_ref, weight_ref, rows_ref, slope_ref):
    lanes = rows_ref.shape[1]
    pre = contract(edge_ref[...], weight_ref[...], 1, 1).T
    logistic = sigmoid(pre)
    rows_ref[...] = stack((pre * logistic).astype(BF16), lanes)
    slope_ref[...] = stack(logistic * (1.0 + pre * (1.0 - logistic)), lanes)


def forward_kernel(shard_ref, rows_ref, *refs):
    rows = rows_ref[...]
    ends, basis, weight_ref = refs[:2], refs[2:4], refs[4]
    totals, fetched_ref, coef_ref = refs[-4:-2], refs[-2], refs[-1]
    shard = shard_ref[0]
    narrow = weight_ref.shape[1]
    groups = totals[0].shape[0] // narrow
    lanes = totals[0].shape[1]
    slots = ends[0].shape[3]
    at = pl.ds(pl.multiple_of(shard * slots, slots), slots)
    for i in range(2):
        high, lane_hot = split_index(ends[i][0, shard], lanes)
        fetched = pick_rows(rows, high, lane_hot, narrow)
        fetched_ref[i] = fetched.astype(BF16)
        coef = contract(weight_ref[...], basis[i][:, at], 0, 0)
        coef_ref[i] = coef.astype(BF16)
        high, lane_hot = split_index(ends[i][1, shard], lanes)
        placed = place_rows(coef * fetched, high, lane_hot, groups)
        if len(refs) == 11:
            placed += refs[5 + i][...]
        totals[i][...] = placed


def dense_kernel(
    count_ref,
    edge_ref,
    cotangent_ref,
    gathered_ref,
    more_ref,
    bilinear_ref,
    up_ref,
    first_ref,
    first_turned_ref,
    second_ref,
    second_turned_ref,
    summed_ref,
    back_ref,
    grads_ref,
    total,
):
    step = pl.program_id(0)
    tile, wide = edge_ref.shape
    narrow = bilinear_ref.shape[0]
    lanes = gathered_ref.shape[1]

    @pl.when(step == 0)
    def _():
        total[...] = jnp.zeros_like(total)

    gathered = unstack((gathered_ref[...] + more_ref[...]).astype(BF16), narrow)
    mixed = contract(bilinear_ref[...], gathered, 0, 0).astype(BF16)
    pre_up = contract(mixed, up_ref[...], 0, 0)
    up_logistic = sigmoid(pre_up)
    summed_half = (edge_ref[...].astype(F32) + pre_up * up_logistic).astype(BF16)
    pre_first = contract(summed_half, first_ref[...], 1, 0)
    first_logistic = sigmoid(pre_first)
    first_rows = (pre_first * first_logistic).astype(BF16)
    pre_second = contract(first_rows, second_ref[...], 1, 0)
    logistic = sigmoid(pre_second)
    row_ids = step * tile + lax.broadcasted_iota(jnp.int32, (tile, 1), 0)
    live = jnp.where(row_ids < count_ref[0, 0], HALF, 0.0)
    back_top = cotangent_ref[...].astype(F32) * live
    back_second = (back_top * (logistic * (1.0 + pre_second * (1.0 - logistic)))).astype(BF16)
    slope = first_logistic * (1.0 + pre_first * (1.0 - first_logistic))
    back_first = (contract(back_second, second_turned_ref[...], 1, 0) * slope).astype(BF16)
    back_summed = back_top + contract(back_first, first_turned_ref[...], 1, 0)
    summed_ref[...] = back_summed.astype(BF16)
    slope = up_logistic * (1.0 + pre_up * (1.0 - up_logistic))
    back_up = (back_summed * slope).astype(BF16)
    back_mixed = contract(back_up, up_ref[...], 1, 1).T.astype(BF16)
    back_ref[...] = stack(contract(bilinear_ref[...], back_mixed, 1, 0).astype(BF16), lanes)
    total[:wide] += contract(summed_half, back_first, 0, 0)
    total[wide : 2 * wide] += contract(first_rows, back_second, 0, 0)
    total[2 * wide : 2 * wide + narrow] += contract(mixed, back_up, 1, 0)
    total[2 * wide + narrow :, :narrow] += contract(gathered, back_mixed, 1, 1)

    @pl.when(step == pl.num_programs(0) - 1)
    def _():
        grads_ref[...] = total[...].astype(BF16)


def backward_kernel(count, shards_ref, own_ref, sibling_ref, *refs):
    fetched, coefs, ends = refs[:count], refs[count : 2 * count], refs[2 * count : 2 * count + 2]
    parts, back_coefs = refs[2 * count + 2 : 3 * count + 2], refs[3 * count + 2 :]
    narrow = fetched[0].shape[1]
    groups = own_ref.shape[0] // narrow
    lanes = own_ref.shape[1]
    for s in range(count):
        shard = shards_ref[s]
        part = None
        for i, back_ref in enumerate((own_ref, sibling_ref)):
            high, lane_hot = split_index(ends[i][1, shard], lanes)
            message = pick_rows(back_ref[...], high, lane_hot, narrow)
            back_coefs[s][i] = (message * fetched[s][i].astype(F32)).astype(BF16)
            high, lane_hot = split_index(ends[i][0, shard], lanes)
            placed = place_rows(message * coefs[s][i].astype(F32), high, lane_hot, groups)
            part = placed if part is None else part + placed
        parts[s][...] = part.astype(BF16)


def basis_kernel(shards_ref, *refs):
    back_coefs, basis, grad_ref = refs[:-3], refs[-3:-1], refs[-1]
    slots = back_coefs[0].shape[2]
    grad = jnp.zeros(grad_ref.shape, F32)
    for s, ref in enumerate(back_coefs):
        at = pl.ds(pl.multiple_of(shards_ref[s] * slots, slots), slots)
        for i in range(2):
            grad += contract(ref[i], basis[i][:, at], 1, 1)
    grad_ref[...] = grad


def final_kernel(count, *refs):
    parts = refs[:count]
    slope_ref, edge_ref, summed_ref, weight_ref, basis_ref, edge_grad_ref, grads_ref, total = refs[
        count:
    ]
    step = pl.program_id(0)
    narrow = weight_ref.shape[0]
    basis_width = basis_ref.shape[1]

    @pl.when(step == 0)
    def _():
        total[...] = jnp.zeros_like(total)

    back_down = parts[0][...].astype(F32)
    for part in parts[1:]:
        back_down += part[...].astype(F32)
    back_pre = unstack((back_down * slope_ref[...]).astype(BF16), narrow)
    total[:narrow] += contract(back_pre, edge_ref[...], 1, 0)
    edge_grad_ref[...] = (
        summed_ref[...].astype(F32) + contract(back_pre, weight_ref[...], 0, 0)
    ).astype(BF16)

    @pl.when(step == pl.num_programs(0) - 1)
    def _():
        total[narrow : narrow + basis_width, :narrow] = basis_ref[...].T
        grads_ref[...] = total[...].astype(BF16)


def scale_kernel(scale, source_ref, *outs):
    row = 0
    for out in outs:
        rows, columns = out.shape
        out[...] = source_ref[row : row + rows, :columns].astype(F32) * scale
        row += rows


def call(kernel, grid, in_specs, out_specs, out_shape, flops, transcendentals=0, scratch=(), aliases=None, grant=8, fused=False):
    def run(*operands):
        size = sum(x.size * x.dtype.itemsize for x in operands)
        size += sum(math.prod(x.shape) * x.dtype.itemsize for x in out_shape)
        return pl.pallas_call(
            kernel,
            grid=grid,
            in_specs=in_specs,
            out_specs=out_specs,
            out_shape=out_shape,
            scratch_shapes=scratch,
            input_output_aliases=aliases or {},
            compiler_params=pltpu.CompilerParams(
                vmem_limit_bytes=grant * MIB, fuse_transposed_lhs_in_matmul=fused
            ),
            cost_estimate=pl.CostEstimate(
                flops=flops, bytes_accessed=size, transcendentals=transcendentals
            ),
        )(*operands)

    return run


def whole(*shape):
    return pl.BlockSpec(shape, lambda *_: (0,) * len(shape))


SMEM = pl.BlockSpec(memory_space=pltpu.SMEM)


def in_hbm(array):
    return pltpu.with_memory_space_constraint(array, pltpu.HBM)


def shape(dims, dtype):
    return jax.ShapeDtypeStruct(dims, dtype)


def turned(count, size, stride, turn):
    pairs = []
    for g in range(count):
        place = g // stride % size
        pairs.append((g, g + ((place + turn) % size - place) * stride))
    return pairs


class Line:
    cores = 2

    def __init__(self):
        self.size = lax.axis_size("graph")
        self.chips = math.gcd(self.size // self.cores, 4)
        self.span = self.chips * self.cores
        self.groups = self.size // self.span
        me = lax.axis_index("graph")
        self.core = me % self.cores
        self.chip = me // self.cores % self.chips
        self.group = me // self.span

    def send(self, array, moves):
        pairs = [
            (base + one * self.cores + core, base + other * self.cores + core)
            for base in range(0, self.size, self.span)
            for one, other in moves
            for core in range(self.cores)
        ]
        return lax.ppermute(array, "graph", pairs)

    def trade(self, array, bits):
        return self.send(array, [(chip, chip ^ bits) for chip in range(self.chips)])

    def pair(self, array):
        return lax.ppermute(array, "graph", [(g, g ^ 2) for g in range(self.size)])

    def swap(self, array):
        return lax.ppermute(array, "graph", [(g, g ^ 1) for g in range(self.size)])

    def next_group(self, array):
        return lax.ppermute(array, "graph", turned(self.size, self.groups, self.span, -1))

    def last_group(self, array):
        return lax.ppermute(array, "graph", turned(self.size, self.groups, self.span, 1))

    def shard(self, turn, bits):
        group = (self.group + turn) % self.groups
        shard = group * self.span + (self.chip ^ bits) * self.cores + self.core
        return shard.astype(jnp.int32).reshape(1)


def add(*arrays):
    return sum(a.astype(F32) for a in arrays).astype(BF16)


def after(arrays, *others):
    return lax.optimization_barrier((tuple(arrays), others))[0]


def dp_pairs(line, step):
    bits = lax.axis_size("dp").bit_length() - 1
    pairs = []
    for dp in range(lax.axis_size("dp")):
        for g in range(line.size):
            bit = (step + g % line.cores) % bits
            pairs.append((dp * line.size + g, (dp ^ (1 << bit)) * line.size + g))
    return pairs


def dp_place(line, step):
    bits = lax.axis_size("dp").bit_length() - 1
    return lax.axis_index("dp") >> ((step + line.core) % bits) & 1


def halves(array, place):
    rows = array.shape[0] // 2
    first = place == 0
    return (
        jnp.where(first, array[:rows], array[rows:]),
        jnp.where(first, array[rows:], array[:rows]),
    )


def joined(mine, other, place):
    return jnp.where(
        place == 0, jnp.concatenate([mine, other]), jnp.concatenate([other, mine])
    )


def across_dp(array, line, step):
    mine, away = halves(array, dp_place(line, step))
    return [mine, lax.ppermute(away, ("dp", "graph"), dp_pairs(line, step))]


def across_chips(array, line):
    mine, away = halves(array, line.chip % 2)
    return [mine, line.pair(away)]


def across_cores(array, line):
    mine, away = halves(array, line.core)
    return [mine, line.swap(away)]


def summed_graph(array, line, bits):
    for bit in bits:
        pairs = [(g, g ^ (1 << bit)) for g in range(line.size)]
        array = add(array, lax.ppermute(array, "graph", pairs))
    return array


def local(
    edge_state,
    cotangent,
    edge_count,
    triplet_basis,
    triplet_in,
    triplet_out,
    down_weight,
    basis_weight,
    bilinear_weight,
    up_weight,
    first_weight,
    second_weight,
):
    edge_rows = edge_state[0]
    row_count, wide = edge_rows.shape
    line = Line()
    shards, chips = line.size, line.chips
    narrow = down_weight.shape[1]
    down_weight = down_weight.T
    basis = triplet_basis[0]
    basis_width, tri_rows = basis.shape
    slots = tri_rows // shards
    lanes = math.gcd(row_count, 256)
    stacked = narrow * (row_count // lanes)
    tile = math.gcd(row_count, 512)
    tiles = row_count // tile
    row_spec = pl.BlockSpec((tile, wide), lambda i: (i, 0))
    stack_spec = pl.BlockSpec((narrow * (tile // lanes), lanes), lambda i: (i, 0))
    rows_spec = whole(stacked, lanes)

    ends = jnp.stack([triplet_in.reshape(shards, 1, slots), triplet_out.reshape(shards, 1, slots)])
    triplet_specs = (
        [whole(2, shards, 1, slots)] * 2
        + [whole(basis_width, tri_rows)] * 2
        + [whole(basis_width, narrow)]
    )
    block_flops = 8 * slots * row_count * narrow

    down_rows, down_slope = call(
        down_kernel,
        (tiles,),
        [row_spec, whole(narrow, wide)],
        [stack_spec] * 2,
        [shape((stacked, lanes), BF16), shape((stacked, lanes), F32)],
        2 * row_count * wide * narrow,
        row_count * narrow,
    )(in_hbm(edge_rows), in_hbm(down_weight))

    slot_spec = whole(2, narrow, slots)
    slot_shape = pltpu.HBM((2, narrow, slots), BF16)

    ends, leaving = after((ends, basis), down_rows)
    ends_sibling = line.swap(ends)
    basis_sibling = line.swap(leaving)
    triplets = (ends, ends_sibling, basis, basis_sibling, basis_weight)

    def forward(turn, bits, rows, totals):
        total_shape = shape((stacked, lanes), F32)
        final = line.groups == 1 and bits == chips - 1
        out = call(
            forward_kernel,
            (),
            [SMEM, rows_spec] + triplet_specs + [rows_spec] * len(totals),
            [rows_spec] * 2 + [slot_spec] * 2,
            [pltpu.HBM((stacked, lanes), F32) if final else total_shape, total_shape]
            + [slot_shape] * 2,
            block_flops,
            aliases={7 + i: i for i in range(len(totals)) if i == 1 or not final},
            grant=FORWARD_GRANT,
        )(line.shard(turn, bits), rows, *triplets, *totals)
        return tuple(out[:2]), tuple(out[2:])

    def forward_line(turn, rows, totals, *others):
        arriving = [line.trade(rows, bits) for bits in range(1, chips)]
        totals, got = forward(turn, 0, rows, totals)
        kept = [got]
        for bits in range(1, chips):
            (rows,) = after((arriving[bits - 1],), *totals, *others)
            totals, got = forward(turn, bits, rows, totals)
            kept.append(got)
        return totals, kept

    first_turned, second_turned = after((first_weight, second_weight), down_rows)
    first_turned, second_turned = first_turned.T, second_turned.T
    totals, kept = forward_line(0, down_rows, (), first_turned, second_turned)
    if line.groups > 1:

        def forward_turn(carry, turn):
            rows, totals = carry
            rows = line.next_group(rows)
            totals, got = forward_line(turn, rows, totals)
            return (rows, totals), got

        (_, totals), more_kept = lax.scan(
            forward_turn, (down_rows, totals), jnp.arange(1, line.groups)
        )

    grad_rows = 2 * wide + 2 * narrow
    back_summed, back_gathered, dense_grads = call(
        dense_kernel,
        (tiles,),
        [
            SMEM,
            row_spec,
            row_spec,
            stack_spec,
            stack_spec,
            whole(narrow, narrow),
            whole(narrow, wide),
            whole(wide, wide),
            whole(wide, wide),
            whole(wide, wide),
            whole(wide, wide),
        ],
        [row_spec, stack_spec, whole(grad_rows, wide)],
        [
            pltpu.HBM((row_count, wide), BF16),
            shape((stacked, lanes), BF16),
            shape((grad_rows, wide), BF16),
        ],
        12 * row_count * wide * wide + 6 * row_count * wide * narrow,
        3 * row_count * wide,
        scratch=[pltpu.VMEM((grad_rows, wide), F32)],
        grant=DENSE_GRANT,
        fused=True,
    )(
        edge_count,
        in_hbm(edge_rows),
        in_hbm(cotangent[0]),
        in_hbm(totals[0]) if line.groups == 1 else totals[0],
        line.swap(totals[1]),
        bilinear_weight,
        up_weight,
        in_hbm(first_weight),
        first_turned,
        in_hbm(second_weight),
        second_turned,
    )
    back_sibling = line.swap(back_gathered)

    def backward(turn, bits, kept, others=()):
        count = len(bits)
        (back,) = after((back_gathered,), *others)
        out = call(
            functools.partial(backward_kernel, count),
            (),
            [SMEM] + [rows_spec] * 2 + [slot_spec] * (2 * count) + triplet_specs[:2],
            [rows_spec] * count + [slot_spec] * count,
            [shape((stacked, lanes), BF16)] * count + [shape((2, narrow, slots), BF16)] * count,
            count * block_flops,
            grant=BACKWARD_GRANT,
        )(
            jnp.concatenate([line.shard(turn, one) for one in bits]),
            back,
            back_sibling,
            *[kept[one][0] for one in bits],
            *[kept[one][1] for one in bits],
            ends,
            ends_sibling,
        )
        return out[:count], out[count:]

    dp_steps = lax.axis_size("dp").bit_length() - 1
    graph_bits = line.size.bit_length() - 1

    def backward_line(turn, kept, pieces=None):
        parts, others = [], ()
        last_coefs = near_coefs = ()
        if chips == 4:
            (last,), last_coefs = backward(turn, (3,), kept)
            passed = line.send(last, [(0, 1), (3, 2)])
            middle = line.send(last, [(1, 2), (2, 1)])
            others = (last,)
        if pieces is not None:
            pieces = add(*after(pieces, *others))
            others = (*others, pieces)
        if chips == 4:
            (near, far), near_coefs = backward(turn, (1, 2), kept, others)
            (passed,) = after((passed,), far)
            far = add(far, passed)
            (middle,) = after((middle,), far)
            (far,) = after((far,), middle)
            others = (far,)
            parts = [middle, line.trade(far, 2), line.trade(near, 1)]
        elif chips == 2:
            (near,), near_coefs = backward(turn, (1,), kept, others)
            parts = [line.trade(near, 1)]
        (own,), own_coefs = backward(turn, (0,), kept, others)
        if pieces is not None:
            for step in range(dp_steps):
                pieces = add(*across_dp(pieces, line, step))
            own_coefs = after(own_coefs, pieces)
        back_coefs = [*own_coefs, *near_coefs, *last_coefs]
        basis_grad = call(
            basis_kernel,
            (),
            [SMEM] + [slot_spec] * chips + triplet_specs[2:4],
            [whole(narrow, basis_width)],
            [shape((narrow, basis_width), F32)],
            4 * chips * slots * narrow * basis_width,
        )(
            jnp.concatenate([line.shard(turn, bits) for bits in range(chips)]),
            *back_coefs,
            basis,
            basis_sibling,
        )[0]
        return [own] + parts, basis_grad, pieces

    back_parts, basis_grad, dense_grads = backward_line(0, kept, across_cores(dense_grads, line))
    if line.groups > 1:

        def backward_turn(carry, one):
            traveling, basis_grad = carry
            turn, got = one
            parts, more, _ = backward_line(turn, got)
            return (line.last_group(add(traveling, *parts)), basis_grad + more), None

        (traveling, basis_grad), _ = lax.scan(
            backward_turn,
            (jnp.zeros((stacked, lanes), BF16), basis_grad),
            (jnp.arange(1, line.groups), more_kept),
            reverse=True,
        )
        back_parts = back_parts + [traveling]

    small_rows = narrow + basis_width
    edge_grad, small_grads = call(
        functools.partial(final_kernel, len(back_parts)),
        (tiles,),
        [stack_spec] * len(back_parts)
        + [stack_spec, row_spec, row_spec, whole(narrow, wide), whole(narrow, basis_width)],
        [row_spec, whole(small_rows, wide)],
        [shape((row_count, wide), BF16), shape((small_rows, wide), BF16)],
        4 * row_count * wide * narrow,
        scratch=[pltpu.VMEM((small_rows, wide), F32)],
        grant=FINAL_GRANT,
    )(
        *back_parts,
        down_slope,
        edge_rows,
        back_summed,
        down_weight,
        basis_grad,
    )

    small_grads = add(*across_cores(small_grads, line))
    if chips > 1:
        dense_grads = add(*across_chips(dense_grads, line))
    for bit in range(2, graph_bits):
        rows = dense_grads.shape[0]
        both = summed_graph(jnp.concatenate([dense_grads, small_grads]), line, (bit,))
        dense_grads, small_grads = both[:rows], both[rows:]

    def shared(swap, place):
        other = swap(jnp.concatenate([dense_grads, small_grads]))
        rows = dense_grads.shape[0]
        return joined(dense_grads, other[:rows], place), add(small_grads, other[rows:])

    if chips > 1:
        dense_grads, small_grads = shared(line.pair, line.chip % 2)
    for step in reversed(range(dp_steps)):
        pairs = dp_pairs(line, step)
        dense_grads, small_grads = shared(
            lambda array: lax.ppermute(array, ("dp", "graph"), pairs), dp_place(line, step)
        )
    rows = dense_grads.shape[0]
    other = line.swap(jnp.concatenate([dense_grads, small_grads]))
    dense_grads = joined(dense_grads, other[:rows], line.core)
    small_grads = joined(small_grads, other[rows:], line.core)
    scale = 1.0 / math.sqrt(lax.axis_size("dp") * shards * row_count)

    def scaled(source, *dims):
        return call(
            functools.partial(scale_kernel, scale),
            (),
            [whole(*source.shape)],
            [whole(*d) for d in dims],
            [shape(d, F32) for d in dims],
            source.size,
        )(source)

    first_grad, second_grad, up_grad, bilinear_grad = scaled(
        dense_grads, (wide, wide), (wide, wide), (narrow, wide), (narrow, narrow)
    )
    down_grad, basis_grad = scaled(small_grads, (narrow, wide), (basis_width, narrow))
    return (
        edge_grad[None],
        down_grad.T,
        basis_grad,
        bilinear_grad,
        up_grad,
        first_grad,
        second_grad,
    )


def solution(mesh):
    in_specs = (
        P("dp", "graph", None),
        P("dp", "graph", None),
        P("dp", "graph"),
        P("dp", None, "graph"),
        P("dp", "graph"),
        P("dp", "graph"),
        P(),
        P(),
        P(),
        P(),
        P(),
        P(),
    )
    out_specs = (P("dp", "graph", None), P(), P(), P(), P(), P(), P())
    return jax.shard_map(local, mesh=mesh, in_specs=in_specs, out_specs=out_specs, check_vma=False)
```

```python
import functools
import math

import jax
import jax.numpy as jnp
from jax import lax
from jax.experimental import pallas as pl
from jax.experimental.pallas import tpu as pltpu
from jax.sharding import PartitionSpec as P

HALF = 0.7071067811865476
F32 = jnp.float32
BF16 = jnp.bfloat16
MIB = 1024 * 1024
FORWARD_GRANT = 10
BACKWARD_GRANT = 10
DENSE_GRANT = 18
FINAL_GRANT = 12


def contract(left, right, left_dim, right_dim):
    return lax.dot_general(
        left, right, (((left_dim,), (right_dim,)), ((), ())), preferred_element_type=F32
    )


def sigmoid(value):
    return 0.5 + 0.5 * jnp.tanh(0.5 * value)


def split_index(index_row, lanes):
    slots = index_row.shape[1]
    low = jnp.bitwise_and(index_row, lanes - 1)
    high = jnp.right_shift(index_row, lanes.bit_length() - 1)
    lane_ids = lax.broadcasted_iota(jnp.int32, (lanes, slots), 0)
    return high, jnp.where(lane_ids == low, 1.0, 0.0).astype(BF16)


def stack(rows, lanes):
    groups = rows.shape[1] // lanes
    return jnp.concatenate([rows[:, g * lanes : (g + 1) * lanes] for g in range(groups)], axis=0)


def unstack(rows, narrow):
    groups = rows.shape[0] // narrow
    return jnp.concatenate([rows[g * narrow : (g + 1) * narrow] for g in range(groups)], axis=1)


def pick_rows(stacked, high, lane_hot, narrow):
    groups = stacked.shape[0] // narrow
    every = contract(stacked, lane_hot, 1, 0)
    picked = jnp.where(high == 0, every[:narrow], 0.0)
    for g in range(1, groups):
        picked = jnp.where(high == g, every[g * narrow : (g + 1) * narrow], picked)
    return picked


def place_rows(values, high, lane_hot, groups):
    zero = jnp.zeros((), values.dtype)
    spread = jnp.concatenate([jnp.where(high == g, values, zero) for g in range(groups)], axis=0)
    return contract(spread.astype(BF16), lane_hot, 1, 1)


def down_kernel(edge_ref, weight_ref, rows_ref, slope_ref):
    lanes = rows_ref.shape[1]
    pre = contract(edge_ref[...], weight_ref[...], 1, 1).T
    logistic = sigmoid(pre)
    rows_ref[...] = stack((pre * logistic).astype(BF16), lanes)
    slope_ref[...] = stack(logistic * (1.0 + pre * (1.0 - logistic)), lanes)


def forward_kernel(shard_ref, rows_ref, *refs):
    rows = rows_ref[...]
    ends, basis, weight_ref = refs[:2], refs[2:4], refs[4]
    totals, fetched_ref, coef_ref = refs[-4:-2], refs[-2], refs[-1]
    shard = shard_ref[0]
    narrow = weight_ref.shape[1]
    groups = totals[0].shape[0] // narrow
    lanes = totals[0].shape[1]
    slots = ends[0].shape[3]
    at = pl.ds(pl.multiple_of(shard * slots, slots), slots)
    for i in range(2):
        high, lane_hot = split_index(ends[i][0, shard], lanes)
        fetched = pick_rows(rows, high, lane_hot, narrow)
        fetched_ref[i] = fetched.astype(BF16)
        coef = contract(weight_ref[...], basis[i][:, at], 0, 0)
        coef_ref[i] = coef.astype(BF16)
        high, lane_hot = split_index(ends[i][1, shard], lanes)
        placed = place_rows(coef * fetched, high, lane_hot, groups)
        if len(refs) == 11:
            placed += refs[5 + i][...]
        totals[i][...] = placed


def dense_kernel(
    count_ref,
    edge_ref,
    cotangent_ref,
    gathered_ref,
    more_ref,
    bilinear_ref,
    up_ref,
    first_ref,
    first_turned_ref,
    second_ref,
    second_turned_ref,
    summed_ref,
    back_ref,
    grads_ref,
    total,
):
    step = pl.program_id(0)
    tile, wide = edge_ref.shape
    narrow = bilinear_ref.shape[0]
    lanes = gathered_ref.shape[1]

    @pl.when(step == 0)
    def _():
        total[...] = jnp.zeros_like(total)

    gathered = unstack((gathered_ref[...] + more_ref[...]).astype(BF16), narrow)
    mixed = contract(bilinear_ref[...], gathered, 0, 0).astype(BF16)
    pre_up = contract(mixed, up_ref[...], 0, 0)
    up_logistic = sigmoid(pre_up)
    summed_half = (edge_ref[...].astype(F32) + pre_up * up_logistic).astype(BF16)
    pre_first = contract(summed_half, first_ref[...], 1, 0)
    first_logistic = sigmoid(pre_first)
    first_rows = (pre_first * first_logistic).astype(BF16)
    pre_second = contract(first_rows, second_ref[...], 1, 0)
    logistic = sigmoid(pre_second)
    row_ids = step * tile + lax.broadcasted_iota(jnp.int32, (tile, 1), 0)
    live = jnp.where(row_ids < count_ref[0, 0], HALF, 0.0)
    back_top = cotangent_ref[...].astype(F32) * live
    back_second = (back_top * (logistic * (1.0 + pre_second * (1.0 - logistic)))).astype(BF16)
    slope = first_logistic * (1.0 + pre_first * (1.0 - first_logistic))
    back_first = (contract(back_second, second_turned_ref[...], 1, 0) * slope).astype(BF16)
    back_summed = back_top + contract(back_first, first_turned_ref[...], 1, 0)
    summed_ref[...] = back_summed.astype(BF16)
    slope = up_logistic * (1.0 + pre_up * (1.0 - up_logistic))
    back_up = (back_summed * slope).astype(BF16)
    back_mixed = contract(back_up, up_ref[...], 1, 1).T.astype(BF16)
    back_ref[...] = stack(contract(bilinear_ref[...], back_mixed, 1, 0).astype(BF16), lanes)
    total[:wide] += contract(summed_half, back_first, 0, 0)
    total[wide : 2 * wide] += contract(first_rows, back_second, 0, 0)
    total[2 * wide : 2 * wide + narrow] += contract(mixed, back_up, 1, 0)
    total[2 * wide + narrow :, :narrow] += contract(gathered, back_mixed, 1, 1)

    @pl.when(step == pl.num_programs(0) - 1)
    def _():
        grads_ref[...] = total[...].astype(BF16)


def backward_kernel(count, shards_ref, own_ref, sibling_ref, *refs):
    fetched, coefs, ends = refs[:count], refs[count : 2 * count], refs[2 * count : 2 * count + 2]
    parts, back_coefs = refs[2 * count + 2 : 3 * count + 2], refs[3 * count + 2 :]
    narrow = fetched[0].shape[1]
    groups = own_ref.shape[0] // narrow
    lanes = own_ref.shape[1]
    for s in range(count):
        shard = shards_ref[s]
        part = None
        for i, back_ref in enumerate((own_ref, sibling_ref)):
            high, lane_hot = split_index(ends[i][1, shard], lanes)
            message = pick_rows(back_ref[...], high, lane_hot, narrow)
            back_coefs[s][i] = (message * fetched[s][i].astype(F32)).astype(BF16)
            high, lane_hot = split_index(ends[i][0, shard], lanes)
            placed = place_rows(message * coefs[s][i].astype(F32), high, lane_hot, groups)
            part = placed if part is None else part + placed
        parts[s][...] = part.astype(BF16)


def basis_kernel(shards_ref, *refs):
    back_coefs, basis, grad_ref = refs[:-3], refs[-3:-1], refs[-1]
    slots = back_coefs[0].shape[2]
    grad = jnp.zeros(grad_ref.shape, F32)
    for s, ref in enumerate(back_coefs):
        at = pl.ds(pl.multiple_of(shards_ref[s] * slots, slots), slots)
        for i in range(2):
            grad += contract(ref[i], basis[i][:, at], 1, 1)
    grad_ref[...] = grad


def final_kernel(count, *refs):
    parts = refs[:count]
    slope_ref, edge_ref, summed_ref, weight_ref, basis_ref, edge_grad_ref, grads_ref, total = refs[
        count:
    ]
    step = pl.program_id(0)
    narrow = weight_ref.shape[0]
    basis_width = basis_ref.shape[1]

    @pl.when(step == 0)
    def _():
        total[...] = jnp.zeros_like(total)

    back_down = parts[0][...].astype(F32)
    for part in parts[1:]:
        back_down += part[...].astype(F32)
    back_pre = unstack((back_down * slope_ref[...]).astype(BF16), narrow)
    total[:narrow] += contract(back_pre, edge_ref[...], 1, 0)
    edge_grad_ref[...] = (
        summed_ref[...].astype(F32) + contract(back_pre, weight_ref[...], 0, 0)
    ).astype(BF16)

    @pl.when(step == pl.num_programs(0) - 1)
    def _():
        total[narrow : narrow + basis_width, :narrow] = basis_ref[...].T
        grads_ref[...] = total[...].astype(BF16)


def scale_kernel(scale, source_ref, *outs):
    row = 0
    for out in outs:
        rows, columns = out.shape
        out[...] = source_ref[row : row + rows, :columns].astype(F32) * scale
        row += rows


def call(kernel, grid, in_specs, out_specs, out_shape, flops, transcendentals=0, scratch=(), aliases=None, grant=8):
    def run(*operands):
        size = sum(x.size * x.dtype.itemsize for x in operands)
        size += sum(math.prod(x.shape) * x.dtype.itemsize for x in out_shape)
        return pl.pallas_call(
            kernel,
            grid=grid,
            in_specs=in_specs,
            out_specs=out_specs,
            out_shape=out_shape,
            scratch_shapes=scratch,
            input_output_aliases=aliases or {},
            compiler_params=pltpu.CompilerParams(vmem_limit_bytes=grant * MIB),
            cost_estimate=pl.CostEstimate(
                flops=flops, bytes_accessed=size, transcendentals=transcendentals
            ),
        )(*operands)

    return run


def whole(*shape):
    return pl.BlockSpec(shape, lambda *_: (0,) * len(shape))


SMEM = pl.BlockSpec(memory_space=pltpu.SMEM)


def in_hbm(array):
    return pltpu.with_memory_space_constraint(array, pltpu.HBM)


def shape(dims, dtype):
    return jax.ShapeDtypeStruct(dims, dtype)


def turned(count, size, stride, turn):
    pairs = []
    for g in range(count):
        place = g // stride % size
        pairs.append((g, g + ((place + turn) % size - place) * stride))
    return pairs


class Line:
    cores = 2

    def __init__(self):
        self.size = lax.axis_size("graph")
        self.chips = math.gcd(self.size // self.cores, 4)
        self.span = self.chips * self.cores
        self.groups = self.size // self.span
        me = lax.axis_index("graph")
        self.core = me % self.cores
        self.chip = me // self.cores % self.chips
        self.group = me // self.span

    def send(self, array, moves):
        pairs = [
            (base + one * self.cores + core, base + other * self.cores + core)
            for base in range(0, self.size, self.span)
            for one, other in moves
            for core in range(self.cores)
        ]
        return lax.ppermute(array, "graph", pairs)

    def trade(self, array, bits):
        return self.send(array, [(chip, chip ^ bits) for chip in range(self.chips)])

    def pair(self, array):
        return lax.ppermute(array, "graph", [(g, g ^ 2) for g in range(self.size)])

    def swap(self, array):
        return lax.ppermute(array, "graph", [(g, g ^ 1) for g in range(self.size)])

    def next_group(self, array):
        return lax.ppermute(array, "graph", turned(self.size, self.groups, self.span, -1))

    def last_group(self, array):
        return lax.ppermute(array, "graph", turned(self.size, self.groups, self.span, 1))

    def shard(self, turn, bits):
        group = (self.group + turn) % self.groups
        shard = group * self.span + (self.chip ^ bits) * self.cores + self.core
        return shard.astype(jnp.int32).reshape(1)


def add(*arrays):
    return sum(a.astype(F32) for a in arrays).astype(BF16)


def after(arrays, *others):
    return lax.optimization_barrier((tuple(arrays), others))[0]


def halves(array, place):
    rows = array.shape[0] // 2
    first = place == 0
    return (
        jnp.where(first, array[:rows], array[rows:]),
        jnp.where(first, array[rows:], array[:rows]),
    )


def joined(mine, other, place):
    return jnp.where(
        place == 0, jnp.concatenate([mine, other]), jnp.concatenate([other, mine])
    )


def piece_of(array, size, place):
    rows = array.shape[0] // size
    return lax.dynamic_slice_in_dim(array, place * rows, rows, 0)


def dp_pieces(array):
    size, me = lax.axis_size("dp"), lax.axis_index("dp")
    arrived = [piece_of(array, size, me)]
    for turn in range(1, size):
        away = piece_of(array, size, (me + turn) % size)
        arrived.append(lax.ppermute(away, "dp", turned(size, size, 1, turn)))
    return arrived


def dp_joined(piece):
    size, me = lax.axis_size("dp"), lax.axis_index("dp")
    rows = piece.shape[0]
    out = jnp.zeros((size * rows, piece.shape[1]), piece.dtype)
    out = lax.dynamic_update_slice_in_dim(out, piece, me * rows, 0)
    for turn in range(1, size):
        other = lax.ppermute(piece, "dp", turned(size, size, 1, turn))
        out = lax.dynamic_update_slice_in_dim(out, other, (me - turn) % size * rows, 0)
    return out


def across_chips(array, line):
    mine, away = halves(array, line.chip % 2)
    return [mine, line.pair(away)]


def across_cores(array, line):
    mine, away = halves(array, line.core)
    return [mine, line.swap(away)]


def summed_dp(array):
    size = lax.axis_size("dp")
    for bit in range(size.bit_length() - 1):
        array = add(array, lax.ppermute(array, "dp", [(g, g ^ (1 << bit)) for g in range(size)]))
    return array


def summed_graph(array, line, bits):
    for bit in bits:
        pairs = [(g, g ^ (1 << bit)) for g in range(line.size)]
        array = add(array, lax.ppermute(array, "graph", pairs))
    return array


def local(
    edge_state,
    cotangent,
    edge_count,
    triplet_basis,
    triplet_in,
    triplet_out,
    down_weight,
    basis_weight,
    bilinear_weight,
    up_weight,
    first_weight,
    second_weight,
):
    edge_rows = edge_state[0]
    row_count, wide = edge_rows.shape
    line = Line()
    shards, chips = line.size, line.chips
    narrow = down_weight.shape[1]
    down_weight = down_weight.T
    basis = triplet_basis[0]
    basis_width, tri_rows = basis.shape
    slots = tri_rows // shards
    lanes = math.gcd(row_count, 256)
    stacked = narrow * (row_count // lanes)
    tile = math.gcd(row_count, 512)
    tiles = row_count // tile
    row_spec = pl.BlockSpec((tile, wide), lambda i: (i, 0))
    stack_spec = pl.BlockSpec((narrow * (tile // lanes), lanes), lambda i: (i, 0))
    rows_spec = whole(stacked, lanes)

    ends = jnp.stack([triplet_in.reshape(shards, 1, slots), triplet_out.reshape(shards, 1, slots)])
    triplet_specs = (
        [whole(2, shards, 1, slots)] * 2
        + [whole(basis_width, tri_rows)] * 2
        + [whole(basis_width, narrow)]
    )
    block_flops = 8 * slots * row_count * narrow

    down_rows, down_slope = call(
        down_kernel,
        (tiles,),
        [row_spec, whole(narrow, wide)],
        [stack_spec] * 2,
        [shape((stacked, lanes), BF16), shape((stacked, lanes), F32)],
        2 * row_count * wide * narrow,
        row_count * narrow,
    )(in_hbm(edge_rows), in_hbm(down_weight))

    slot_spec = whole(2, narrow, slots)
    slot_shape = pltpu.HBM((2, narrow, slots), BF16)

    ends, leaving = after((ends, basis), down_rows)
    ends_sibling = line.swap(ends)
    basis_sibling = line.swap(leaving)
    triplets = (ends, ends_sibling, basis, basis_sibling, basis_weight)

    def forward(turn, bits, rows, totals):
        total_shape = shape((stacked, lanes), F32)
        final = line.groups == 1 and bits == chips - 1
        out = call(
            forward_kernel,
            (),
            [SMEM, rows_spec] + triplet_specs + [rows_spec] * len(totals),
            [rows_spec] * 2 + [slot_spec] * 2,
            [pltpu.HBM((stacked, lanes), F32) if final else total_shape, total_shape]
            + [slot_shape] * 2,
            block_flops,
            aliases={7 + i: i for i in range(len(totals)) if i == 1 or not final},
            grant=FORWARD_GRANT,
        )(line.shard(turn, bits), rows, *triplets, *totals)
        return tuple(out[:2]), tuple(out[2:])

    def forward_line(turn, rows, totals, *others):
        arriving = [line.trade(rows, bits) for bits in range(1, chips)]
        totals, got = forward(turn, 0, rows, totals)
        kept = [got]
        for bits in range(1, chips):
            (rows,) = after((arriving[bits - 1],), *totals, *others)
            totals, got = forward(turn, bits, rows, totals)
            kept.append(got)
        return totals, kept

    first_turned, second_turned = after((first_weight, second_weight), down_rows)
    first_turned, second_turned = first_turned.T, second_turned.T
    totals, kept = forward_line(0, down_rows, (), first_turned, second_turned)
    if line.groups > 1:

        def forward_turn(carry, turn):
            rows, totals = carry
            rows = line.next_group(rows)
            totals, got = forward_line(turn, rows, totals)
            return (rows, totals), got

        (_, totals), more_kept = lax.scan(
            forward_turn, (down_rows, totals), jnp.arange(1, line.groups)
        )

    grad_rows = 2 * wide + 2 * narrow
    back_summed, back_gathered, dense_grads = call(
        dense_kernel,
        (tiles,),
        [
            SMEM,
            row_spec,
            row_spec,
            stack_spec,
            stack_spec,
            whole(narrow, narrow),
            whole(narrow, wide),
            whole(wide, wide),
            whole(wide, wide),
            whole(wide, wide),
            whole(wide, wide),
        ],
        [row_spec, stack_spec, whole(grad_rows, wide)],
        [
            pltpu.HBM((row_count, wide), BF16),
            shape((stacked, lanes), BF16),
            shape((grad_rows, wide), BF16),
        ],
        12 * row_count * wide * wide + 6 * row_count * wide * narrow,
        3 * row_count * wide,
        scratch=[pltpu.VMEM((grad_rows, wide), F32)],
        grant=DENSE_GRANT,
    )(
        edge_count,
        in_hbm(edge_rows),
        in_hbm(cotangent[0]),
        in_hbm(totals[0]) if line.groups == 1 else totals[0],
        line.swap(totals[1]),
        bilinear_weight,
        up_weight,
        in_hbm(first_weight),
        first_turned,
        in_hbm(second_weight),
        second_turned,
    )
    back_sibling = line.swap(back_gathered)

    def backward(turn, bits, kept, others=()):
        count = len(bits)
        (back,) = after((back_gathered,), *others)
        out = call(
            functools.partial(backward_kernel, count),
            (),
            [SMEM] + [rows_spec] * 2 + [slot_spec] * (2 * count) + triplet_specs[:2],
            [rows_spec] * count + [slot_spec] * count,
            [shape((stacked, lanes), BF16)] * count + [shape((2, narrow, slots), BF16)] * count,
            count * block_flops,
            grant=BACKWARD_GRANT,
        )(
            jnp.concatenate([line.shard(turn, one) for one in bits]),
            back,
            back_sibling,
            *[kept[one][0] for one in bits],
            *[kept[one][1] for one in bits],
            ends,
            ends_sibling,
        )
        return out[:count], out[count:]

    graph_bits = line.size.bit_length() - 1

    def backward_line(turn, kept, pieces=None):
        parts, others = [], ()
        last_coefs = near_coefs = ()
        if chips == 4:
            (last,), last_coefs = backward(turn, (3,), kept)
            passed = line.send(last, [(0, 1), (3, 2)])
            middle = line.send(last, [(1, 2), (2, 1)])
            others = (last,)
        if pieces is not None:
            pieces = add(*after(pieces, *others))
            others = (*others, pieces)
            arriving = dp_pieces(pieces)
        if chips == 4:
            (near, far), near_coefs = backward(turn, (1, 2), kept, others)
            (passed,) = after((passed,), far)
            if pieces is not None:
                pieces = add(*after(arriving, far))
                (far,) = after((far,), pieces)
            far = add(far, passed)
            (middle,) = after((middle,), far)
            (far,) = after((far,), middle)
            others = (far,)
            parts = [middle, line.trade(far, 2), line.trade(near, 1)]
        elif chips == 2:
            (near,), near_coefs = backward(turn, (1,), kept, others)
            parts = [line.trade(near, 1)]
        (own,), own_coefs = backward(turn, (0,), kept, others)
        if pieces is not None and chips < 4:
            pieces = add(*arriving)
        back_coefs = [*own_coefs, *near_coefs, *last_coefs]
        basis_grad = call(
            basis_kernel,
            (),
            [SMEM] + [slot_spec] * chips + triplet_specs[2:4],
            [whole(narrow, basis_width)],
            [shape((narrow, basis_width), F32)],
            4 * chips * slots * narrow * basis_width,
        )(
            jnp.concatenate([line.shard(turn, bits) for bits in range(chips)]),
            *back_coefs,
            basis,
            basis_sibling,
        )[0]
        return [own] + parts, basis_grad, pieces

    back_parts, basis_grad, dense_grads = backward_line(0, kept, across_cores(dense_grads, line))
    if chips > 1:
        dense_grads = add(*across_chips(dense_grads, line))
    dense_grads = summed_graph(dense_grads, line, range(2, graph_bits))
    if line.groups > 1:

        def backward_turn(carry, one):
            traveling, basis_grad = carry
            turn, got = one
            parts, more, _ = backward_line(turn, got)
            return (line.last_group(add(traveling, *parts)), basis_grad + more), None

        (traveling, basis_grad), _ = lax.scan(
            backward_turn,
            (jnp.zeros((stacked, lanes), BF16), basis_grad),
            (jnp.arange(1, line.groups), more_kept),
            reverse=True,
        )
        back_parts = back_parts + [traveling]

    small_rows = narrow + basis_width
    edge_grad, small_grads = call(
        functools.partial(final_kernel, len(back_parts)),
        (tiles,),
        [stack_spec] * len(back_parts)
        + [stack_spec, row_spec, row_spec, whole(narrow, wide), whole(narrow, basis_width)],
        [row_spec, whole(small_rows, wide)],
        [shape((row_count, wide), BF16), shape((small_rows, wide), BF16)],
        4 * row_count * wide * narrow,
        scratch=[pltpu.VMEM((small_rows, wide), F32)],
        grant=FINAL_GRANT,
    )(
        *back_parts,
        down_slope,
        edge_rows,
        back_summed,
        down_weight,
        basis_grad,
    )

    small_grads = add(*across_cores(small_grads, line))
    small_grads = summed_dp(summed_graph(small_grads, line, range(1, graph_bits)))
    small_grads = joined(small_grads, line.swap(small_grads), line.core)
    if chips > 1:
        dense_grads = joined(dense_grads, line.pair(dense_grads), line.chip % 2)
    dense_grads = dp_joined(dense_grads)
    dense_grads = joined(dense_grads, line.swap(dense_grads), line.core)
    scale = 1.0 / math.sqrt(lax.axis_size("dp") * shards * row_count)

    def scaled(source, *dims):
        return call(
            functools.partial(scale_kernel, scale),
            (),
            [whole(*source.shape)],
            [whole(*d) for d in dims],
            [shape(d, F32) for d in dims],
            source.size,
        )(source)

    first_grad, second_grad, up_grad, bilinear_grad = scaled(
        dense_grads, (wide, wide), (wide, wide), (narrow, wide), (narrow, narrow)
    )
    down_grad, basis_grad = scaled(small_grads, (narrow, wide), (basis_width, narrow))
    return (
        edge_grad[None],
        down_grad.T,
        basis_grad,
        bilinear_grad,
        up_grad,
        first_grad,
        second_grad,
    )


def solution(mesh):
    in_specs = (
        P("dp", "graph", None),
        P("dp", "graph", None),
        P("dp", "graph"),
        P("dp", None, "graph"),
        P("dp", "graph"),
        P("dp", "graph"),
        P(),
        P(),
        P(),
        P(),
        P(),
        P(),
    )
    out_specs = (P("dp", "graph", None), P(), P(), P(), P(), P(), P())
    return jax.shard_map(local, mesh=mesh, in_specs=in_specs, out_specs=out_specs, check_vma=False)
```

```python
import functools
import math

import jax
import jax.numpy as jnp
from jax import lax
from jax.experimental import pallas as pl
from jax.experimental.pallas import tpu as pltpu
from jax.sharding import PartitionSpec as P

HALF = 0.7071067811865476
F32 = jnp.float32
BF16 = jnp.bfloat16
MIB = 1024 * 1024
FORWARD_GRANT = 10
BACKWARD_GRANT = 10
DENSE_GRANT = 18
FINAL_GRANT = 12


def contract(left, right, left_dim, right_dim):
    return lax.dot_general(
        left, right, (((left_dim,), (right_dim,)), ((), ())), preferred_element_type=F32
    )


def sigmoid(value):
    return 0.5 + 0.5 * jnp.tanh(0.5 * value)


def slope_of(argument, logistic):
    return logistic * (1.0 + argument * (1.0 - logistic))


def split_index(index_row, lanes):
    slots = index_row.shape[1]
    low = jnp.bitwise_and(index_row, lanes - 1)
    high = jnp.right_shift(index_row, lanes.bit_length() - 1)
    lane_ids = lax.broadcasted_iota(jnp.int32, (lanes, slots), 0)
    return high, jnp.where(lane_ids == low, 1.0, 0.0).astype(BF16)


def stack(rows, lanes):
    groups = rows.shape[1] // lanes
    return jnp.concatenate([rows[:, g * lanes : (g + 1) * lanes] for g in range(groups)], axis=0)


def unstack(rows, narrow):
    groups = rows.shape[0] // narrow
    return jnp.concatenate([rows[g * narrow : (g + 1) * narrow] for g in range(groups)], axis=1)


def pick_rows(stacked, high, lane_hot, narrow):
    groups = stacked.shape[0] // narrow
    every = contract(stacked, lane_hot, 1, 0)
    picked = jnp.where(high == 0, every[:narrow], 0.0)
    for g in range(1, groups):
        picked = jnp.where(high == g, every[g * narrow : (g + 1) * narrow], picked)
    return picked


def place_rows(values, high, lane_hot, groups):
    zero = jnp.zeros((), values.dtype)
    spread = jnp.concatenate([jnp.where(high == g, values, zero) for g in range(groups)], axis=0)
    return contract(spread.astype(BF16), lane_hot, 1, 1)


def down_kernel(edge_ref, weight_ref, rows_ref, slope_ref):
    lanes = rows_ref.shape[1]
    pre = contract(edge_ref[...], weight_ref[...], 1, 1).T
    logistic = sigmoid(pre)
    rows_ref[...] = stack((pre * logistic).astype(BF16), lanes)
    slope_ref[...] = stack(slope_of(pre, logistic), lanes)


def forward_kernel(shard_ref, rows_ref, *refs):
    rows = rows_ref[...]
    ends, basis, weight_ref = refs[:2], refs[2:4], refs[4]
    totals, fetched_ref, coef_ref = refs[-4:-2], refs[-2], refs[-1]
    shard = shard_ref[0]
    narrow = weight_ref.shape[1]
    groups = totals[0].shape[0] // narrow
    lanes = totals[0].shape[1]
    slots = ends[0].shape[3]
    at = pl.ds(pl.multiple_of(shard * slots, slots), slots)
    for i in range(2):
        high, lane_hot = split_index(ends[i][0, shard], lanes)
        fetched = pick_rows(rows, high, lane_hot, narrow)
        fetched_ref[i] = fetched.astype(BF16)
        coef = contract(weight_ref[...], basis[i][:, at], 0, 0)
        coef_ref[i] = coef.astype(BF16)
        high, lane_hot = split_index(ends[i][1, shard], lanes)
        placed = place_rows(coef * fetched, high, lane_hot, groups)
        if len(refs) == 11:
            placed += refs[5 + i][...]
        totals[i][...] = placed


def dense_kernel(
    count_ref,
    edge_ref,
    cotangent_ref,
    gathered_ref,
    more_ref,
    bilinear_ref,
    up_ref,
    first_ref,
    first_turned_ref,
    second_ref,
    second_turned_ref,
    summed_ref,
    back_ref,
    mine_ref,
    away_ref,
    total,
):
    step = pl.program_id(0)
    tile, wide = edge_ref.shape
    narrow = bilinear_ref.shape[0]
    lanes = gathered_ref.shape[1]

    @pl.when(step == 0)
    def _():
        total[...] = jnp.zeros_like(total)

    half = tile // 2
    spans = [slice(i * half, (i + 1) * half) for i in range(2)]
    gathered = unstack((gathered_ref[...] + more_ref[...]).astype(BF16), narrow)
    mixed = contract(bilinear_ref[...], gathered, 0, 0).astype(BF16)
    pre_up = [contract(mixed[:, at], up_ref[...], 0, 0) for at in spans]
    up_logistic = [sigmoid(x) for x in pre_up]
    summed_half = [
        (edge_ref[at, :].astype(F32) + x * y).astype(BF16)
        for at, x, y in zip(spans, pre_up, up_logistic)
    ]
    pre_first = [contract(x, first_ref[...], 1, 0) for x in summed_half]
    first_logistic = [sigmoid(x) for x in pre_first]
    first_rows = [(x * y).astype(BF16) for x, y in zip(pre_first, first_logistic)]
    pre_second = [contract(x, second_ref[...], 1, 0) for x in first_rows]
    back_top, back_second = [], []
    for at, x in zip(spans, pre_second):
        row_ids = step * tile + at.start + lax.broadcasted_iota(jnp.int32, (half, 1), 0)
        live = jnp.where(row_ids < count_ref[0], HALF, 0.0)
        back_top.append(cotangent_ref[at, :].astype(F32) * live)
        back_second.append((back_top[-1] * slope_of(x, sigmoid(x))).astype(BF16))
    back_first = [
        (contract(x, second_turned_ref[...], 1, 0) * slope_of(y, z)).astype(BF16)
        for x, y, z in zip(back_second, pre_first, first_logistic)
    ]
    back_summed = [
        x + contract(y, first_turned_ref[...], 1, 0) for x, y in zip(back_top, back_first)
    ]
    back_up = [
        (x * slope_of(y, z)).astype(BF16) for x, y, z in zip(back_summed, pre_up, up_logistic)
    ]
    for at, x in zip(spans, back_summed):
        summed_ref[at, :] = x.astype(BF16)
    back_up = jnp.concatenate(back_up)
    back_mixed = contract(back_up, up_ref[...], 1, 1).T.astype(BF16)
    back_ref[...] = stack(contract(bilinear_ref[...], back_mixed, 1, 0).astype(BF16), lanes)
    total[:wide] += contract(jnp.concatenate(summed_half), jnp.concatenate(back_first), 0, 0)
    total[wide : 2 * wide] += contract(
        jnp.concatenate(first_rows), jnp.concatenate(back_second), 0, 0
    )
    total[2 * wide : 2 * wide + narrow] += contract(mixed, back_up, 1, 0)
    total[2 * wide + narrow :, :narrow] += contract(gathered, back_mixed, 1, 1)

    @pl.when(step == pl.num_programs(0) - 1)
    def _():
        rows = mine_ref.shape[0]
        core = count_ref[1]
        mine_ref[...] = total[pl.ds(pl.multiple_of(core * rows, 16), rows), :].astype(BF16)
        away_ref[...] = total[pl.ds(pl.multiple_of((1 - core) * rows, 16), rows), :].astype(BF16)


def backward_kernel(count, shards_ref, own_ref, sibling_ref, *refs):
    fetched, coefs, ends = refs[:count], refs[count : 2 * count], refs[2 * count : 2 * count + 2]
    parts, back_coefs = refs[2 * count + 2 : 3 * count + 2], refs[3 * count + 2 :]
    narrow = fetched[0].shape[1]
    groups = own_ref.shape[0] // narrow
    lanes = own_ref.shape[1]
    for s in range(count):
        shard = shards_ref[s]
        part = None
        for i, back_ref in enumerate((own_ref, sibling_ref)):
            high, lane_hot = split_index(ends[i][1, shard], lanes)
            message = pick_rows(back_ref[...], high, lane_hot, narrow)
            back_coefs[s][i] = (message * fetched[s][i].astype(F32)).astype(BF16)
            high, lane_hot = split_index(ends[i][0, shard], lanes)
            placed = place_rows(message * coefs[s][i].astype(F32), high, lane_hot, groups)
            part = placed if part is None else part + placed
        parts[s][...] = part.astype(BF16)


def basis_kernel(shards_ref, *refs):
    back_coefs, basis, grad_ref = refs[:-3], refs[-3:-1], refs[-1]
    slots = back_coefs[0].shape[2]
    grad = jnp.zeros(grad_ref.shape, F32)
    for s, ref in enumerate(back_coefs):
        at = pl.ds(pl.multiple_of(shards_ref[s] * slots, slots), slots)
        for i in range(2):
            grad += contract(ref[i], basis[i][:, at], 1, 1)
    grad_ref[...] = grad


def final_kernel(count, *refs):
    parts = refs[:count]
    slope_ref, edge_ref, summed_ref, weight_ref, basis_ref, edge_grad_ref, grads_ref, total = refs[
        count:
    ]
    step = pl.program_id(0)
    narrow = weight_ref.shape[0]
    basis_width = basis_ref.shape[1]

    @pl.when(step == 0)
    def _():
        total[...] = jnp.zeros_like(total)

    back_down = parts[0][...].astype(F32)
    for part in parts[1:]:
        back_down += part[...].astype(F32)
    back_pre = unstack((back_down * slope_ref[...]).astype(BF16), narrow)
    total[:narrow] += contract(back_pre, edge_ref[...], 1, 0)
    edge_grad_ref[...] = (
        summed_ref[...].astype(F32) + contract(back_pre, weight_ref[...], 0, 0)
    ).astype(BF16)

    @pl.when(step == pl.num_programs(0) - 1)
    def _():
        total[narrow : narrow + basis_width, :narrow] = basis_ref[...].T
        grads_ref[...] = total[...].astype(BF16)


def scale_kernel(scale, source_ref, *outs):
    row = 0
    for out in outs:
        rows, columns = out.shape
        out[...] = source_ref[row : row + rows, :columns].astype(F32) * scale
        row += rows


def call(kernel, grid, in_specs, out_specs, out_shape, flops, transcendentals=0, scratch=(), aliases=None, grant=8):
    def run(*operands):
        size = sum(x.size * x.dtype.itemsize for x in operands)
        size += sum(math.prod(x.shape) * x.dtype.itemsize for x in out_shape)
        return pl.pallas_call(
            kernel,
            grid=grid,
            in_specs=in_specs,
            out_specs=out_specs,
            out_shape=out_shape,
            scratch_shapes=scratch,
            input_output_aliases=aliases or {},
            compiler_params=pltpu.CompilerParams(vmem_limit_bytes=grant * MIB),
            cost_estimate=pl.CostEstimate(
                flops=flops, bytes_accessed=size, transcendentals=transcendentals
            ),
        )(*operands)

    return run


def whole(*shape):
    return pl.BlockSpec(shape, lambda *_: (0,) * len(shape))


SMEM = pl.BlockSpec(memory_space=pltpu.SMEM)


def in_hbm(array):
    return pltpu.with_memory_space_constraint(array, pltpu.HBM)


def shape(dims, dtype):
    return jax.ShapeDtypeStruct(dims, dtype)


def turned(count, size, stride, turn):
    pairs = []
    for g in range(count):
        place = g // stride % size
        pairs.append((g, g + ((place + turn) % size - place) * stride))
    return pairs


class Line:
    cores = 2

    def __init__(self):
        self.size = lax.axis_size("graph")
        self.chips = math.gcd(self.size // self.cores, 4)
        self.span = self.chips * self.cores
        self.groups = self.size // self.span
        me = lax.axis_index("graph")
        self.core = me % self.cores
        self.chip = me // self.cores % self.chips
        self.group = me // self.span

    def send(self, array, moves):
        pairs = [
            (base + one * self.cores + core, base + other * self.cores + core)
            for base in range(0, self.size, self.span)
            for one, other in moves
            for core in range(self.cores)
        ]
        return lax.ppermute(array, "graph", pairs)

    def trade(self, array, bits):
        return self.send(array, [(chip, chip ^ bits) for chip in range(self.chips)])

    def pair(self, array):
        return lax.ppermute(array, "graph", [(g, g ^ 2) for g in range(self.size)])

    def swap(self, array):
        return lax.ppermute(array, "graph", [(g, g ^ 1) for g in range(self.size)])

    def next_group(self, array):
        return lax.ppermute(array, "graph", turned(self.size, self.groups, self.span, -1))

    def last_group(self, array):
        return lax.ppermute(array, "graph", turned(self.size, self.groups, self.span, 1))

    def shard(self, turn, bits):
        group = (self.group + turn) % self.groups
        shard = group * self.span + (self.chip ^ bits) * self.cores + self.core
        return shard.astype(jnp.int32).reshape(1)


def add(*arrays):
    return sum(a.astype(F32) for a in arrays).astype(BF16)


def after(arrays, *others):
    return lax.optimization_barrier((tuple(arrays), others))[0]


def halves(array, place):
    rows = array.shape[0] // 2
    first = place == 0
    return (
        jnp.where(first, array[:rows], array[rows:]),
        jnp.where(first, array[rows:], array[:rows]),
    )


def joined(mine, other, place):
    return jnp.where(
        place == 0, jnp.concatenate([mine, other]), jnp.concatenate([other, mine])
    )


def piece_of(array, size, place):
    rows = array.shape[0] // size
    return lax.dynamic_slice_in_dim(array, place * rows, rows, 0)


def dp_pieces(array):
    size, me = lax.axis_size("dp"), lax.axis_index("dp")
    arrived = [piece_of(array, size, me)]
    for turn in range(1, size):
        away = piece_of(array, size, (me + turn) % size)
        arrived.append(lax.ppermute(away, "dp", turned(size, size, 1, turn)))
    return arrived


def dp_joined(piece):
    size, me = lax.axis_size("dp"), lax.axis_index("dp")
    rows = piece.shape[0]
    out = jnp.zeros((size * rows, piece.shape[1]), piece.dtype)
    out = lax.dynamic_update_slice_in_dim(out, piece, me * rows, 0)
    for turn in range(1, size):
        other = lax.ppermute(piece, "dp", turned(size, size, 1, turn))
        out = lax.dynamic_update_slice_in_dim(out, other, (me - turn) % size * rows, 0)
    return out


def across_chips(array, line):
    mine, away = halves(array, line.chip % 2)
    return [mine, line.pair(away)]


def across_cores(array, line):
    mine, away = halves(array, line.core)
    return [mine, line.swap(away)]


def summed_dp(array):
    size = lax.axis_size("dp")
    for bit in range(size.bit_length() - 1):
        array = add(array, lax.ppermute(array, "dp", [(g, g ^ (1 << bit)) for g in range(size)]))
    return array


def summed_graph(array, line, bits):
    for bit in bits:
        pairs = [(g, g ^ (1 << bit)) for g in range(line.size)]
        array = add(array, lax.ppermute(array, "graph", pairs))
    return array


def local(
    edge_state,
    cotangent,
    edge_count,
    triplet_basis,
    triplet_in,
    triplet_out,
    down_weight,
    basis_weight,
    bilinear_weight,
    up_weight,
    first_weight,
    second_weight,
):
    edge_rows = edge_state[0]
    row_count, wide = edge_rows.shape
    line = Line()
    shards, chips = line.size, line.chips
    narrow = down_weight.shape[1]
    down_weight = down_weight.T
    basis = triplet_basis[0]
    basis_width, tri_rows = basis.shape
    slots = tri_rows // shards
    lanes = math.gcd(row_count, 256)
    stacked = narrow * (row_count // lanes)
    tile = math.gcd(row_count, 512)
    tiles = row_count // tile
    row_spec = pl.BlockSpec((tile, wide), lambda i: (i, 0))
    stack_spec = pl.BlockSpec((narrow * (tile // lanes), lanes), lambda i: (i, 0))
    rows_spec = whole(stacked, lanes)

    ends = jnp.stack([triplet_in.reshape(shards, 1, slots), triplet_out.reshape(shards, 1, slots)])
    triplet_specs = (
        [whole(2, shards, 1, slots)] * 2
        + [whole(basis_width, tri_rows)] * 2
        + [whole(basis_width, narrow)]
    )
    block_flops = 8 * slots * row_count * narrow

    down_rows, down_slope = call(
        down_kernel,
        (tiles,),
        [row_spec, whole(narrow, wide)],
        [stack_spec] * 2,
        [shape((stacked, lanes), BF16), shape((stacked, lanes), F32)],
        2 * row_count * wide * narrow,
        row_count * narrow,
    )(in_hbm(edge_rows), in_hbm(down_weight))

    slot_spec = whole(2, narrow, slots)
    slot_shape = pltpu.HBM((2, narrow, slots), BF16)

    ends, leaving = after((ends, basis), down_rows)
    ends_sibling = line.swap(ends)
    basis_sibling = line.swap(leaving)
    triplets = (ends, ends_sibling, basis, basis_sibling, basis_weight)

    def forward(turn, bits, rows, totals):
        total_shape = shape((stacked, lanes), F32)
        final = line.groups == 1 and bits == chips - 1
        out = call(
            forward_kernel,
            (),
            [SMEM, rows_spec] + triplet_specs + [rows_spec] * len(totals),
            [rows_spec] * 2 + [slot_spec] * 2,
            [pltpu.HBM((stacked, lanes), F32) if final else total_shape, total_shape]
            + [slot_shape] * 2,
            block_flops,
            aliases={7 + i: i for i in range(len(totals)) if i == 1 or not final},
            grant=FORWARD_GRANT,
        )(line.shard(turn, bits), rows, *triplets, *totals)
        return tuple(out[:2]), tuple(out[2:])

    def forward_line(turn, rows, totals, *others):
        arriving = [line.trade(rows, bits) for bits in range(1, chips)]
        totals, got = forward(turn, 0, rows, totals)
        kept = [got]
        for bits in range(1, chips):
            (rows,) = after((arriving[bits - 1],), *totals, *others)
            totals, got = forward(turn, bits, rows, totals)
            kept.append(got)
        return totals, kept

    first_turned, second_turned = after((first_weight, second_weight), down_rows)
    first_turned, second_turned = first_turned.T, second_turned.T
    totals, kept = forward_line(0, down_rows, (), first_turned, second_turned)
    if line.groups > 1:

        def forward_turn(carry, turn):
            rows, totals = carry
            rows = line.next_group(rows)
            totals, got = forward_line(turn, rows, totals)
            return (rows, totals), got

        (_, totals), more_kept = lax.scan(
            forward_turn, (down_rows, totals), jnp.arange(1, line.groups)
        )

    grad_rows = 2 * wide + 2 * narrow
    back_summed, back_gathered, mine, away = call(
        dense_kernel,
        (tiles,),
        [
            SMEM,
            row_spec,
            row_spec,
            stack_spec,
            stack_spec,
            whole(narrow, narrow),
            whole(narrow, wide),
            whole(wide, wide),
            whole(wide, wide),
            whole(wide, wide),
            whole(wide, wide),
        ],
        [row_spec, stack_spec] + [whole(grad_rows // 2, wide)] * 2,
        [
            pltpu.HBM((row_count, wide), BF16),
            shape((stacked, lanes), BF16),
            shape((grad_rows // 2, wide), BF16),
            shape((grad_rows // 2, wide), BF16),
        ],
        12 * row_count * wide * wide + 6 * row_count * wide * narrow,
        3 * row_count * wide,
        scratch=[pltpu.VMEM((grad_rows, wide), F32)],
        grant=DENSE_GRANT,
    )(
        jnp.stack([edge_count[0, 0], line.core.astype(jnp.int32)]),
        in_hbm(edge_rows),
        in_hbm(cotangent[0]),
        in_hbm(totals[0]) if line.groups == 1 else totals[0],
        line.swap(totals[1]),
        bilinear_weight,
        up_weight,
        in_hbm(first_weight),
        first_turned,
        in_hbm(second_weight),
        second_turned,
    )
    back_sibling = line.swap(back_gathered)

    def backward(turn, bits, kept, others=()):
        count = len(bits)
        (back,) = after((back_gathered,), *others)
        out = call(
            functools.partial(backward_kernel, count),
            (),
            [SMEM] + [rows_spec] * 2 + [slot_spec] * (2 * count) + triplet_specs[:2],
            [rows_spec] * count + [slot_spec] * count,
            [shape((stacked, lanes), BF16)] * count + [shape((2, narrow, slots), BF16)] * count,
            count * block_flops,
            grant=BACKWARD_GRANT,
        )(
            jnp.concatenate([line.shard(turn, one) for one in bits]),
            back,
            back_sibling,
            *[kept[one][0] for one in bits],
            *[kept[one][1] for one in bits],
            ends,
            ends_sibling,
        )
        return out[:count], out[count:]

    graph_bits = line.size.bit_length() - 1

    def backward_line(turn, kept, pieces=None):
        parts, others = [], ()
        last_coefs = near_coefs = ()
        if chips == 4:
            (last,), last_coefs = backward(turn, (3,), kept)
            passed = line.send(last, [(0, 1), (3, 2)])
            middle = line.send(last, [(1, 2), (2, 1)])
            others = (last,)
        if pieces is not None:
            pieces = add(*after(pieces, *others))
            others = (*others, pieces)
            arriving = dp_pieces(pieces)
        if chips == 4:
            (near, far), near_coefs = backward(turn, (1, 2), kept, others)
            (passed,) = after((passed,), far)
            if pieces is not None:
                pieces = add(*after(arriving, far))
                (far,) = after((far,), pieces)
            far = add(far, passed)
            (middle,) = after((middle,), far)
            (far,) = after((far,), middle)
            others = (far,)
            parts = [middle, line.trade(far, 2), line.trade(near, 1)]
        elif chips == 2:
            (near,), near_coefs = backward(turn, (1,), kept, others)
            parts = [line.trade(near, 1)]
        (own,), own_coefs = backward(turn, (0,), kept, others)
        if pieces is not None and chips < 4:
            pieces = add(*arriving)
        back_coefs = [*own_coefs, *near_coefs, *last_coefs]
        basis_grad = call(
            basis_kernel,
            (),
            [SMEM] + [slot_spec] * chips + triplet_specs[2:4],
            [whole(narrow, basis_width)],
            [shape((narrow, basis_width), F32)],
            4 * chips * slots * narrow * basis_width,
        )(
            jnp.concatenate([line.shard(turn, bits) for bits in range(chips)]),
            *back_coefs,
            basis,
            basis_sibling,
        )[0]
        return [own] + parts, basis_grad, pieces

    back_parts, basis_grad, dense_grads = backward_line(0, kept, [mine, line.swap(away)])
    if chips > 1:
        dense_grads = add(*across_chips(dense_grads, line))
    dense_grads = summed_graph(dense_grads, line, range(2, graph_bits))
    if line.groups > 1:

        def backward_turn(carry, one):
            traveling, basis_grad = carry
            turn, got = one
            parts, more, _ = backward_line(turn, got)
            return (line.last_group(add(traveling, *parts)), basis_grad + more), None

        (traveling, basis_grad), _ = lax.scan(
            backward_turn,
            (jnp.zeros((stacked, lanes), BF16), basis_grad),
            (jnp.arange(1, line.groups), more_kept),
            reverse=True,
        )
        back_parts = back_parts + [traveling]

    small_rows = narrow + basis_width
    edge_grad, small_grads = call(
        functools.partial(final_kernel, len(back_parts)),
        (tiles,),
        [stack_spec] * len(back_parts)
        + [stack_spec, row_spec, row_spec, whole(narrow, wide), whole(narrow, basis_width)],
        [row_spec, whole(small_rows, wide)],
        [shape((row_count, wide), BF16), shape((small_rows, wide), BF16)],
        4 * row_count * wide * narrow,
        scratch=[pltpu.VMEM((small_rows, wide), F32)],
        grant=FINAL_GRANT,
    )(
        *back_parts,
        down_slope,
        edge_rows,
        back_summed,
        down_weight,
        basis_grad,
    )

    small_grads = add(*across_cores(small_grads, line))
    small_grads = summed_dp(summed_graph(small_grads, line, range(1, graph_bits)))
    small_grads = joined(small_grads, line.swap(small_grads), line.core)
    if chips > 1:
        dense_grads = joined(dense_grads, line.pair(dense_grads), line.chip % 2)
    dense_grads = dp_joined(dense_grads)
    dense_grads = joined(dense_grads, line.swap(dense_grads), line.core)
    scale = 1.0 / math.sqrt(lax.axis_size("dp") * shards * row_count)

    def scaled(source, *dims):
        return call(
            functools.partial(scale_kernel, scale),
            (),
            [whole(*source.shape)],
            [whole(*d) for d in dims],
            [shape(d, F32) for d in dims],
            source.size,
        )(source)

    first_grad, second_grad, up_grad, bilinear_grad = scaled(
        dense_grads, (wide, wide), (wide, wide), (narrow, wide), (narrow, narrow)
    )
    down_grad, basis_grad = scaled(small_grads, (narrow, wide), (basis_width, narrow))
    return (
        edge_grad[None],
        down_grad.T,
        basis_grad,
        bilinear_grad,
        up_grad,
        first_grad,
        second_grad,
    )


def solution(mesh):
    in_specs = (
        P("dp", "graph", None),
        P("dp", "graph", None),
        P("dp", "graph"),
        P("dp", None, "graph"),
        P("dp", "graph"),
        P("dp", "graph"),
        P(),
        P(),
        P(),
        P(),
        P(),
        P(),
    )
    out_specs = (P("dp", "graph", None), P(), P(), P(), P(), P(), P())
    return jax.shard_map(local, mesh=mesh, in_specs=in_specs, out_specs=out_specs, check_vma=False)
```

```python
import functools
import math

import jax
import jax.numpy as jnp
from jax import lax
from jax.experimental import pallas as pl
from jax.experimental.pallas import tpu as pltpu
from jax.sharding import PartitionSpec as P

HALF = 0.7071067811865476
F32 = jnp.float32
BF16 = jnp.bfloat16
MIB = 1024 * 1024
FORWARD_GRANT = 10
BACKWARD_GRANT = 10
DENSE_GRANT = 18
FINAL_GRANT = 12


def contract(left, right, left_dim, right_dim):
    return lax.dot_general(
        left, right, (((left_dim,), (right_dim,)), ((), ())), preferred_element_type=F32
    )


def sigmoid(value):
    return 0.5 + 0.5 * jnp.tanh(0.5 * value)


def split_index(index_row, lanes):
    slots = index_row.shape[1]
    low = jnp.bitwise_and(index_row, lanes - 1)
    high = jnp.right_shift(index_row, lanes.bit_length() - 1)
    lane_ids = lax.broadcasted_iota(jnp.int32, (lanes, slots), 0)
    return high, jnp.where(lane_ids == low, 1.0, 0.0).astype(BF16)


def stack(rows, lanes):
    groups = rows.shape[1] // lanes
    return jnp.concatenate([rows[:, g * lanes : (g + 1) * lanes] for g in range(groups)], axis=0)


def unstack(rows, narrow):
    groups = rows.shape[0] // narrow
    return jnp.concatenate([rows[g * narrow : (g + 1) * narrow] for g in range(groups)], axis=1)


def pick_rows(stacked, high, lane_hot, narrow):
    groups = stacked.shape[0] // narrow
    every = contract(stacked, lane_hot, 1, 0)
    picked = jnp.where(high == 0, every[:narrow], 0.0)
    for g in range(1, groups):
        picked = jnp.where(high == g, every[g * narrow : (g + 1) * narrow], picked)
    return picked


def place_rows(values, high, lane_hot, groups):
    zero = jnp.zeros((), values.dtype)
    spread = jnp.concatenate([jnp.where(high == g, values, zero) for g in range(groups)], axis=0)
    return contract(spread.astype(BF16), lane_hot, 1, 1)


def down_kernel(edge_ref, weight_ref, rows_ref, slope_ref):
    lanes = rows_ref.shape[1]
    pre = contract(edge_ref[...], weight_ref[...], 1, 1).T
    logistic = sigmoid(pre)
    rows_ref[...] = stack((pre * logistic).astype(BF16), lanes)
    slope_ref[...] = stack(logistic * (1.0 + pre * (1.0 - logistic)), lanes)


def forward_kernel(shard_ref, rows_ref, *refs):
    rows = rows_ref[...]
    ends, basis, weight_ref = refs[:2], refs[2:4], refs[4]
    totals, fetched_ref, coef_ref = refs[-4:-2], refs[-2], refs[-1]
    shard = shard_ref[0]
    narrow = weight_ref.shape[1]
    groups = totals[0].shape[0] // narrow
    lanes = totals[0].shape[1]
    slots = ends[0].shape[3]
    at = pl.ds(pl.multiple_of(shard * slots, slots), slots)
    for i in range(2):
        high, lane_hot = split_index(ends[i][0, shard], lanes)
        fetched = pick_rows(rows, high, lane_hot, narrow)
        fetched_ref[i] = fetched.astype(BF16)
        coef = contract(weight_ref[...], basis[i][:, at], 0, 0)
        coef_ref[i] = coef.astype(BF16)
        high, lane_hot = split_index(ends[i][1, shard], lanes)
        placed = place_rows(coef * fetched, high, lane_hot, groups)
        if len(refs) == 11:
            placed += refs[5 + i][...]
        totals[i][...] = placed


def dense_kernel(
    count_ref,
    edge_ref,
    cotangent_ref,
    gathered_ref,
    more_ref,
    bilinear_ref,
    up_ref,
    first_ref,
    first_turned_ref,
    second_ref,
    second_turned_ref,
    summed_ref,
    back_ref,
    grads_ref,
    total,
):
    step = pl.program_id(0)
    tile, wide = edge_ref.shape
    narrow = bilinear_ref.shape[0]
    lanes = gathered_ref.shape[1]

    @pl.when(step == 0)
    def _():
        total[...] = jnp.zeros_like(total)

    gathered = unstack((gathered_ref[...] + more_ref[...]).astype(BF16), narrow)
    mixed = contract(bilinear_ref[...], gathered, 0, 0).astype(BF16)
    pre_up = contract(mixed, up_ref[...], 0, 0)
    up_logistic = sigmoid(pre_up)
    summed_half = (edge_ref[...].astype(F32) + pre_up * up_logistic).astype(BF16)
    pre_first = contract(summed_half, first_ref[...], 1, 0)
    first_logistic = sigmoid(pre_first)
    first_rows = (pre_first * first_logistic).astype(BF16)
    pre_second = contract(first_rows, second_ref[...], 1, 0)
    logistic = sigmoid(pre_second)
    row_ids = step * tile + lax.broadcasted_iota(jnp.int32, (tile, 1), 0)
    live = jnp.where(row_ids < count_ref[0, 0], HALF, 0.0)
    back_top = cotangent_ref[...].astype(F32) * live
    back_second = (back_top * (logistic * (1.0 + pre_second * (1.0 - logistic)))).astype(BF16)
    slope = first_logistic * (1.0 + pre_first * (1.0 - first_logistic))
    back_first = (contract(back_second, second_turned_ref[...], 1, 0) * slope).astype(BF16)
    back_summed = back_top + contract(back_first, first_turned_ref[...], 1, 0)
    summed_ref[...] = back_summed.astype(BF16)
    slope = up_logistic * (1.0 + pre_up * (1.0 - up_logistic))
    back_up = (back_summed * slope).astype(BF16)
    back_mixed = contract(back_up, up_ref[...], 1, 1).T.astype(BF16)
    back_ref[...] = stack(contract(bilinear_ref[...], back_mixed, 1, 0).astype(BF16), lanes)
    total[:wide] += contract(summed_half, back_first, 0, 0)
    total[wide : 2 * wide] += contract(first_rows, back_second, 0, 0)
    total[2 * wide : 2 * wide + narrow] += contract(mixed, back_up, 1, 0)
    total[2 * wide + narrow :, :narrow] += contract(gathered, back_mixed, 1, 1)

    @pl.when(step == pl.num_programs(0) - 1)
    def _():
        grads_ref[...] = total[...].astype(BF16)


def backward_kernel(count, shards_ref, own_ref, sibling_ref, *refs):
    fetched, coefs, ends = refs[:count], refs[count : 2 * count], refs[2 * count : 2 * count + 2]
    parts, back_coefs = refs[2 * count + 2 : 3 * count + 2], refs[3 * count + 2 :]
    narrow = fetched[0].shape[1]
    groups = own_ref.shape[0] // narrow
    lanes = own_ref.shape[1]
    for s in range(count):
        shard = shards_ref[s]
        part = None
        for i, back_ref in enumerate((own_ref, sibling_ref)):
            high, lane_hot = split_index(ends[i][1, shard], lanes)
            message = pick_rows(back_ref[...], high, lane_hot, narrow)
            back_coefs[s][i] = (message * fetched[s][i].astype(F32)).astype(BF16)
            high, lane_hot = split_index(ends[i][0, shard], lanes)
            placed = place_rows(message * coefs[s][i].astype(F32), high, lane_hot, groups)
            part = placed if part is None else part + placed
        parts[s][...] = part.astype(BF16)


def basis_kernel(shards_ref, *refs):
    back_coefs, basis, grad_ref = refs[:-3], refs[-3:-1], refs[-1]
    slots = back_coefs[0].shape[2]
    grad = jnp.zeros(grad_ref.shape, F32)
    for s, ref in enumerate(back_coefs):
        at = pl.ds(pl.multiple_of(shards_ref[s] * slots, slots), slots)
        for i in range(2):
            grad += contract(ref[i], basis[i][:, at], 1, 1)
    grad_ref[...] = grad


def final_kernel(count, *refs):
    parts = refs[:count]
    slope_ref, edge_ref, summed_ref, weight_ref, basis_ref, edge_grad_ref, grads_ref, total = refs[
        count:
    ]
    step = pl.program_id(0)
    narrow = weight_ref.shape[0]
    basis_width = basis_ref.shape[1]

    @pl.when(step == 0)
    def _():
        total[...] = jnp.zeros_like(total)

    back_down = parts[0][...].astype(F32)
    for part in parts[1:]:
        back_down += part[...].astype(F32)
    back_pre = unstack((back_down * slope_ref[...]).astype(BF16), narrow)
    total[:narrow] += contract(back_pre, edge_ref[...], 1, 0)
    edge_grad_ref[...] = (
        summed_ref[...].astype(F32) + contract(back_pre, weight_ref[...], 0, 0)
    ).astype(BF16)

    @pl.when(step == pl.num_programs(0) - 1)
    def _():
        total[narrow : narrow + basis_width, :narrow] = basis_ref[...].T
        grads_ref[...] = total[...].astype(BF16)


def scale_kernel(scale, source_ref, *outs):
    row = 0
    for out in outs:
        rows, columns = out.shape
        out[...] = source_ref[row : row + rows, :columns].astype(F32) * scale
        row += rows


def call(kernel, grid, in_specs, out_specs, out_shape, flops, transcendentals=0, scratch=(), aliases=None, grant=8):
    def run(*operands):
        size = sum(x.size * x.dtype.itemsize for x in operands)
        size += sum(math.prod(x.shape) * x.dtype.itemsize for x in out_shape)
        return pl.pallas_call(
            kernel,
            grid=grid,
            in_specs=in_specs,
            out_specs=out_specs,
            out_shape=out_shape,
            scratch_shapes=scratch,
            input_output_aliases=aliases or {},
            compiler_params=pltpu.CompilerParams(vmem_limit_bytes=grant * MIB),
            cost_estimate=pl.CostEstimate(
                flops=flops, bytes_accessed=size, transcendentals=transcendentals
            ),
        )(*operands)

    return run


def whole(*shape):
    return pl.BlockSpec(shape, lambda *_: (0,) * len(shape))


SMEM = pl.BlockSpec(memory_space=pltpu.SMEM)


def in_hbm(array):
    return pltpu.with_memory_space_constraint(array, pltpu.HBM)


def shape(dims, dtype):
    return jax.ShapeDtypeStruct(dims, dtype)


def turned(count, size, stride, turn):
    pairs = []
    for g in range(count):
        place = g // stride % size
        pairs.append((g, g + ((place + turn) % size - place) * stride))
    return pairs


class Line:
    cores = 2

    def __init__(self):
        self.size = lax.axis_size("graph")
        self.chips = math.gcd(self.size // self.cores, 4)
        self.span = self.chips * self.cores
        self.groups = self.size // self.span
        me = lax.axis_index("graph")
        self.core = me % self.cores
        self.chip = me // self.cores % self.chips
        self.group = me // self.span

    def send(self, array, moves):
        pairs = [
            (base + one * self.cores + core, base + other * self.cores + core)
            for base in range(0, self.size, self.span)
            for one, other in moves
            for core in range(self.cores)
        ]
        return lax.ppermute(array, "graph", pairs)

    def trade(self, array, bits):
        return self.send(array, [(chip, chip ^ bits) for chip in range(self.chips)])

    def pair(self, array):
        return lax.ppermute(array, "graph", [(g, g ^ 2) for g in range(self.size)])

    def swap(self, array):
        return lax.ppermute(array, "graph", [(g, g ^ 1) for g in range(self.size)])

    def next_group(self, array):
        return lax.ppermute(array, "graph", turned(self.size, self.groups, self.span, -1))

    def last_group(self, array):
        return lax.ppermute(array, "graph", turned(self.size, self.groups, self.span, 1))

    def shard(self, turn, bits):
        group = (self.group + turn) % self.groups
        shard = group * self.span + (self.chip ^ bits) * self.cores + self.core
        return shard.astype(jnp.int32).reshape(1)


def add(*arrays):
    return sum(a.astype(F32) for a in arrays).astype(BF16)


def after(arrays, *others):
    return lax.optimization_barrier((tuple(arrays), others))[0]


def halves(array, place):
    rows = array.shape[0] // 2
    first = place == 0
    return (
        jnp.where(first, array[:rows], array[rows:]),
        jnp.where(first, array[rows:], array[:rows]),
    )


def joined(mine, other, place):
    return jnp.where(
        place == 0, jnp.concatenate([mine, other]), jnp.concatenate([other, mine])
    )


def piece_of(array, size, place):
    rows = array.shape[0] // size
    return lax.dynamic_slice_in_dim(array, place * rows, rows, 0)


def dp_pieces(array):
    size, me = lax.axis_size("dp"), lax.axis_index("dp")
    arrived = [piece_of(array, size, me)]
    for turn in range(1, size):
        away = piece_of(array, size, (me + turn) % size)
        arrived.append(lax.ppermute(away, "dp", turned(size, size, 1, turn)))
    return arrived


def dp_joined(piece):
    size, me = lax.axis_size("dp"), lax.axis_index("dp")
    rows = piece.shape[0]
    out = jnp.zeros((size * rows, piece.shape[1]), piece.dtype)
    out = lax.dynamic_update_slice_in_dim(out, piece, me * rows, 0)
    for turn in range(1, size):
        other = lax.ppermute(piece, "dp", turned(size, size, 1, turn))
        out = lax.dynamic_update_slice_in_dim(out, other, (me - turn) % size * rows, 0)
    return out


def across_chips(array, line):
    mine, away = halves(array, line.chip % 2)
    return [mine, line.pair(away)]


def across_cores(array, line):
    mine, away = halves(array, line.core)
    return [mine, line.swap(away)]


def summed_dp(array, *others):
    size = lax.axis_size("dp")
    bits = size.bit_length() - 1
    for bit in range(bits):
        other = lax.ppermute(array, "dp", [(g, g ^ (1 << bit)) for g in range(size)])
        if bit == bits - 1:
            (other,) = after((other,), *others)
        array = add(array, other)
    return array


def summed_graph(array, line, bits):
    for bit in bits:
        pairs = [(g, g ^ (1 << bit)) for g in range(line.size)]
        array = add(array, lax.ppermute(array, "graph", pairs))
    return array


def local(
    edge_state,
    cotangent,
    edge_count,
    triplet_basis,
    triplet_in,
    triplet_out,
    down_weight,
    basis_weight,
    bilinear_weight,
    up_weight,
    first_weight,
    second_weight,
):
    edge_rows = edge_state[0]
    row_count, wide = edge_rows.shape
    line = Line()
    shards, chips = line.size, line.chips
    narrow = down_weight.shape[1]
    down_weight = down_weight.T
    basis = triplet_basis[0]
    basis_width, tri_rows = basis.shape
    slots = tri_rows // shards
    lanes = math.gcd(row_count, 256)
    stacked = narrow * (row_count // lanes)
    tile = math.gcd(row_count, 512)
    tiles = row_count // tile
    row_spec = pl.BlockSpec((tile, wide), lambda i: (i, 0))
    stack_spec = pl.BlockSpec((narrow * (tile // lanes), lanes), lambda i: (i, 0))
    rows_spec = whole(stacked, lanes)

    ends = jnp.stack([triplet_in.reshape(shards, 1, slots), triplet_out.reshape(shards, 1, slots)])
    triplet_specs = (
        [whole(2, shards, 1, slots)] * 2
        + [whole(basis_width, tri_rows)] * 2
        + [whole(basis_width, narrow)]
    )
    block_flops = 8 * slots * row_count * narrow

    down_rows, down_slope = call(
        down_kernel,
        (tiles,),
        [row_spec, whole(narrow, wide)],
        [stack_spec] * 2,
        [shape((stacked, lanes), BF16), shape((stacked, lanes), F32)],
        2 * row_count * wide * narrow,
        row_count * narrow,
    )(in_hbm(edge_rows), in_hbm(down_weight))

    slot_spec = whole(2, narrow, slots)
    slot_shape = pltpu.HBM((2, narrow, slots), BF16)

    ends, leaving = after((ends, basis), down_rows)
    ends_sibling = line.swap(ends)
    basis_sibling = line.swap(leaving)
    triplets = (ends, ends_sibling, basis, basis_sibling, basis_weight)

    def forward(turn, bits, rows, totals):
        total_shape = shape((stacked, lanes), F32)
        final = line.groups == 1 and bits == chips - 1
        out = call(
            forward_kernel,
            (),
            [SMEM, rows_spec] + triplet_specs + [rows_spec] * len(totals),
            [rows_spec] * 2 + [slot_spec] * 2,
            [pltpu.HBM((stacked, lanes), F32) if final else total_shape, total_shape]
            + [slot_shape] * 2,
            block_flops,
            aliases={7 + i: i for i in range(len(totals)) if i == 1 or not final},
            grant=FORWARD_GRANT,
        )(line.shard(turn, bits), rows, *triplets, *totals)
        return tuple(out[:2]), tuple(out[2:])

    def forward_line(turn, rows, totals, *others):
        arriving = [line.trade(rows, bits) for bits in range(1, chips)]
        totals, got = forward(turn, 0, rows, totals)
        kept = [got]
        for bits in range(1, chips):
            (rows,) = after((arriving[bits - 1],), *totals, *others)
            totals, got = forward(turn, bits, rows, totals)
            kept.append(got)
        return totals, kept

    first_turned, second_turned = after((first_weight, second_weight), down_rows)
    first_turned, second_turned = first_turned.T, second_turned.T
    totals, kept = forward_line(0, down_rows, (), first_turned, second_turned)
    if line.groups > 1:

        def forward_turn(carry, turn):
            rows, totals = carry
            rows = line.next_group(rows)
            totals, got = forward_line(turn, rows, totals)
            return (rows, totals), got

        (_, totals), more_kept = lax.scan(
            forward_turn, (down_rows, totals), jnp.arange(1, line.groups)
        )

    grad_rows = 2 * wide + 2 * narrow
    back_summed, back_gathered, dense_grads = call(
        dense_kernel,
        (tiles,),
        [
            SMEM,
            row_spec,
            row_spec,
            stack_spec,
            stack_spec,
            whole(narrow, narrow),
            whole(narrow, wide),
            whole(wide, wide),
            whole(wide, wide),
            whole(wide, wide),
            whole(wide, wide),
        ],
        [row_spec, stack_spec, whole(grad_rows, wide)],
        [
            pltpu.HBM((row_count, wide), BF16),
            shape((stacked, lanes), BF16),
            shape((grad_rows, wide), BF16),
        ],
        12 * row_count * wide * wide + 6 * row_count * wide * narrow,
        3 * row_count * wide,
        scratch=[pltpu.VMEM((grad_rows, wide), F32)],
        grant=DENSE_GRANT,
    )(
        edge_count,
        in_hbm(edge_rows),
        in_hbm(cotangent[0]),
        in_hbm(totals[0]) if line.groups == 1 else totals[0],
        line.swap(totals[1]),
        bilinear_weight,
        up_weight,
        in_hbm(first_weight),
        first_turned,
        in_hbm(second_weight),
        second_turned,
    )
    back_sibling = line.swap(back_gathered)

    def backward(turn, bits, kept, others=()):
        count = len(bits)
        (back,) = after((back_gathered,), *others)
        out = call(
            functools.partial(backward_kernel, count),
            (),
            [SMEM] + [rows_spec] * 2 + [slot_spec] * (2 * count) + triplet_specs[:2],
            [rows_spec] * count + [slot_spec] * count,
            [shape((stacked, lanes), BF16)] * count + [shape((2, narrow, slots), BF16)] * count,
            count * block_flops,
            grant=BACKWARD_GRANT,
        )(
            jnp.concatenate([line.shard(turn, one) for one in bits]),
            back,
            back_sibling,
            *[kept[one][0] for one in bits],
            *[kept[one][1] for one in bits],
            ends,
            ends_sibling,
        )
        return out[:count], out[count:]

    graph_bits = line.size.bit_length() - 1

    def backward_line(turn, kept, pieces=None):
        parts, others = [], ()
        last_coefs = near_coefs = ()
        if chips == 4:
            (last,), last_coefs = backward(turn, (3,), kept)
            passed = line.send(last, [(0, 1), (3, 2)])
            middle = line.send(last, [(1, 2), (2, 1)])
            others = (last,)
        if pieces is not None:
            pieces = add(*after(pieces, *others))
            others = (*others, pieces)
            arriving = dp_pieces(pieces)
        if chips == 4:
            (near, far), near_coefs = backward(turn, (1, 2), kept, others)
            (passed,) = after((passed,), far)
            if pieces is not None:
                pieces = add(*after(arriving, far))
                (far,) = after((far,), pieces)
            far = add(far, passed)
            (middle,) = after((middle,), far)
            (far,) = after((far,), middle)
            others = (far,)
            parts = [middle, line.trade(far, 2), line.trade(near, 1)]
        elif chips == 2:
            (near,), near_coefs = backward(turn, (1,), kept, others)
            parts = [line.trade(near, 1)]
        (own,), own_coefs = backward(turn, (0,), kept, others)
        if pieces is not None and chips < 4:
            pieces = add(*arriving)
        back_coefs = [*own_coefs, *near_coefs, *last_coefs]
        basis_grad = call(
            basis_kernel,
            (),
            [SMEM] + [slot_spec] * chips + triplet_specs[2:4],
            [whole(narrow, basis_width)],
            [shape((narrow, basis_width), F32)],
            4 * chips * slots * narrow * basis_width,
        )(
            jnp.concatenate([line.shard(turn, bits) for bits in range(chips)]),
            *back_coefs,
            basis,
            basis_sibling,
        )[0]
        return [own] + parts, basis_grad, pieces

    back_parts, basis_grad, dense_grads = backward_line(0, kept, across_cores(dense_grads, line))
    if chips > 1:
        dense_grads = add(*across_chips(dense_grads, line))
    dense_grads = summed_graph(dense_grads, line, range(2, graph_bits))
    if line.groups > 1:

        def backward_turn(carry, one):
            traveling, basis_grad = carry
            turn, got = one
            parts, more, _ = backward_line(turn, got)
            return (line.last_group(add(traveling, *parts)), basis_grad + more), None

        (traveling, basis_grad), _ = lax.scan(
            backward_turn,
            (jnp.zeros((stacked, lanes), BF16), basis_grad),
            (jnp.arange(1, line.groups), more_kept),
            reverse=True,
        )
        back_parts = back_parts + [traveling]

    small_rows = narrow + basis_width
    edge_grad, small_grads = call(
        functools.partial(final_kernel, len(back_parts)),
        (tiles,),
        [stack_spec] * len(back_parts)
        + [stack_spec, row_spec, row_spec, whole(narrow, wide), whole(narrow, basis_width)],
        [row_spec, whole(small_rows, wide)],
        [shape((row_count, wide), BF16), shape((small_rows, wide), BF16)],
        4 * row_count * wide * narrow,
        scratch=[pltpu.VMEM((small_rows, wide), F32)],
        grant=FINAL_GRANT,
    )(
        *back_parts,
        down_slope,
        edge_rows,
        back_summed,
        down_weight,
        basis_grad,
    )

    if chips > 1:
        dense_grads = joined(dense_grads, line.pair(dense_grads), line.chip % 2)
    dense_grads = dp_joined(dense_grads)
    dense_grads = joined(dense_grads, line.swap(dense_grads), line.core)
    scale = 1.0 / math.sqrt(lax.axis_size("dp") * shards * row_count)

    def scaled(source, *dims):
        return call(
            functools.partial(scale_kernel, scale),
            (),
            [whole(*source.shape)],
            [whole(*d) for d in dims],
            [shape(d, F32) for d in dims],
            source.size,
        )(source)

    first_grad, second_grad, up_grad, bilinear_grad = scaled(
        dense_grads, (wide, wide), (wide, wide), (narrow, wide), (narrow, narrow)
    )
    small_grads = add(*across_cores(small_grads, line))
    small_grads = summed_graph(small_grads, line, range(1, graph_bits))
    small_grads = summed_dp(small_grads, bilinear_grad)
    small_grads = joined(small_grads, line.swap(small_grads), line.core)
    down_grad, basis_grad = scaled(small_grads, (narrow, wide), (basis_width, narrow))
    return (
        edge_grad[None],
        down_grad.T,
        basis_grad,
        bilinear_grad,
        up_grad,
        first_grad,
        second_grad,
    )


def solution(mesh):
    in_specs = (
        P("dp", "graph", None),
        P("dp", "graph", None),
        P("dp", "graph"),
        P("dp", None, "graph"),
        P("dp", "graph"),
        P("dp", "graph"),
        P(),
        P(),
        P(),
        P(),
        P(),
        P(),
    )
    out_specs = (P("dp", "graph", None), P(), P(), P(), P(), P(), P())
    return jax.shard_map(local, mesh=mesh, in_specs=in_specs, out_specs=out_specs, check_vma=False)
```

```python
import functools
import math

import jax
import jax.numpy as jnp
from jax import lax
from jax.experimental import pallas as pl
from jax.experimental.pallas import tpu as pltpu
from jax.sharding import PartitionSpec as P

HALF = 0.7071067811865476
F32 = jnp.float32
BF16 = jnp.bfloat16
MIB = 1024 * 1024
FORWARD_GRANT = 10
BACKWARD_GRANT = 10
DENSE_GRANT = 18
FINAL_GRANT = 12


def contract(left, right, left_dim, right_dim):
    return lax.dot_general(
        left, right, (((left_dim,), (right_dim,)), ((), ())), preferred_element_type=F32
    )


def sigmoid(value):
    return 0.5 + 0.5 * jnp.tanh(0.5 * value)


def split_index(index_row, lanes):
    slots = index_row.shape[1]
    low = jnp.bitwise_and(index_row, lanes - 1)
    high = jnp.right_shift(index_row, lanes.bit_length() - 1)
    lane_ids = lax.broadcasted_iota(jnp.int32, (lanes, slots), 0)
    return high, jnp.where(lane_ids == low, 1.0, 0.0).astype(BF16)


def stack(rows, lanes):
    groups = rows.shape[1] // lanes
    return jnp.concatenate([rows[:, g * lanes : (g + 1) * lanes] for g in range(groups)], axis=0)


def unstack(rows, narrow):
    groups = rows.shape[0] // narrow
    return jnp.concatenate([rows[g * narrow : (g + 1) * narrow] for g in range(groups)], axis=1)


def pick_rows(stacked, high, lane_hot, narrow):
    groups = stacked.shape[0] // narrow
    every = contract(stacked, lane_hot, 1, 0)
    picked = jnp.where(high == 0, every[:narrow], 0.0)
    for g in range(1, groups):
        picked = jnp.where(high == g, every[g * narrow : (g + 1) * narrow], picked)
    return picked


def place_rows(values, high, lane_hot, groups):
    zero = jnp.zeros((), values.dtype)
    spread = jnp.concatenate([jnp.where(high == g, values, zero) for g in range(groups)], axis=0)
    return contract(spread.astype(BF16), lane_hot, 1, 1)


def down_kernel(edge_ref, weight_ref, rows_ref, slope_ref):
    lanes = rows_ref.shape[1]
    pre = contract(edge_ref[...], weight_ref[...], 1, 1).T
    logistic = sigmoid(pre)
    rows_ref[...] = stack((pre * logistic).astype(BF16), lanes)
    slope_ref[...] = stack(logistic * (1.0 + pre * (1.0 - logistic)), lanes)


def forward_kernel(shard_ref, rows_ref, *refs):
    rows = rows_ref[...]
    ends, basis, weight_ref = refs[:2], refs[2:4], refs[4]
    totals, fetched_ref, coef_ref = refs[-4:-2], refs[-2], refs[-1]
    shard = shard_ref[0]
    narrow = weight_ref.shape[1]
    groups = totals[0].shape[0] // narrow
    lanes = totals[0].shape[1]
    slots = ends[0].shape[3]
    at = pl.ds(pl.multiple_of(shard * slots, slots), slots)
    for i in range(2):
        high, lane_hot = split_index(ends[i][0, shard], lanes)
        fetched = pick_rows(rows, high, lane_hot, narrow)
        fetched_ref[i] = fetched.astype(BF16)
        coef = contract(weight_ref[...], basis[i][:, at], 0, 0)
        coef_ref[i] = coef.astype(BF16)
        high, lane_hot = split_index(ends[i][1, shard], lanes)
        placed = place_rows(coef * fetched, high, lane_hot, groups)
        if len(refs) == 11:
            placed += refs[5 + i][...]
        totals[i][...] = placed


def dense_kernel(
    count_ref,
    edge_ref,
    cotangent_ref,
    gathered_ref,
    more_ref,
    bilinear_ref,
    up_ref,
    first_ref,
    first_turned_ref,
    second_ref,
    second_turned_ref,
    summed_ref,
    back_ref,
    grads_ref,
    total,
):
    step = pl.program_id(0)
    tile, wide = edge_ref.shape
    narrow = bilinear_ref.shape[0]
    lanes = gathered_ref.shape[1]

    @pl.when(step == 0)
    def _():
        total[...] = jnp.zeros_like(total)

    gathered = unstack((gathered_ref[...] + more_ref[...]).astype(BF16), narrow)
    mixed = contract(bilinear_ref[...], gathered, 0, 0).astype(BF16)
    pre_up = contract(mixed, up_ref[...], 0, 0)
    up_logistic = sigmoid(pre_up)
    summed_half = (edge_ref[...].astype(F32) + pre_up * up_logistic).astype(BF16)
    pre_first = contract(summed_half, first_ref[...], 1, 0)
    first_logistic = sigmoid(pre_first)
    first_rows = (pre_first * first_logistic).astype(BF16)
    pre_second = contract(first_rows, second_ref[...], 1, 0)
    logistic = sigmoid(pre_second)
    row_ids = step * tile + lax.broadcasted_iota(jnp.int32, (tile, 1), 0)
    live = jnp.where(row_ids < count_ref[0, 0], HALF, 0.0)
    back_top = cotangent_ref[...].astype(F32) * live
    back_second = (back_top * (logistic * (1.0 + pre_second * (1.0 - logistic)))).astype(BF16)
    slope = first_logistic * (1.0 + pre_first * (1.0 - first_logistic))
    back_first = (contract(back_second, second_turned_ref[...], 1, 0) * slope).astype(BF16)
    back_summed = back_top + contract(back_first, first_turned_ref[...], 1, 0)
    summed_ref[...] = back_summed.astype(BF16)
    slope = up_logistic * (1.0 + pre_up * (1.0 - up_logistic))
    back_up = (back_summed * slope).astype(BF16)
    back_mixed = contract(back_up, up_ref[...], 1, 1).T.astype(BF16)
    back_ref[...] = stack(contract(bilinear_ref[...], back_mixed, 1, 0).astype(BF16), lanes)
    total[:wide] += contract(summed_half, back_first, 0, 0)
    total[wide : 2 * wide] += contract(first_rows, back_second, 0, 0)
    total[2 * wide : 2 * wide + narrow] += contract(mixed, back_up, 1, 0)
    total[2 * wide + narrow :, :narrow] += contract(gathered, back_mixed, 1, 1)

    @pl.when(step == pl.num_programs(0) - 1)
    def _():
        grads_ref[...] = total[...].astype(BF16)


def backward_kernel(count, shards_ref, own_ref, sibling_ref, *refs):
    fetched, coefs, ends = refs[:count], refs[count : 2 * count], refs[2 * count : 2 * count + 2]
    parts, back_coefs = refs[2 * count + 2 : 3 * count + 2], refs[3 * count + 2 :]
    narrow = fetched[0].shape[1]
    groups = own_ref.shape[0] // narrow
    lanes = own_ref.shape[1]
    for s in range(count):
        shard = shards_ref[s]
        part = None
        for i, back_ref in enumerate((own_ref, sibling_ref)):
            high, lane_hot = split_index(ends[i][1, shard], lanes)
            message = pick_rows(back_ref[...], high, lane_hot, narrow)
            back_coefs[s][i] = (message * fetched[s][i].astype(F32)).astype(BF16)
            high, lane_hot = split_index(ends[i][0, shard], lanes)
            placed = place_rows(message * coefs[s][i].astype(F32), high, lane_hot, groups)
            part = placed if part is None else part + placed
        parts[s][...] = part.astype(BF16)


def basis_kernel(shards_ref, *refs):
    back_coefs, basis, grad_ref = refs[:-3], refs[-3:-1], refs[-1]
    slots = back_coefs[0].shape[2]
    grad = jnp.zeros(grad_ref.shape, F32)
    for s, ref in enumerate(back_coefs):
        at = pl.ds(pl.multiple_of(shards_ref[s] * slots, slots), slots)
        for i in range(2):
            grad += contract(ref[i], basis[i][:, at], 1, 1)
    grad_ref[...] = grad


def final_kernel(count, *refs):
    parts = refs[:count]
    slope_ref, edge_ref, summed_ref, weight_ref, basis_ref, edge_grad_ref, grads_ref, total = refs[
        count:
    ]
    step = pl.program_id(0)
    narrow = weight_ref.shape[0]
    basis_width = basis_ref.shape[1]

    @pl.when(step == 0)
    def _():
        total[...] = jnp.zeros_like(total)

    back_down = parts[0][...].astype(F32)
    for part in parts[1:]:
        back_down += part[...].astype(F32)
    back_pre = unstack((back_down * slope_ref[...]).astype(BF16), narrow)
    total[:narrow] += contract(back_pre, edge_ref[...], 1, 0)
    edge_grad_ref[...] = (
        summed_ref[...].astype(F32) + contract(back_pre, weight_ref[...], 0, 0)
    ).astype(BF16)

    @pl.when(step == pl.num_programs(0) - 1)
    def _():
        total[narrow : narrow + basis_width, :narrow] = basis_ref[...].T
        grads_ref[...] = total[...].astype(BF16)


def scale_kernel(scale, source_ref, *outs):
    row = 0
    for out in outs:
        rows, columns = out.shape
        out[...] = source_ref[row : row + rows, :columns].astype(F32) * scale
        row += rows


def call(kernel, grid, in_specs, out_specs, out_shape, flops, transcendentals=0, scratch=(), aliases=None, grant=8):
    def run(*operands):
        size = sum(x.size * x.dtype.itemsize for x in operands)
        size += sum(math.prod(x.shape) * x.dtype.itemsize for x in out_shape)
        return pl.pallas_call(
            kernel,
            grid=grid,
            in_specs=in_specs,
            out_specs=out_specs,
            out_shape=out_shape,
            scratch_shapes=scratch,
            input_output_aliases=aliases or {},
            compiler_params=pltpu.CompilerParams(vmem_limit_bytes=grant * MIB),
            cost_estimate=pl.CostEstimate(
                flops=flops, bytes_accessed=size, transcendentals=transcendentals
            ),
        )(*operands)

    return run


def whole(*shape):
    return pl.BlockSpec(shape, lambda *_: (0,) * len(shape))


SMEM = pl.BlockSpec(memory_space=pltpu.SMEM)


def in_hbm(array):
    return pltpu.with_memory_space_constraint(array, pltpu.HBM)


def shape(dims, dtype):
    return jax.ShapeDtypeStruct(dims, dtype)


def turned(count, size, stride, turn):
    pairs = []
    for g in range(count):
        place = g // stride % size
        pairs.append((g, g + ((place + turn) % size - place) * stride))
    return pairs


class Line:
    cores = 2

    def __init__(self):
        self.size = lax.axis_size("graph")
        self.chips = math.gcd(self.size // self.cores, 4)
        self.span = self.chips * self.cores
        self.groups = self.size // self.span
        me = lax.axis_index("graph")
        self.core = me % self.cores
        self.chip = me // self.cores % self.chips
        self.group = me // self.span

    def send(self, array, moves):
        pairs = [
            (base + one * self.cores + core, base + other * self.cores + core)
            for base in range(0, self.size, self.span)
            for one, other in moves
            for core in range(self.cores)
        ]
        return lax.ppermute(array, "graph", pairs)

    def trade(self, array, bits):
        return self.send(array, [(chip, chip ^ bits) for chip in range(self.chips)])

    def pair(self, array):
        return lax.ppermute(array, "graph", [(g, g ^ 2) for g in range(self.size)])

    def swap(self, array):
        return lax.ppermute(array, "graph", [(g, g ^ 1) for g in range(self.size)])

    def next_group(self, array):
        return lax.ppermute(array, "graph", turned(self.size, self.groups, self.span, -1))

    def last_group(self, array):
        return lax.ppermute(array, "graph", turned(self.size, self.groups, self.span, 1))

    def shard(self, turn, bits):
        group = (self.group + turn) % self.groups
        shard = group * self.span + (self.chip ^ bits) * self.cores + self.core
        return shard.astype(jnp.int32).reshape(1)


def add(*arrays):
    return sum(a.astype(F32) for a in arrays).astype(BF16)


def after(arrays, *others):
    return lax.optimization_barrier((tuple(arrays), others))[0]


def halves(array, place):
    rows = array.shape[0] // 2
    first = place == 0
    return (
        jnp.where(first, array[:rows], array[rows:]),
        jnp.where(first, array[rows:], array[:rows]),
    )


def joined(mine, other, place):
    return jnp.where(
        place == 0, jnp.concatenate([mine, other]), jnp.concatenate([other, mine])
    )


def piece_of(array, size, place):
    rows = array.shape[0] // size
    return lax.dynamic_slice_in_dim(array, place * rows, rows, 0)


def dp_pieces(array):
    size, me = lax.axis_size("dp"), lax.axis_index("dp")
    arrived = [piece_of(array, size, me)]
    for turn in range(1, size):
        away = piece_of(array, size, (me + turn) % size)
        arrived.append(lax.ppermute(away, "dp", turned(size, size, 1, turn)))
    return arrived


def dp_joined(piece):
    size, me = lax.axis_size("dp"), lax.axis_index("dp")
    rows = piece.shape[0]
    out = jnp.zeros((size * rows, piece.shape[1]), piece.dtype)
    out = lax.dynamic_update_slice_in_dim(out, piece, me * rows, 0)
    for turn in range(1, size):
        other = lax.ppermute(piece, "dp", turned(size, size, 1, turn))
        out = lax.dynamic_update_slice_in_dim(out, other, (me - turn) % size * rows, 0)
    return out


def across_chips(array, line):
    mine, away = halves(array, line.chip % 2)
    return [mine, line.pair(away)]


def across_cores(array, line):
    mine, away = halves(array, line.core)
    return [mine, line.swap(away)]


def summed_dp(array, *others):
    size = lax.axis_size("dp")
    bits = size.bit_length() - 1
    for bit in range(bits):
        other = lax.ppermute(array, "dp", [(g, g ^ (1 << bit)) for g in range(size)])
        if bit == bits - 1:
            (other,) = after((other,), *others)
        array = add(array, other)
    return array


def summed_graph(array, line, bits, *others):
    for bit in bits:
        pairs = [(g, g ^ (1 << bit)) for g in range(line.size)]
        (other,) = after((lax.ppermute(array, "graph", pairs),), *others)
        array = add(array, other)
    return array


def local(
    edge_state,
    cotangent,
    edge_count,
    triplet_basis,
    triplet_in,
    triplet_out,
    down_weight,
    basis_weight,
    bilinear_weight,
    up_weight,
    first_weight,
    second_weight,
):
    edge_rows = edge_state[0]
    row_count, wide = edge_rows.shape
    line = Line()
    shards, chips = line.size, line.chips
    narrow = down_weight.shape[1]
    down_weight = down_weight.T
    basis = triplet_basis[0]
    basis_width, tri_rows = basis.shape
    slots = tri_rows // shards
    lanes = math.gcd(row_count, 256)
    stacked = narrow * (row_count // lanes)
    tile = math.gcd(row_count, 512)
    tiles = row_count // tile
    row_spec = pl.BlockSpec((tile, wide), lambda i: (i, 0))
    stack_spec = pl.BlockSpec((narrow * (tile // lanes), lanes), lambda i: (i, 0))
    rows_spec = whole(stacked, lanes)

    ends = jnp.stack([triplet_in.reshape(shards, 1, slots), triplet_out.reshape(shards, 1, slots)])
    triplet_specs = (
        [whole(2, shards, 1, slots)] * 2
        + [whole(basis_width, tri_rows)] * 2
        + [whole(basis_width, narrow)]
    )
    block_flops = 8 * slots * row_count * narrow

    down_rows, down_slope = call(
        down_kernel,
        (tiles,),
        [row_spec, whole(narrow, wide)],
        [stack_spec] * 2,
        [shape((stacked, lanes), BF16), shape((stacked, lanes), F32)],
        2 * row_count * wide * narrow,
        row_count * narrow,
    )(in_hbm(edge_rows), in_hbm(down_weight))

    slot_spec = whole(2, narrow, slots)
    slot_shape = pltpu.HBM((2, narrow, slots), BF16)

    ends, leaving = after((ends, basis), down_rows)
    ends_sibling = line.swap(ends)
    basis_sibling = line.swap(leaving)
    triplets = (ends, ends_sibling, basis, basis_sibling, basis_weight)

    def forward(turn, bits, rows, totals):
        total_shape = shape((stacked, lanes), F32)
        final = line.groups == 1 and bits == chips - 1
        out = call(
            forward_kernel,
            (),
            [SMEM, rows_spec] + triplet_specs + [rows_spec] * len(totals),
            [rows_spec] * 2 + [slot_spec] * 2,
            [pltpu.HBM((stacked, lanes), F32) if final else total_shape, total_shape]
            + [slot_shape] * 2,
            block_flops,
            aliases={7 + i: i for i in range(len(totals)) if i == 1 or not final},
            grant=FORWARD_GRANT,
        )(line.shard(turn, bits), rows, *triplets, *totals)
        return tuple(out[:2]), tuple(out[2:])

    def forward_line(turn, rows, totals, *others):
        arriving = [line.trade(rows, bits) for bits in range(1, chips)]
        totals, got = forward(turn, 0, rows, totals)
        kept = [got]
        for bits in range(1, chips):
            (rows,) = after((arriving[bits - 1],), *totals, *others)
            totals, got = forward(turn, bits, rows, totals)
            kept.append(got)
        return totals, kept

    first_turned, second_turned = after((first_weight, second_weight), down_rows)
    first_turned, second_turned = first_turned.T, second_turned.T
    totals, kept = forward_line(0, down_rows, (), first_turned, second_turned)
    if line.groups > 1:

        def forward_turn(carry, turn):
            rows, totals = carry
            rows = line.next_group(rows)
            totals, got = forward_line(turn, rows, totals)
            return (rows, totals), got

        (_, totals), more_kept = lax.scan(
            forward_turn, (down_rows, totals), jnp.arange(1, line.groups)
        )

    grad_rows = 2 * wide + 2 * narrow
    back_summed, back_gathered, dense_grads = call(
        dense_kernel,
        (tiles,),
        [
            SMEM,
            row_spec,
            row_spec,
            stack_spec,
            stack_spec,
            whole(narrow, narrow),
            whole(narrow, wide),
            whole(wide, wide),
            whole(wide, wide),
            whole(wide, wide),
            whole(wide, wide),
        ],
        [row_spec, stack_spec, whole(grad_rows, wide)],
        [
            pltpu.HBM((row_count, wide), BF16),
            shape((stacked, lanes), BF16),
            shape((grad_rows, wide), BF16),
        ],
        12 * row_count * wide * wide + 6 * row_count * wide * narrow,
        3 * row_count * wide,
        scratch=[pltpu.VMEM((grad_rows, wide), F32)],
        grant=DENSE_GRANT,
    )(
        edge_count,
        in_hbm(edge_rows),
        in_hbm(cotangent[0]),
        in_hbm(totals[0]) if line.groups == 1 else totals[0],
        line.swap(totals[1]),
        bilinear_weight,
        up_weight,
        in_hbm(first_weight),
        first_turned,
        in_hbm(second_weight),
        second_turned,
    )
    back_sibling = line.swap(back_gathered)

    def backward(turn, bits, kept, others=()):
        count = len(bits)
        (back,) = after((back_gathered,), *others)
        out = call(
            functools.partial(backward_kernel, count),
            (),
            [SMEM] + [rows_spec] * 2 + [slot_spec] * (2 * count) + triplet_specs[:2],
            [rows_spec] * count + [slot_spec] * count,
            [shape((stacked, lanes), BF16)] * count + [shape((2, narrow, slots), BF16)] * count,
            count * block_flops,
            grant=BACKWARD_GRANT,
        )(
            jnp.concatenate([line.shard(turn, one) for one in bits]),
            back,
            back_sibling,
            *[kept[one][0] for one in bits],
            *[kept[one][1] for one in bits],
            ends,
            ends_sibling,
        )
        return out[:count], out[count:]

    graph_bits = line.size.bit_length() - 1

    def backward_line(turn, kept, pieces=None):
        parts, others = [], ()
        last_coefs = near_coefs = ()
        if chips == 4:
            (last,), last_coefs = backward(turn, (3,), kept)
            passed = line.send(last, [(0, 1), (3, 2)])
            middle = line.send(last, [(1, 2), (2, 1)])
            others = (last,)
        if pieces is not None:
            pieces = add(*after(pieces, *others))
            others = (*others, pieces)
            arriving = dp_pieces(pieces)
        if chips == 4:
            (near, far), near_coefs = backward(turn, (1, 2), kept, others)
            (passed,) = after((passed,), far)
            if pieces is not None:
                pieces = add(*after(arriving, far))
                (far,) = after((far,), pieces)
            far = add(far, passed)
            (middle,) = after((middle,), far)
            (far,) = after((far,), middle)
            others = (far,)
            parts = [middle, line.trade(far, 2), line.trade(near, 1)]
        elif chips == 2:
            (near,), near_coefs = backward(turn, (1,), kept, others)
            parts = [line.trade(near, 1)]
        (own,), own_coefs = backward(turn, (0,), kept, others)
        if pieces is not None and chips < 4:
            pieces = add(*arriving)
        back_coefs = [*own_coefs, *near_coefs, *last_coefs]
        basis_grad = call(
            basis_kernel,
            (),
            [SMEM] + [slot_spec] * chips + triplet_specs[2:4],
            [whole(narrow, basis_width)],
            [shape((narrow, basis_width), F32)],
            4 * chips * slots * narrow * basis_width,
        )(
            jnp.concatenate([line.shard(turn, bits) for bits in range(chips)]),
            *back_coefs,
            basis,
            basis_sibling,
        )[0]
        return [own] + parts, basis_grad, pieces

    back_parts, basis_grad, dense_grads = backward_line(0, kept, across_cores(dense_grads, line))
    if chips > 1:
        dense_grads = add(*after(across_chips(dense_grads, line), basis_grad))
    if line.groups > 1:

        def backward_turn(carry, one):
            traveling, basis_grad = carry
            turn, got = one
            parts, more, _ = backward_line(turn, got)
            return (line.last_group(add(traveling, *parts)), basis_grad + more), None

        (traveling, basis_grad), _ = lax.scan(
            backward_turn,
            (jnp.zeros((stacked, lanes), BF16), basis_grad),
            (jnp.arange(1, line.groups), more_kept),
            reverse=True,
        )
        back_parts = back_parts + [traveling]

    small_rows = narrow + basis_width
    edge_grad, small_grads = call(
        functools.partial(final_kernel, len(back_parts)),
        (tiles,),
        [stack_spec] * len(back_parts)
        + [stack_spec, row_spec, row_spec, whole(narrow, wide), whole(narrow, basis_width)],
        [row_spec, whole(small_rows, wide)],
        [shape((row_count, wide), BF16), shape((small_rows, wide), BF16)],
        4 * row_count * wide * narrow,
        scratch=[pltpu.VMEM((small_rows, wide), F32)],
        grant=FINAL_GRANT,
    )(
        *back_parts,
        down_slope,
        edge_rows,
        back_summed,
        down_weight,
        basis_grad,
    )

    dense_grads = summed_graph(dense_grads, line, range(2, graph_bits), small_grads)
    if chips > 1:
        dense_grads = joined(dense_grads, line.pair(dense_grads), line.chip % 2)
    dense_grads = dp_joined(dense_grads)
    dense_grads = joined(dense_grads, line.swap(dense_grads), line.core)
    scale = 1.0 / math.sqrt(lax.axis_size("dp") * shards * row_count)

    def scaled(source, *dims):
        return call(
            functools.partial(scale_kernel, scale),
            (),
            [whole(*source.shape)],
            [whole(*d) for d in dims],
            [shape(d, F32) for d in dims],
            source.size,
        )(source)

    first_grad, second_grad, up_grad, bilinear_grad = scaled(
        dense_grads, (wide, wide), (wide, wide), (narrow, wide), (narrow, narrow)
    )
    small_grads = add(*across_cores(small_grads, line))
    small_grads = summed_graph(small_grads, line, range(1, graph_bits))
    small_grads = summed_dp(small_grads, bilinear_grad)
    small_grads = joined(small_grads, line.swap(small_grads), line.core)
    down_grad, basis_grad = scaled(small_grads, (narrow, wide), (basis_width, narrow))
    return (
        edge_grad[None],
        down_grad.T,
        basis_grad,
        bilinear_grad,
        up_grad,
        first_grad,
        second_grad,
    )


def solution(mesh):
    in_specs = (
        P("dp", "graph", None),
        P("dp", "graph", None),
        P("dp", "graph"),
        P("dp", None, "graph"),
        P("dp", "graph"),
        P("dp", "graph"),
        P(),
        P(),
        P(),
        P(),
        P(),
        P(),
    )
    out_specs = (P("dp", "graph", None), P(), P(), P(), P(), P(), P())
    return jax.shard_map(local, mesh=mesh, in_specs=in_specs, out_specs=out_specs, check_vma=False)
```

```python
import functools
import math

import jax
import jax.numpy as jnp
from jax import lax
from jax.experimental import pallas as pl
from jax.experimental.pallas import tpu as pltpu
from jax.sharding import PartitionSpec as P

HALF = 0.7071067811865476
F32 = jnp.float32
BF16 = jnp.bfloat16
MIB = 1024 * 1024
FORWARD_GRANT = 10
BACKWARD_GRANT = 10
DENSE_GRANT = 18
FINAL_GRANT = 12


def contract(left, right, left_dim, right_dim):
    return lax.dot_general(
        left, right, (((left_dim,), (right_dim,)), ((), ())), preferred_element_type=F32
    )


def sigmoid(value):
    return 0.5 + 0.5 * jnp.tanh(0.5 * value)


def split_index(index_row, lanes):
    slots = index_row.shape[1]
    low = jnp.bitwise_and(index_row, lanes - 1)
    high = jnp.right_shift(index_row, lanes.bit_length() - 1)
    lane_ids = lax.broadcasted_iota(jnp.int32, (lanes, slots), 0)
    return high, jnp.where(lane_ids == low, 1.0, 0.0).astype(BF16)


def stack(rows, lanes):
    groups = rows.shape[1] // lanes
    return jnp.concatenate([rows[:, g * lanes : (g + 1) * lanes] for g in range(groups)], axis=0)


def unstack(rows, narrow):
    groups = rows.shape[0] // narrow
    return jnp.concatenate([rows[g * narrow : (g + 1) * narrow] for g in range(groups)], axis=1)


def pick_rows(stacked, high, lane_hot, narrow):
    groups = stacked.shape[0] // narrow
    every = contract(stacked, lane_hot, 1, 0)
    picked = jnp.where(high == 0, every[:narrow], 0.0)
    for g in range(1, groups):
        picked = jnp.where(high == g, every[g * narrow : (g + 1) * narrow], picked)
    return picked


def place_rows(values, high, lane_hot, groups):
    zero = jnp.zeros((), values.dtype)
    spread = jnp.concatenate([jnp.where(high == g, values, zero) for g in range(groups)], axis=0)
    return contract(spread.astype(BF16), lane_hot, 1, 1)


def down_kernel(edge_ref, weight_ref, rows_ref, slope_ref):
    lanes = rows_ref.shape[1]
    pre = contract(edge_ref[...], weight_ref[...], 1, 1).T
    logistic = sigmoid(pre)
    rows_ref[...] = stack((pre * logistic).astype(BF16), lanes)
    slope_ref[...] = stack(logistic * (1.0 + pre * (1.0 - logistic)), lanes)


def forward_kernel(shard_ref, rows_ref, *refs):
    rows = rows_ref[...]
    ends, basis, weight_ref = refs[:2], refs[2:4], refs[4]
    totals, fetched_ref, coef_ref = refs[-4:-2], refs[-2], refs[-1]
    shard = shard_ref[0]
    narrow = weight_ref.shape[1]
    groups = totals[0].shape[0] // narrow
    lanes = totals[0].shape[1]
    slots = ends[0].shape[3]
    at = pl.ds(pl.multiple_of(shard * slots, slots), slots)
    for i in range(2):
        high, lane_hot = split_index(ends[i][0, shard], lanes)
        fetched = pick_rows(rows, high, lane_hot, narrow)
        fetched_ref[i] = fetched.astype(BF16)
        coef = contract(weight_ref[...], basis[i][:, at], 0, 0)
        coef_ref[i] = coef.astype(BF16)
        high, lane_hot = split_index(ends[i][1, shard], lanes)
        placed = place_rows(coef * fetched, high, lane_hot, groups)
        if len(refs) == 11:
            placed += refs[5 + i][...]
        totals[i][...] = placed


def dense_kernel(
    count_ref,
    edge_ref,
    cotangent_ref,
    gathered_ref,
    more_ref,
    bilinear_ref,
    up_ref,
    first_ref,
    first_turned_ref,
    second_ref,
    second_turned_ref,
    summed_ref,
    back_ref,
    grads_ref,
    total,
):
    step = pl.program_id(0)
    tile, wide = edge_ref.shape
    narrow = bilinear_ref.shape[0]
    lanes = gathered_ref.shape[1]

    @pl.when(step == 0)
    def _():
        total[...] = jnp.zeros_like(total)

    gathered = unstack((gathered_ref[...] + more_ref[...]).astype(BF16), narrow)
    mixed = contract(bilinear_ref[...], gathered, 0, 0).astype(BF16)
    pre_up = contract(mixed, up_ref[...], 0, 0)
    up_logistic = sigmoid(pre_up)
    summed_half = (edge_ref[...].astype(F32) + pre_up * up_logistic).astype(BF16)
    pre_first = contract(summed_half, first_ref[...], 1, 0)
    first_logistic = sigmoid(pre_first)
    first_rows = (pre_first * first_logistic).astype(BF16)
    pre_second = contract(first_rows, second_ref[...], 1, 0)
    logistic = sigmoid(pre_second)
    row_ids = step * tile + lax.broadcasted_iota(jnp.int32, (tile, 1), 0)
    live = jnp.where(row_ids < count_ref[0], HALF, 0.0)
    back_top = cotangent_ref[...].astype(F32) * live
    back_second = (back_top * (logistic * (1.0 + pre_second * (1.0 - logistic)))).astype(BF16)
    slope = first_logistic * (1.0 + pre_first * (1.0 - first_logistic))
    back_first = (contract(back_second, second_turned_ref[...], 1, 0) * slope).astype(BF16)
    back_summed = back_top + contract(back_first, first_turned_ref[...], 1, 0)
    summed_ref[...] = back_summed.astype(BF16)
    slope = up_logistic * (1.0 + pre_up * (1.0 - up_logistic))
    back_up = (back_summed * slope).astype(BF16)
    back_mixed = contract(back_up, up_ref[...], 1, 1).T.astype(BF16)
    back_ref[...] = stack(contract(bilinear_ref[...], back_mixed, 1, 0).astype(BF16), lanes)
    total[:wide] += contract(summed_half, back_first, 0, 0)
    total[wide : 2 * wide] += contract(first_rows, back_second, 0, 0)
    total[2 * wide : 2 * wide + narrow] += contract(mixed, back_up, 1, 0)
    total[2 * wide + narrow :, :narrow] += contract(gathered, back_mixed, 1, 1)

    @pl.when(step == pl.num_programs(0) - 1)
    def _():
        rows = total.shape[0] // 2
        core = count_ref[1]
        for i, place in enumerate((core, 1 - core)):
            at = pl.ds(pl.multiple_of(place * rows, 16), rows)
            grads_ref[i * rows : (i + 1) * rows, :] = total[at, :].astype(BF16)


def backward_kernel(count, shards_ref, own_ref, sibling_ref, *refs):
    fetched, coefs, ends = refs[:count], refs[count : 2 * count], refs[2 * count : 2 * count + 2]
    parts, back_coefs = refs[2 * count + 2 : 3 * count + 2], refs[3 * count + 2 :]
    narrow = fetched[0].shape[1]
    groups = own_ref.shape[0] // narrow
    lanes = own_ref.shape[1]
    for s in range(count):
        shard = shards_ref[s]
        part = None
        for i, back_ref in enumerate((own_ref, sibling_ref)):
            high, lane_hot = split_index(ends[i][1, shard], lanes)
            message = pick_rows(back_ref[...], high, lane_hot, narrow)
            back_coefs[s][i] = (message * fetched[s][i].astype(F32)).astype(BF16)
            high, lane_hot = split_index(ends[i][0, shard], lanes)
            placed = place_rows(message * coefs[s][i].astype(F32), high, lane_hot, groups)
            part = placed if part is None else part + placed
        parts[s][...] = part.astype(BF16)


def basis_kernel(shards_ref, *refs):
    back_coefs, basis, grad_ref = refs[:-3], refs[-3:-1], refs[-1]
    slots = back_coefs[0].shape[2]
    grad = jnp.zeros(grad_ref.shape, F32)
    for s, ref in enumerate(back_coefs):
        at = pl.ds(pl.multiple_of(shards_ref[s] * slots, slots), slots)
        for i in range(2):
            grad += contract(ref[i], basis[i][:, at], 1, 1)
    grad_ref[...] = grad


def final_kernel(count, *refs):
    parts = refs[:count]
    slope_ref, edge_ref, summed_ref, weight_ref, basis_ref, edge_grad_ref, grads_ref, total = refs[
        count:
    ]
    step = pl.program_id(0)
    narrow = weight_ref.shape[0]
    basis_width = basis_ref.shape[1]

    @pl.when(step == 0)
    def _():
        total[...] = jnp.zeros_like(total)

    back_down = parts[0][...].astype(F32)
    for part in parts[1:]:
        back_down += part[...].astype(F32)
    back_pre = unstack((back_down * slope_ref[...]).astype(BF16), narrow)
    total[:narrow] += contract(back_pre, edge_ref[...], 1, 0)
    edge_grad_ref[...] = (
        summed_ref[...].astype(F32) + contract(back_pre, weight_ref[...], 0, 0)
    ).astype(BF16)

    @pl.when(step == pl.num_programs(0) - 1)
    def _():
        total[narrow : narrow + basis_width, :narrow] = basis_ref[...].T
        grads_ref[...] = total[...].astype(BF16)


def scale_kernel(scale, source_ref, *outs):
    row = 0
    for out in outs:
        rows, columns = out.shape
        out[...] = source_ref[row : row + rows, :columns].astype(F32) * scale
        row += rows


def call(kernel, grid, in_specs, out_specs, out_shape, flops, transcendentals=0, scratch=(), aliases=None, grant=8):
    def run(*operands):
        size = sum(x.size * x.dtype.itemsize for x in operands)
        size += sum(math.prod(x.shape) * x.dtype.itemsize for x in out_shape)
        return pl.pallas_call(
            kernel,
            grid=grid,
            in_specs=in_specs,
            out_specs=out_specs,
            out_shape=out_shape,
            scratch_shapes=scratch,
            input_output_aliases=aliases or {},
            compiler_params=pltpu.CompilerParams(vmem_limit_bytes=grant * MIB),
            cost_estimate=pl.CostEstimate(
                flops=flops, bytes_accessed=size, transcendentals=transcendentals
            ),
        )(*operands)

    return run


def whole(*shape):
    return pl.BlockSpec(shape, lambda *_: (0,) * len(shape))


SMEM = pl.BlockSpec(memory_space=pltpu.SMEM)


def in_hbm(array):
    return pltpu.with_memory_space_constraint(array, pltpu.HBM)


def shape(dims, dtype):
    return jax.ShapeDtypeStruct(dims, dtype)


def turned(count, size, stride, turn):
    pairs = []
    for g in range(count):
        place = g // stride % size
        pairs.append((g, g + ((place + turn) % size - place) * stride))
    return pairs


class Line:
    cores = 2

    def __init__(self):
        self.size = lax.axis_size("graph")
        self.chips = math.gcd(self.size // self.cores, 4)
        self.span = self.chips * self.cores
        self.groups = self.size // self.span
        me = lax.axis_index("graph")
        self.core = me % self.cores
        self.chip = me // self.cores % self.chips
        self.group = me // self.span

    def send(self, array, moves):
        pairs = [
            (base + one * self.cores + core, base + other * self.cores + core)
            for base in range(0, self.size, self.span)
            for one, other in moves
            for core in range(self.cores)
        ]
        return lax.ppermute(array, "graph", pairs)

    def trade(self, array, bits):
        return self.send(array, [(chip, chip ^ bits) for chip in range(self.chips)])

    def pair(self, array):
        return lax.ppermute(array, "graph", [(g, g ^ 2) for g in range(self.size)])

    def swap(self, array):
        return lax.ppermute(array, "graph", [(g, g ^ 1) for g in range(self.size)])

    def next_group(self, array):
        return lax.ppermute(array, "graph", turned(self.size, self.groups, self.span, -1))

    def last_group(self, array):
        return lax.ppermute(array, "graph", turned(self.size, self.groups, self.span, 1))

    def shard(self, turn, bits):
        group = (self.group + turn) % self.groups
        shard = group * self.span + (self.chip ^ bits) * self.cores + self.core
        return shard.astype(jnp.int32).reshape(1)


def add(*arrays):
    return sum(a.astype(F32) for a in arrays).astype(BF16)


def after(arrays, *others):
    return lax.optimization_barrier((tuple(arrays), others))[0]


def halves(array, place):
    rows = array.shape[0] // 2
    first = place == 0
    return (
        jnp.where(first, array[:rows], array[rows:]),
        jnp.where(first, array[rows:], array[:rows]),
    )


def joined(mine, other, place):
    return jnp.where(
        place == 0, jnp.concatenate([mine, other]), jnp.concatenate([other, mine])
    )


def piece_of(array, size, place):
    rows = array.shape[0] // size
    return lax.dynamic_slice_in_dim(array, place * rows, rows, 0)


def dp_pieces(array):
    size, me = lax.axis_size("dp"), lax.axis_index("dp")
    arrived = [piece_of(array, size, me)]
    for turn in range(1, size):
        away = piece_of(array, size, (me + turn) % size)
        arrived.append(lax.ppermute(away, "dp", turned(size, size, 1, turn)))
    return arrived


def dp_joined(piece):
    size, me = lax.axis_size("dp"), lax.axis_index("dp")
    rows = piece.shape[0]
    out = jnp.zeros((size * rows, piece.shape[1]), piece.dtype)
    out = lax.dynamic_update_slice_in_dim(out, piece, me * rows, 0)
    for turn in range(1, size):
        other = lax.ppermute(piece, "dp", turned(size, size, 1, turn))
        out = lax.dynamic_update_slice_in_dim(out, other, (me - turn) % size * rows, 0)
    return out


def across_chips(array, line):
    mine, away = halves(array, line.chip % 2)
    return [mine, line.pair(away)]


def across_cores(array, line):
    mine, away = halves(array, line.core)
    return [mine, line.swap(away)]


def summed_dp(array):
    size = lax.axis_size("dp")
    for bit in range(size.bit_length() - 1):
        array = add(array, lax.ppermute(array, "dp", [(g, g ^ (1 << bit)) for g in range(size)]))
    return array


def summed_graph(array, line, bits):
    for bit in bits:
        pairs = [(g, g ^ (1 << bit)) for g in range(line.size)]
        array = add(array, lax.ppermute(array, "graph", pairs))
    return array


def local(
    edge_state,
    cotangent,
    edge_count,
    triplet_basis,
    triplet_in,
    triplet_out,
    down_weight,
    basis_weight,
    bilinear_weight,
    up_weight,
    first_weight,
    second_weight,
):
    edge_rows = edge_state[0]
    row_count, wide = edge_rows.shape
    line = Line()
    shards, chips = line.size, line.chips
    narrow = down_weight.shape[1]
    down_weight = down_weight.T
    basis = triplet_basis[0]
    basis_width, tri_rows = basis.shape
    slots = tri_rows // shards
    lanes = math.gcd(row_count, 256)
    stacked = narrow * (row_count // lanes)
    tile = math.gcd(row_count, 512)
    tiles = row_count // tile
    row_spec = pl.BlockSpec((tile, wide), lambda i: (i, 0))
    stack_spec = pl.BlockSpec((narrow * (tile // lanes), lanes), lambda i: (i, 0))
    rows_spec = whole(stacked, lanes)

    ends = jnp.stack([triplet_in.reshape(shards, 1, slots), triplet_out.reshape(shards, 1, slots)])
    triplet_specs = (
        [whole(2, shards, 1, slots)] * 2
        + [whole(basis_width, tri_rows)] * 2
        + [whole(basis_width, narrow)]
    )
    block_flops = 8 * slots * row_count * narrow

    down_rows, down_slope = call(
        down_kernel,
        (tiles,),
        [row_spec, whole(narrow, wide)],
        [stack_spec] * 2,
        [shape((stacked, lanes), BF16), shape((stacked, lanes), F32)],
        2 * row_count * wide * narrow,
        row_count * narrow,
    )(in_hbm(edge_rows), in_hbm(down_weight))

    slot_spec = whole(2, narrow, slots)
    slot_shape = pltpu.HBM((2, narrow, slots), BF16)

    ends, leaving = after((ends, basis), down_rows)
    ends_sibling = line.swap(ends)
    basis_sibling = line.swap(leaving)
    triplets = (ends, ends_sibling, basis, basis_sibling, basis_weight)

    def forward(turn, bits, rows, totals):
        total_shape = shape((stacked, lanes), F32)
        final = line.groups == 1 and bits == chips - 1
        out = call(
            forward_kernel,
            (),
            [SMEM, rows_spec] + triplet_specs + [rows_spec] * len(totals),
            [rows_spec] * 2 + [slot_spec] * 2,
            [pltpu.HBM((stacked, lanes), F32) if final else total_shape, total_shape]
            + [slot_shape] * 2,
            block_flops,
            aliases={7 + i: i for i in range(len(totals)) if i == 1 or not final},
            grant=FORWARD_GRANT,
        )(line.shard(turn, bits), rows, *triplets, *totals)
        return tuple(out[:2]), tuple(out[2:])

    def forward_line(turn, rows, totals, *others):
        arriving = [line.trade(rows, bits) for bits in range(1, chips)]
        totals, got = forward(turn, 0, rows, totals)
        kept = [got]
        for bits in range(1, chips):
            (rows,) = after((arriving[bits - 1],), *totals, *others)
            totals, got = forward(turn, bits, rows, totals)
            kept.append(got)
        return totals, kept

    first_turned, second_turned = after((first_weight, second_weight), down_rows)
    first_turned, second_turned = first_turned.T, second_turned.T
    totals, kept = forward_line(0, down_rows, (), first_turned, second_turned)
    if line.groups > 1:

        def forward_turn(carry, turn):
            rows, totals = carry
            rows = line.next_group(rows)
            totals, got = forward_line(turn, rows, totals)
            return (rows, totals), got

        (_, totals), more_kept = lax.scan(
            forward_turn, (down_rows, totals), jnp.arange(1, line.groups)
        )

    grad_rows = 2 * wide + 2 * narrow
    back_summed, back_gathered, dense_grads = call(
        dense_kernel,
        (tiles,),
        [
            SMEM,
            row_spec,
            row_spec,
            stack_spec,
            stack_spec,
            whole(narrow, narrow),
            whole(narrow, wide),
            whole(wide, wide),
            whole(wide, wide),
            whole(wide, wide),
            whole(wide, wide),
        ],
        [row_spec, stack_spec, whole(grad_rows, wide)],
        [
            pltpu.HBM((row_count, wide), BF16),
            shape((stacked, lanes), BF16),
            shape((grad_rows, wide), BF16),
        ],
        12 * row_count * wide * wide + 6 * row_count * wide * narrow,
        3 * row_count * wide,
        scratch=[pltpu.VMEM((grad_rows, wide), F32)],
        grant=DENSE_GRANT,
    )(
        jnp.stack([edge_count[0, 0], line.core.astype(jnp.int32)]),
        in_hbm(edge_rows),
        in_hbm(cotangent[0]),
        in_hbm(totals[0]) if line.groups == 1 else totals[0],
        line.swap(totals[1]),
        bilinear_weight,
        up_weight,
        in_hbm(first_weight),
        first_turned,
        in_hbm(second_weight),
        second_turned,
    )
    back_sibling = line.swap(back_gathered)

    def backward(turn, bits, kept, others=()):
        count = len(bits)
        (back,) = after((back_gathered,), *others)
        out = call(
            functools.partial(backward_kernel, count),
            (),
            [SMEM] + [rows_spec] * 2 + [slot_spec] * (2 * count) + triplet_specs[:2],
            [rows_spec] * count + [slot_spec] * count,
            [shape((stacked, lanes), BF16)] * count + [shape((2, narrow, slots), BF16)] * count,
            count * block_flops,
            grant=BACKWARD_GRANT,
        )(
            jnp.concatenate([line.shard(turn, one) for one in bits]),
            back,
            back_sibling,
            *[kept[one][0] for one in bits],
            *[kept[one][1] for one in bits],
            ends,
            ends_sibling,
        )
        return out[:count], out[count:]

    graph_bits = line.size.bit_length() - 1

    def backward_line(turn, kept, pieces=None):
        parts, others = [], ()
        last_coefs = near_coefs = ()
        if chips == 4:
            (last,), last_coefs = backward(turn, (3,), kept)
            passed = line.send(last, [(0, 1), (3, 2)])
            middle = line.send(last, [(1, 2), (2, 1)])
            others = (last,)
        if pieces is not None:
            pieces = add(*after(pieces, *others))
            others = (*others, pieces)
            arriving = dp_pieces(pieces)
        if chips == 4:
            (near, far), near_coefs = backward(turn, (1, 2), kept, others)
            (passed,) = after((passed,), far)
            if pieces is not None:
                pieces = add(*after(arriving, far))
                (far,) = after((far,), pieces)
            far = add(far, passed)
            (middle,) = after((middle,), far)
            (far,) = after((far,), middle)
            others = (far,)
            parts = [middle, line.trade(far, 2), line.trade(near, 1)]
        elif chips == 2:
            (near,), near_coefs = backward(turn, (1,), kept, others)
            parts = [line.trade(near, 1)]
        (own,), own_coefs = backward(turn, (0,), kept, others)
        if pieces is not None and chips < 4:
            pieces = add(*arriving)
        back_coefs = [*own_coefs, *near_coefs, *last_coefs]
        basis_grad = call(
            basis_kernel,
            (),
            [SMEM] + [slot_spec] * chips + triplet_specs[2:4],
            [whole(narrow, basis_width)],
            [shape((narrow, basis_width), F32)],
            4 * chips * slots * narrow * basis_width,
        )(
            jnp.concatenate([line.shard(turn, bits) for bits in range(chips)]),
            *back_coefs,
            basis,
            basis_sibling,
        )[0]
        return [own] + parts, basis_grad, pieces

    back_parts, basis_grad, dense_grads = backward_line(
        0, kept, [dense_grads[: grad_rows // 2], line.swap(dense_grads[grad_rows // 2 :])]
    )
    if chips > 1:
        dense_grads = add(*across_chips(dense_grads, line))
    dense_grads = summed_graph(dense_grads, line, range(2, graph_bits))
    if line.groups > 1:

        def backward_turn(carry, one):
            traveling, basis_grad = carry
            turn, got = one
            parts, more, _ = backward_line(turn, got)
            return (line.last_group(add(traveling, *parts)), basis_grad + more), None

        (traveling, basis_grad), _ = lax.scan(
            backward_turn,
            (jnp.zeros((stacked, lanes), BF16), basis_grad),
            (jnp.arange(1, line.groups), more_kept),
            reverse=True,
        )
        back_parts = back_parts + [traveling]

    small_rows = narrow + basis_width
    edge_grad, small_grads = call(
        functools.partial(final_kernel, len(back_parts)),
        (tiles,),
        [stack_spec] * len(back_parts)
        + [stack_spec, row_spec, row_spec, whole(narrow, wide), whole(narrow, basis_width)],
        [row_spec, whole(small_rows, wide)],
        [shape((row_count, wide), BF16), shape((small_rows, wide), BF16)],
        4 * row_count * wide * narrow,
        scratch=[pltpu.VMEM((small_rows, wide), F32)],
        grant=FINAL_GRANT,
    )(
        *back_parts,
        down_slope,
        edge_rows,
        back_summed,
        down_weight,
        basis_grad,
    )

    small_grads = add(*across_cores(small_grads, line))
    small_grads = summed_dp(summed_graph(small_grads, line, range(1, graph_bits)))
    small_grads = joined(small_grads, line.swap(small_grads), line.core)
    if chips > 1:
        dense_grads = joined(dense_grads, line.pair(dense_grads), line.chip % 2)
    dense_grads = dp_joined(dense_grads)
    dense_grads = joined(dense_grads, line.swap(dense_grads), line.core)
    scale = 1.0 / math.sqrt(lax.axis_size("dp") * shards * row_count)

    def scaled(source, *dims):
        return call(
            functools.partial(scale_kernel, scale),
            (),
            [whole(*source.shape)],
            [whole(*d) for d in dims],
            [shape(d, F32) for d in dims],
            source.size,
        )(source)

    first_grad, second_grad, up_grad, bilinear_grad = scaled(
        dense_grads, (wide, wide), (wide, wide), (narrow, wide), (narrow, narrow)
    )
    down_grad, basis_grad = scaled(small_grads, (narrow, wide), (basis_width, narrow))
    return (
        edge_grad[None],
        down_grad.T,
        basis_grad,
        bilinear_grad,
        up_grad,
        first_grad,
        second_grad,
    )


def solution(mesh):
    in_specs = (
        P("dp", "graph", None),
        P("dp", "graph", None),
        P("dp", "graph"),
        P("dp", None, "graph"),
        P("dp", "graph"),
        P("dp", "graph"),
        P(),
        P(),
        P(),
        P(),
        P(),
        P(),
    )
    out_specs = (P("dp", "graph", None), P(), P(), P(), P(), P(), P())
    return jax.shard_map(local, mesh=mesh, in_specs=in_specs, out_specs=out_specs, check_vma=False)
```
